32 devices in a mesh: tm: 8 (over z, x), gz: 4 (over y, core).
Axes of the slice: x: 2, y: 2, z: 4, core: 2. Of those that a mesh axis runs over, the one named last changes fastest.
Arguments:
- states: float32 [8, 3, 64, 16, 128], P('tm', None, 'gz'), may hold values from -4 to 4
- rate: float32 [64, 16, 128], P('gz'), may hold values from 0.1 to 40
Outputs:
- new_states: float32 [8, 3, 64, 16, 128], P('tm', None, 'gz')
The draws below stay inside these ranges and needn't reach their ends.
All inputs are finite; a program needn't handle non-finite values.
Results may differ from the reference program's by a relative error of at most 0.000044.
Values sent between devices are 32-bit elements; how exact they have to be, the bound alone decides.
No kernel may reach another device: no remote copies, remote signals or barrier semaphores. Data moves between devices by JAX's collectives and lax.ppermute only.
A program may use at most 128 MiB of HBM per device.

```python
import math
import jax
import jax.numpy as jnp
from jax import lax

NX = 128
NY = 16
STEPS = 2
NZ = 64
SLICES = 8


def steps_of(key, shape, cuts, low, largest):
    gain = 1.0
    for dim, shards_of in cuts:
        steps = jax.random.uniform(jax.random.fold_in(jax.random.fold_in(key, 6), dim), (shards_of,), jnp.float32, low / len(cuts), largest / len(cuts))
        gain = gain * jnp.repeat(jnp.exp(steps), shape[dim] // shards_of).reshape((-1,) + (1,) * (len(shape) - 1 - dim))
    return gain


def gaussian(rng, extent, scale, limit, shards=(), held_as=jnp.bfloat16):
    values = jax.random.normal(rng, extent, jnp.float32) * scale
    if len(shards) > 0:
        values = steps_of(rng, extent, shards, -0.22, 0.18) * values
    return jnp.clip(values, min=-limit, max=limit).astype(held_as)


def setup_inputs(seed: int = 0) -> dict:
    key_of = jax.random.split(jax.random.key(seed), 3)
    states = gaussian(key_of[0], (SLICES, 3, NZ, NY, NX), 0.5, 4.0, ((0, 8), (2, 4)), jnp.float32)
    rate = jnp.clip(jnp.exp(math.log(40.0) - 5.9914645 * jax.random.uniform(key_of[1], (NZ, NY, NX), jnp.float32) ** steps_of(key_of[1], (NZ, NY, NX), ((0, 4),), -0.2, 0.2)), 0.1, 40.0)
    return dict(states=states, rate=rate)


VISCOSITY = 0.05
TIME_STEP = 0.2


def tendency(padded):
    core = padded[:, 1:-1]
    along_x = (jnp.roll(core, -1, 3) - jnp.roll(core, 1, 3)) * 0.5
    along_y = (jnp.roll(core, -1, 2) - jnp.roll(core, 1, 2)) * 0.5
    along_z = (padded[:, 2:] - padded[:, :-2]) * 0.5
    spread = jnp.roll(core, -1, 3) + jnp.roll(core, 1, 3) + jnp.roll(core, -1, 2) + jnp.roll(core, 1, 2)
    spread = spread + padded[:, 2:] + padded[:, :-2] - 6.0 * core
    advect = core[0:1] * along_x + core[1:2] * along_y + core[2:3] * along_z
    return -advect + VISCOSITY * spread


def rate_of(field):
    return tendency(jnp.pad(field, ((0, 0), (1, 1), (0, 0), (0, 0)), mode="wrap"))


def fine(field):
    for step in range(STEPS):
        first = field + TIME_STEP * rate_of(field)
        second = 0.75 * field + 0.25 * (first + TIME_STEP * rate_of(first))
        field = (1.0 / 3.0) * field + (2.0 / 3.0) * (second + TIME_STEP * rate_of(second))
    return field


def reference(states, rate):
    damp = jnp.exp(-rate / SLICES).astype(jnp.float32)

    def slice_jump(field):
        return fine(field) - damp * field

    jumps = lax.map(slice_jump, states)

    def chain(carry, jump):
        nexts = damp * carry + jump
        return nexts, nexts

    _, later = lax.scan(chain, states[0], jumps[:-1])
    return jnp.concatenate([states[0:1], later], 0)
```

```python
import functools

import jax
import jax.numpy as jnp
from jax import lax
from jax.experimental import pallas as pl
from jax.experimental.pallas import tpu as pltpu
from jax.sharding import PartitionSpec as P

STEPS = 2
STAGES = 3 * STEPS
VISCOSITY = 0.05
TIME_STEP = 0.2
VMEM = pl.BlockSpec(memory_space=pltpu.VMEM)
PARAMS = pltpu.CompilerParams(vmem_limit_bytes=16 * 1024 * 1024)


def call(kernel, out_shape, *args, scratch=()):
    return pl.pallas_call(
        kernel,
        out_shape=out_shape,
        in_specs=[VMEM] * len(args),
        out_specs=jax.tree.map(lambda _: VMEM, out_shape),
        scratch_shapes=list(scratch),
        compiler_params=PARAMS,
    )(*args)


def f32(*shape):
    return jax.ShapeDtypeStruct(shape, jnp.float32)


def split_rows(ref, *lead):
    half = ref.shape[-2] // 2
    return [ref[(*lead, pl.ds(odd, half, stride=2), slice(None))] for odd in (0, 1)]


def join_rows(ref, lead, pair):
    half = ref.shape[-2] // 2
    for odd in (0, 1):
        ref[(*lead, pl.ds(odd, half, stride=2), slice(None))] = pair[odd]


def advance(below, here, above, alpha):
    diffuse = alpha * TIME_STEP * VISCOSITY
    carry = alpha * TIME_STEP * 0.5
    result = [[None, None] for _ in range(3)]
    for odd in (0, 1):
        speed = [here[c][odd] * carry for c in range(3)]
        to_next = [diffuse - s for s in speed]
        to_last = [diffuse + s for s in speed]
        for c in range(3):
            w = here[c][odd]
            rows, width = w.shape
            other = here[c][1 - odd]
            if odd:
                y_next, y_last = pltpu.roll(other, rows - 1, 0), other
            else:
                y_next, y_last = other, pltpu.roll(other, 1, 0)
            total = (alpha - 6.0 * diffuse) * w
            total = total + (
                to_next[0] * pltpu.roll(w, width - 1, 1) + to_last[0] * pltpu.roll(w, 1, 1)
            )
            total = total + (to_next[1] * y_next + to_last[1] * y_last)
            total = total + (to_next[2] * above[c][odd] + to_last[2] * below[c][odd])
            result[c][odd] = total
    return result


def fine_kernel(group, own_ref, low_ref, high_ref, rate_ref, *refs):
    outs, damp_ref, field, first, second = refs[:-4], refs[-4], refs[-3], refs[-2], refs[-1]
    layers = own_ref.shape[1]
    halo = STAGES
    whole = layers + 2 * halo
    slices = lax.axis_size("tm")
    mine = lax.axis_index("tm")

    def load(ref, z):
        return [[ref[c, z, odd] for odd in (0, 1)] for c in range(3)]

    def fill(source, start, count):
        def body(z, _):
            for c in range(3):
                for odd, value in enumerate(split_rows(source, c, z)):
                    field[c, start + z, odd] = value
            return 0

        lax.fori_loop(0, count, body, 0, unroll=2)

    fill(low_ref, 0, halo)
    fill(own_ref, halo, layers)
    fill(high_ref, halo + layers, halo)

    def stage(source, target, base, alpha, beta, lo, hi):
        unroll = 4
        count = -(-(hi - lo) // unroll)

        def body(turn, carry):
            below, here = carry
            start = lo + turn * unroll
            for k in range(unroll):
                z = start + k
                above = load(source, z + 1)
                new = advance(below, here, above, alpha)
                for c in range(3):
                    for odd in (0, 1):
                        value = new[c][odd]
                        if beta is not None:
                            value = value + beta * base[c, z, odd]
                        target[c, z, odd] = value
                below, here = here, above
            return below, here

        lax.fori_loop(0, count, body, (load(source, lo - 1), load(source, lo)))

    lo, hi = 1, whole - 1
    for step in range(STEPS):
        stage(field, first, None, 1.0, None, lo, hi)
        stage(first, second, field, 0.25, 0.75, lo + 1, hi - 1)
        stage(second, field, field, 2.0 / 3.0, 1.0 / 3.0, lo + 2, hi - 2)
        lo, hi = lo + 3, hi - 3

    share = layers // group
    place = lax.rem(mine, group)
    keep = (mine != 0).astype(jnp.float32)
    for k, out in enumerate(outs):
        chunk = lax.bitwise_xor(place, k) * share

        def body(z, _):
            damp = [jnp.exp(r / -slices) * keep for r in split_rows(rate_ref, chunk + z)]
            for c in range(3):
                start = split_rows(own_ref, c, chunk + z)
                for odd in (0, 1):
                    out[c, z, odd] = field[c, halo + chunk + z, odd] - damp[odd] * start[odd]
            return 0

        lax.fori_loop(0, share, body, 0)

    def damp_body(z, _):
        for odd, r in enumerate(split_rows(rate_ref, place * share + z)):
            damp_ref[z, odd] = jnp.exp(r / -slices)
        return 0

    lax.fori_loop(0, share, damp_body, 0)


def carry_kernel(group, *refs):
    jumps, damp_ref, out, order = refs[:group], refs[group], refs[group + 1], refs[group + 2]
    place = lax.rem(lax.axis_index("tm"), group)
    for k in range(group):
        order[lax.bitwise_xor(place, k)] = jumps[k][...]
    damp = damp_ref[...]
    total = order[0]
    for j in range(1, group):
        total = damp[None] * total + order[j]
    out[...] = total


def spread_kernel(group, *refs):
    jumps, damp_ref, carry_ref = refs[:group], refs[group], refs[group + 1]
    outs, order = refs[group + 2 : -1], refs[-1]
    place = lax.rem(lax.axis_index("tm"), group)
    for k in range(group):
        order[lax.bitwise_xor(place, k)] = jumps[k][...]
    damp = damp_ref[...]
    total = carry_ref[...]
    for j in range(group):
        jump = order[j]
        order[j] = total
        total = damp[None] * total + jump
    for k in range(group):
        outs[k][...] = order[lax.bitwise_xor(place, k)]


def finish_kernel(group, own_ref, *refs):
    pieces, out = refs[:group], refs[group]
    share = pieces[0].shape[1]
    mine = lax.axis_index("tm")
    place = lax.rem(mine, group)

    @pl.when(mine == 0)
    def _():
        out[...] = own_ref[...]

    @pl.when(mine != 0)
    def _():
        for k, piece in enumerate(pieces):
            chunk = lax.bitwise_xor(place, k) * share
            for z in range(share):
                for c in range(3):
                    join_rows(out, (c, chunk + z), [piece[c, z, odd] for odd in (0, 1)])


def shards(states, rate):
    slices = lax.axis_size("tm")
    slabs = lax.axis_size("gz")
    group = 4 if slices % 4 == 0 else (2 if slices % 2 == 0 else 1)
    groups = slices // group
    own = states[0]
    layers, rows, width = own.shape[1:]
    share = layers // group
    half = rows // 2

    low = lax.ppermute(own[:, layers - STAGES :], "gz", [(i, (i + 1) % slabs) for i in range(slabs)])
    high = lax.ppermute(own[:, :STAGES], "gz", [((i + 1) % slabs, i) for i in range(slabs)])

    piece = f32(3, share, 2, half, width)
    field = pltpu.VMEM((3, layers + 2 * STAGES + 4, 2, half, width), jnp.float32)
    *jumps, damp = call(
        functools.partial(fine_kernel, group),
        [piece] * group + [f32(share, 2, half, width)],
        own, low, high, rate,
        scratch=[field] * 3,
    )

    def swap(parts):
        return [parts[0]] + [
            lax.ppermute(parts[k], "tm", [(i, i ^ k) for i in range(slices)]) for k in range(1, group)
        ]

    def onward(value, distance):
        step = distance * group
        return lax.ppermute(value, "tm", [(i, i + step) for i in range(slices - step)])

    jumps = swap(jumps)
    order = pltpu.VMEM((group,) + piece.shape, jnp.float32)
    if groups > 1:
        total = call(functools.partial(carry_kernel, group), piece, *jumps, damp, scratch=[order])
        carry = onward(total, 1)
        distance, factor = 1, damp**group
        while distance < groups - 1:
            carry = carry + factor * onward(carry, distance)
            distance, factor = 2 * distance, factor * factor
    else:
        carry = jnp.zeros(piece.shape, jnp.float32)
    news = call(
        functools.partial(spread_kernel, group), [piece] * group, *jumps, damp, carry, scratch=[order]
    )
    news = swap(news)
    updated = call(functools.partial(finish_kernel, group), f32(*own.shape), own, *news)
    return updated[None]


def solution(mesh):
    return jax.shard_map(
        shards,
        mesh=mesh,
        in_specs=(P("tm", None, "gz", None, None), P("gz", None, None)),
        out_specs=P("tm", None, "gz", None, None),
        check_vma=False,
    )
```

```python
import functools

import jax
import jax.numpy as jnp
from jax import lax
from jax.experimental import pallas as pl
from jax.experimental.pallas import tpu as pltpu
from jax.sharding import PartitionSpec as P

STEPS = 2
STAGES = 3 * STEPS
VISCOSITY = 0.05
TIME_STEP = 0.2
VMEM = pl.BlockSpec(memory_space=pltpu.VMEM)
PARAMS = pltpu.CompilerParams(vmem_limit_bytes=16 * 1024 * 1024)


def call(kernel, out_shape, *args, scratch=()):
    return pl.pallas_call(
        kernel,
        out_shape=out_shape,
        in_specs=[VMEM] * len(args),
        out_specs=jax.tree.map(lambda _: VMEM, out_shape),
        scratch_shapes=list(scratch),
        compiler_params=PARAMS,
    )(*args)


def f32(*shape):
    return jax.ShapeDtypeStruct(shape, jnp.float32)


def split_rows(ref, *lead):
    half = ref.shape[-2] // 2
    return [ref[(*lead, pl.ds(odd, half, stride=2), slice(None))] for odd in (0, 1)]


def join_rows(ref, lead, pair):
    half = ref.shape[-2] // 2
    for odd in (0, 1):
        ref[(*lead, pl.ds(odd, half, stride=2), slice(None))] = pair[odd]


def advance(below, here, above, alpha):
    diffuse = alpha * TIME_STEP * VISCOSITY
    carry = alpha * TIME_STEP * 0.5
    result = [[None, None] for _ in range(3)]
    for odd in (0, 1):
        speed = [here[c][odd] * carry for c in range(3)]
        to_next = [diffuse - s for s in speed]
        to_last = [diffuse + s for s in speed]
        for c in range(3):
            w = here[c][odd]
            rows, width = w.shape
            other = here[c][1 - odd]
            if odd:
                y_next, y_last = pltpu.roll(other, rows - 1, 0), other
            else:
                y_next, y_last = other, pltpu.roll(other, 1, 0)
            total = (alpha - 6.0 * diffuse) * w
            total = total + (
                to_next[0] * pltpu.roll(w, width - 1, 1) + to_last[0] * pltpu.roll(w, 1, 1)
            )
            total = total + (to_next[1] * y_next + to_last[1] * y_last)
            total = total + (to_next[2] * above[c][odd] + to_last[2] * below[c][odd])
            result[c][odd] = total
    return result


def fine_kernel(group, own_ref, low_ref, high_ref, rate_ref, *refs):
    out, damp_ref, field, first, second = refs
    layers = own_ref.shape[1]
    halo = STAGES
    whole = layers + 2 * halo
    slices = lax.axis_size("tm")
    mine = lax.axis_index("tm")

    def load(ref, z):
        return [[ref[c, z, odd] for odd in (0, 1)] for c in range(3)]

    def fill(source, start, count):
        def body(z, _):
            for c in range(3):
                for odd, value in enumerate(split_rows(source, c, z)):
                    field[c, start + z, odd] = value
            return 0

        lax.fori_loop(0, count, body, 0, unroll=2)

    fill(low_ref, 0, halo)
    fill(own_ref, halo, layers)
    fill(high_ref, halo + layers, halo)

    def stage(source, target, base, alpha, beta, lo, hi):
        unroll = 4
        count = -(-(hi - lo) // unroll)

        def body(turn, carry):
            below, here = carry
            start = lo + turn * unroll
            for k in range(unroll):
                z = start + k
                above = load(source, z + 1)
                new = advance(below, here, above, alpha)
                for c in range(3):
                    for odd in (0, 1):
                        value = new[c][odd]
                        if beta is not None:
                            value = value + beta * base[c, z, odd]
                        target[c, z, odd] = value
                below, here = here, above
            return below, here

        lax.fori_loop(0, count, body, (load(source, lo - 1), load(source, lo)))

    lo, hi = 1, whole - 1
    for step in range(STEPS):
        stage(field, first, None, 1.0, None, lo, hi)
        stage(first, second, field, 0.25, 0.75, lo + 1, hi - 1)
        stage(second, field, field, 2.0 / 3.0, 1.0 / 3.0, lo + 2, hi - 2)
        lo, hi = lo + 3, hi - 3

    share = layers // group
    place = lax.rem(mine, group)
    keep = (mine != 0).astype(jnp.float32)
    for part in range(group):
        for z in range(share):
            layer = part * share + z
            damp = [jnp.exp(r / -slices) * keep for r in split_rows(rate_ref, layer)]
            for c in range(3):
                start = split_rows(own_ref, c, layer)
                for odd in (0, 1):
                    out[part, c, z, odd] = field[c, halo + layer, odd] - damp[odd] * start[odd]

    def damp_body(z, _):
        for odd, r in enumerate(split_rows(rate_ref, place * share + z)):
            damp_ref[z, odd] = jnp.exp(r / -slices)
        return 0

    lax.fori_loop(0, share, damp_body, 0)


def carry_kernel(jumps, damp_ref, out):
    damp = damp_ref[...]
    total = jumps[0]
    for j in range(1, jumps.shape[0]):
        total = damp[None] * total + jumps[j]
    out[...] = total


def spread_kernel(jumps, damp_ref, carry_ref, out):
    damp = damp_ref[...]
    total = carry_ref[...]
    for j in range(jumps.shape[0]):
        out[j] = total
        total = damp[None] * total + jumps[j]


def finish_kernel(own_ref, pieces, out):
    group, _, share = pieces.shape[:3]
    mine = lax.axis_index("tm")

    @pl.when(mine == 0)
    def _():
        out[...] = own_ref[...]

    @pl.when(mine != 0)
    def _():
        for part in range(group):
            for z in range(share):
                for c in range(3):
                    join_rows(out, (c, part * share + z), [pieces[part, c, z, odd] for odd in (0, 1)])


def shards(states, rate):
    slices = lax.axis_size("tm")
    slabs = lax.axis_size("gz")
    group = 4 if slices % 4 == 0 else (2 if slices % 2 == 0 else 1)
    groups = slices // group
    own = states[0]
    layers, rows, width = own.shape[1:]
    share = layers // group
    half = rows // 2

    low = lax.ppermute(own[:, layers - STAGES :], "gz", [(i, (i + 1) % slabs) for i in range(slabs)])
    high = lax.ppermute(own[:, :STAGES], "gz", [((i + 1) % slabs, i) for i in range(slabs)])

    piece = f32(3, share, 2, half, width)
    field = pltpu.VMEM((3, layers + 2 * STAGES + 4, 2, half, width), jnp.float32)
    jumps, damp = call(
        functools.partial(fine_kernel, group),
        [f32(group, *piece.shape), f32(share, 2, half, width)],
        own, low, high, rate,
        scratch=[field] * 3,
    )
    teams = [[g * group + k for k in range(group)] for g in range(groups)]

    def swap(parts):
        return lax.all_to_all(parts, "tm", 0, 0, axis_index_groups=teams, tiled=True)

    def onward(value, distance):
        step = distance * group
        return lax.ppermute(value, "tm", [(i, i + step) for i in range(slices - step)])

    jumps = swap(jumps)
    if groups > 1:
        total = call(carry_kernel, piece, jumps, damp)
        carry = onward(total, 1)
        distance, factor = 1, damp**group
        while distance < groups - 1:
            carry = carry + factor * onward(carry, distance)
            distance, factor = 2 * distance, factor * factor
    else:
        carry = jnp.zeros(piece.shape, jnp.float32)
    news = call(spread_kernel, f32(*jumps.shape), jumps, damp, carry)
    updated = call(finish_kernel, f32(*own.shape), own, swap(news))
    return updated[None]


def solution(mesh):
    return jax.shard_map(
        shards,
        mesh=mesh,
        in_specs=(P("tm", None, "gz", None, None), P("gz", None, None)),
        out_specs=P("tm", None, "gz", None, None),
        check_vma=False,
    )
```

```python
import functools

import jax
import jax.numpy as jnp
from jax import lax
from jax.experimental import pallas as pl
from jax.experimental.pallas import tpu as pltpu
from jax.sharding import PartitionSpec as P

STEPS = 2
STAGES = 3 * STEPS
VISCOSITY = 0.05
TIME_STEP = 0.2
MIX = ((1.0, None), (0.25, 0.75), (2.0 / 3.0, 1.0 / 3.0))
VMEM = pl.BlockSpec(memory_space=pltpu.VMEM)
HBM = pl.BlockSpec(memory_space=pltpu.HBM)
PARAMS = pltpu.CompilerParams(vmem_limit_bytes=16 * 1024 * 1024)


def call(kernel, out_shape, *args, scratch=(), specs=None, flops=None):
    cost = None if flops is None else pl.CostEstimate(flops=flops, bytes_accessed=1 << 20, transcendentals=0)
    return pl.pallas_call(
        kernel,
        out_shape=out_shape,
        in_specs=specs or [VMEM] * len(args),
        out_specs=jax.tree.map(lambda _: VMEM, out_shape),
        scratch_shapes=list(scratch),
        compiler_params=PARAMS,
        cost_estimate=cost,
    )(*args)


def partner(group, k):
    return (group - k) % group


def f32(*shape):
    return jax.ShapeDtypeStruct(shape, jnp.float32)


def split_rows(ref, *lead):
    half = ref.shape[-2] // 2
    return [ref[(*lead, pl.ds(odd, half, stride=2), slice(None))] for odd in (0, 1)]


def join_rows(ref, lead, pair):
    half = ref.shape[-2] // 2
    for odd in (0, 1):
        ref[(*lead, pl.ds(odd, half, stride=2), slice(None))] = pair[odd]


def load(ref, *lead):
    return [[ref[(*lead, c, odd)] for odd in (0, 1)] for c in range(3)]


def store(ref, lead, value):
    for c in range(3):
        for odd in (0, 1):
            ref[(*lead, c, odd)] = value[c][odd]


def advance(below, here, above, alpha):
    diffuse = alpha * TIME_STEP * VISCOSITY
    carry = alpha * TIME_STEP * 0.5
    result = [[None, None] for _ in range(3)]
    for odd in (0, 1):
        speed = [here[c][odd] * carry for c in range(3)]
        to_next = [diffuse - s for s in speed]
        to_last = [diffuse + s for s in speed]
        for c in range(3):
            w = here[c][odd]
            rows, width = w.shape
            other = here[c][1 - odd]
            if odd:
                y_next, y_last = pltpu.roll(other, rows - 1, 0), other
            else:
                y_next, y_last = other, pltpu.roll(other, 1, 0)
            total = (alpha - 6.0 * diffuse) * w
            total = total + (
                to_next[0] * pltpu.roll(w, width - 1, 1) + to_last[0] * pltpu.roll(w, 1, 1)
            )
            total = total + (to_next[1] * y_next + to_last[1] * y_last)
            total = total + (to_next[2] * above[c][odd] + to_last[2] * below[c][odd])
            result[c][odd] = total
    return result


def blend(new, beta, base):
    return [[new[c][odd] + beta * base[c][odd] for odd in (0, 1)] for c in range(3)]


def faces_kernel(own_ref, far_ref, near_ref, sems):
    layers, width = own_ref.shape[1], near_ref.shape[1]
    odd = lax.rem(lax.axis_index("gz"), 2)
    top = layers - width
    near = pltpu.make_async_copy(own_ref.at[:, pl.ds((1 - odd) * top, width)], near_ref, sems.at[0])
    far = pltpu.make_async_copy(own_ref.at[:, pl.ds(odd * top, width)], far_ref, sems.at[1])
    far.start()
    near.start()
    far.wait()
    near.wait()


def inside_kernel(group, own_ref, rate_ref, edges, middle, faded, damp_ref, *fields):
    layers = own_ref.shape[1]
    share = layers // group
    slices = lax.axis_size("tm")
    mine = lax.axis_index("tm")
    keep = (mine != 0).astype(jnp.float32)

    def fill(z, _):
        for c in range(3):
            for odd, value in enumerate(split_rows(own_ref, c, z)):
                fields[0][z, c, odd] = value
        return 0

    lax.fori_loop(0, layers, fill, 0, unroll=2)

    def save(stage, field):
        for j in range(3):
            store(edges, (stage, 0, j), load(field, stage + j))
            store(edges, (stage, 1, j), load(field, layers - 1 - stage - j))

    def sweep(stage, source, target, base, alpha, beta):
        def body(turn, carry):
            below, here = carry
            for k in range(2):
                z = stage + 2 * turn + k
                above = load(source, z + 1)
                new = advance(below, here, above, alpha)
                if beta is not None:
                    new = blend(new, beta, load(base, z))
                store(target, (z,), new)
                below, here = here, above
            return below, here

        first = (load(source, stage - 1), load(source, stage))
        lax.fori_loop(0, (layers - 2 * stage) // 2, body, first)

    save(0, fields[0])
    for stage in range(1, STAGES + 1):
        kind = (stage - 1) % 3
        source, base = fields[kind], fields[0]
        target = fields[(kind + 1) % 3]
        sweep(stage, source, target, base, *MIX[kind])
        if stage < STAGES:
            save(stage, target)

    def fade(z, odd):
        return jnp.exp(split_rows(rate_ref, z)[odd] * (-1.0 / slices)) * keep

    for z in range(layers):
        damp = [fade(z, odd) for odd in (0, 1)]
        for c in range(3):
            start = split_rows(own_ref, c, z)
            for odd in (0, 1):
                lost = damp[odd] * start[odd]
                if z < STAGES:
                    faded[0, z, c, odd] = lost
                elif z >= layers - STAGES:
                    faded[1, layers - 1 - z, c, odd] = lost
                else:
                    middle[z - STAGES, c, odd] = fields[0][z, c, odd] - lost

    place = lax.rem(mine, group)
    for z in range(share):
        for odd, r in enumerate(split_rows(rate_ref, place * share + z)):
            damp_ref[z, odd] = jnp.exp(r * (-1.0 / slices))


def border_kernel(group, far_ref, near_ref, edges, middle, faded, *refs):
    outs, strip, jumps = refs[:group], refs[group], refs[group + 1]
    width = STAGES
    odd_slab = lax.rem(lax.axis_index("gz"), 2)
    for ref, side in ((near_ref, 1 - odd_slab), (far_ref, odd_slab)):
        for slot in range(width):
            place = slot + side * (width - 1 - 2 * slot)
            for c in range(3):
                for odd, value in enumerate(split_rows(ref, c, place)):
                    strip[0, side, slot, c, odd] = value

    def at(stage, side, slot):
        if slot < width:
            return load(strip, stage, side, slot)
        return load(edges, stage, side, slot - width)

    def step(turn, _):
        for kind, (alpha, beta) in enumerate(MIX):
            stage = 3 * turn + kind
            for side in (0, 1):
                last, here = at(stage, side, 0), at(stage, side, 1)
                for slot in range(width):
                    ahead = at(stage, side, slot + 2)
                    pair = (last, ahead) if side == 0 else (ahead, last)
                    new = advance(pair[0], here, pair[1], alpha)
                    if beta is not None:
                        new = blend(new, beta, at(3 * turn, side, slot + 1 + kind))
                    store(strip, (stage + 1, side, slot), new)
                    last, here = here, ahead
        return 0

    lax.fori_loop(0, STEPS, step, 0)

    share = outs[0].shape[0]
    layers = share * group
    for z in range(layers):
        if z < width:
            side, slot = 0, z
        elif z >= layers - width:
            side, slot = 1, layers - 1 - z
        else:
            store(jumps, (z // share, z % share), load(middle, z - width))
            continue
        end, lost = load(strip, STAGES, side, slot), load(faded, side, slot)
        for c in range(3):
            for odd in (0, 1):
                jumps[z // share, z % share, c, odd] = end[c][odd] - lost[c][odd]
    place = lax.rem(lax.axis_index("tm"), group)
    for k, out in enumerate(outs):
        out[...] = jumps[lax.bitwise_xor(place, partner(group, k))]


def carry_kernel(group, *refs):
    jumps, damp_ref, out, order = refs[:group], refs[group], refs[group + 1], refs[group + 2]
    place = lax.rem(lax.axis_index("tm"), group)
    for k in range(group):
        order[lax.bitwise_xor(place, partner(group, k))] = jumps[k][...]
    damp = damp_ref[...][:, None]
    total = order[0]
    for j in range(1, group):
        total = damp * total + order[j]
    out[...] = total


def spread_kernel(group, *refs):
    jumps, damp_ref, carry_ref = refs[:group], refs[group], refs[group + 1]
    outs, order = refs[group + 2 : -1], refs[-1]
    mine = lax.axis_index("tm")
    place = lax.rem(mine, group)
    for k in range(group):
        order[lax.bitwise_xor(place, partner(group, k))] = jumps[k][...]
    damp = damp_ref[...][:, None]
    total = jnp.where(mine < group, 0.0, carry_ref[...])
    for j in range(group):
        jump = order[j]
        order[j] = total
        total = damp * total + jump
    for k in range(group):
        outs[k][...] = order[lax.bitwise_xor(place, partner(group, k))]


def finish_kernel(group, own_ref, *refs):
    pieces, out = refs[:group], refs[group]
    share = pieces[0].shape[0]
    mine = lax.axis_index("tm")
    place = lax.rem(mine, group)

    @pl.when(mine == 0)
    def _():
        out[...] = own_ref[...]

    @pl.when(mine != 0)
    def _():
        for k, piece in enumerate(pieces):
            chunk = lax.bitwise_xor(place, partner(group, k)) * share
            for z in range(share):
                for c in range(3):
                    join_rows(out, (c, chunk + z), [piece[z, c, odd] for odd in (0, 1)])


def shards(states, rate):
    slices = lax.axis_size("tm")
    slabs = lax.axis_size("gz")
    group = 4 if slices % 4 == 0 else (2 if slices % 2 == 0 else 1)
    groups = slices // group
    own = states[0]
    layers, rows, width = own.shape[1:]
    share = layers // group
    tile = (3, 2, rows // 2, width)
    face = f32(3, STAGES, rows, width)
    team = lax.axis_index("tm") // group

    far, near = call(
        faces_kernel, [face, face], own, specs=[HBM], scratch=[pltpu.SemaphoreType.DMA((2,))]
    )
    far = lax.ppermute(far, "gz", [(i, (i + 1 if i % 2 else i - 1) % slabs) for i in range(slabs)])
    near = lax.ppermute(near, "gz", [(i, i ^ 1) for i in range(slabs)])
    edges, middle, faded, damp = call(
        functools.partial(inside_kernel, group),
        [
            f32(STAGES, 2, 3, *tile),
            f32(layers - 2 * STAGES, *tile),
            f32(2, STAGES, *tile),
            f32(share, *tile[1:]),
        ],
        own, rate,
        scratch=[pltpu.VMEM((layers, *tile), jnp.float32)] * 3,
        flops=1 << 26,
    )
    piece = f32(share, *tile)
    jumps = call(
        functools.partial(border_kernel, group),
        [piece] * group,
        far, near, edges, middle, faded,
        scratch=[
            pltpu.VMEM((STAGES + 1, 2, STAGES, *tile), jnp.float32),
            pltpu.VMEM((group, *piece.shape), jnp.float32),
        ],
    )

    def swap(parts):
        return [parts[0]] + [
            lax.ppermute(parts[k], "tm", [(i, i ^ partner(group, k)) for i in range(slices)])
            for k in range(1, group)
        ]

    def onward(value, distance):
        step = distance * group
        return lax.ppermute(value, "tm", [(i, (i + step) % slices) for i in range(slices)])

    jumps = swap(jumps)
    order = pltpu.VMEM((group, *piece.shape), jnp.float32)
    if groups > 1:
        total = call(functools.partial(carry_kernel, group), piece, *jumps, damp, scratch=[order])
        carry = onward(total, 1)
        if groups > 2:
            carry = jnp.where(team < 1, 0.0, carry)
        distance, factor = 1, (damp**group)[:, None]
        while distance < groups - 1:
            carry = carry + jnp.where(team < distance, 0.0, factor * onward(carry, distance))
            distance, factor = 2 * distance, factor * factor
    else:
        carry = jnp.zeros(piece.shape, jnp.float32)
    news = call(
        functools.partial(spread_kernel, group), [piece] * group, *jumps, damp, carry, scratch=[order]
    )
    updated = call(functools.partial(finish_kernel, group), f32(*own.shape), own, *swap(news))
    return updated[None]


def solution(mesh):
    return jax.shard_map(
        shards,
        mesh=mesh,
        in_specs=(P("tm", None, "gz", None, None), P("gz", None, None)),
        out_specs=P("tm", None, "gz", None, None),
        check_vma=False,
    )
```

```python
import functools

import jax
import jax.numpy as jnp
from jax import lax
from jax.experimental import pallas as pl
from jax.experimental.pallas import tpu as pltpu
from jax.sharding import PartitionSpec as P

STEPS = 2
STAGES = 3 * STEPS
VISCOSITY = 0.05
TIME_STEP = 0.2
MIX = ((1.0, None), (0.25, 0.75), (2.0 / 3.0, 1.0 / 3.0))
VMEM = pl.BlockSpec(memory_space=pltpu.VMEM)
HBM = pl.BlockSpec(memory_space=pltpu.HBM)
PARAMS = pltpu.CompilerParams(vmem_limit_bytes=16 * 1024 * 1024)


def call(kernel, out_shape, *args, scratch=(), specs=None, flops=None, moved=1 << 20):
    cost = None
    if flops is not None:
        cost = pl.CostEstimate(flops=flops, bytes_accessed=moved, transcendentals=0)
    return pl.pallas_call(
        kernel,
        out_shape=out_shape,
        in_specs=specs or [VMEM] * len(args),
        out_specs=jax.tree.map(lambda _: VMEM, out_shape),
        scratch_shapes=list(scratch),
        compiler_params=PARAMS,
        cost_estimate=cost,
    )(*args)


def partner(group, k):
    return (group - k) % group


def f32(*shape):
    return jax.ShapeDtypeStruct(shape, jnp.float32)


def split_rows(ref, *lead):
    half = ref.shape[-2] // 2
    return [ref[(*lead, pl.ds(odd, half, stride=2), slice(None))] for odd in (0, 1)]


def join_rows(ref, lead, pair):
    half = ref.shape[-2] // 2
    for odd in (0, 1):
        ref[(*lead, pl.ds(odd, half, stride=2), slice(None))] = pair[odd]


def load(ref, *lead):
    return [[ref[(*lead, c, odd)] for odd in (0, 1)] for c in range(3)]


def store(ref, lead, value):
    for c in range(3):
        for odd in (0, 1):
            ref[(*lead, c, odd)] = value[c][odd]


def advance(below, here, above, alpha):
    diffuse = alpha * TIME_STEP * VISCOSITY
    carry = alpha * TIME_STEP * 0.5
    result = [[None, None] for _ in range(3)]
    for odd in (0, 1):
        speed = [here[c][odd] * carry for c in range(3)]
        to_next = [diffuse - s for s in speed]
        to_last = [diffuse + s for s in speed]
        for c in range(3):
            w = here[c][odd]
            rows, width = w.shape
            other = here[c][1 - odd]
            if odd:
                y_next, y_last = pltpu.roll(other, rows - 1, 0), other
            else:
                y_next, y_last = other, pltpu.roll(other, 1, 0)
            total = (alpha - 6.0 * diffuse) * w
            total = total + (
                to_next[0] * pltpu.roll(w, width - 1, 1) + to_last[0] * pltpu.roll(w, 1, 1)
            )
            total = total + (to_next[1] * y_next + to_last[1] * y_last)
            total = total + (to_next[2] * above[c][odd] + to_last[2] * below[c][odd])
            result[c][odd] = total
    return result


def blend(new, beta, base):
    return [[new[c][odd] + beta * base[c][odd] for odd in (0, 1)] for c in range(3)]


def faces_kernel(own_ref, far_ref, near_ref, sems):
    layers, width = own_ref.shape[1], near_ref.shape[1]
    odd = lax.rem(lax.axis_index("gz"), 2)
    top = layers - width
    near = pltpu.make_async_copy(own_ref.at[:, pl.ds((1 - odd) * top, width)], near_ref, sems.at[0])
    far = pltpu.make_async_copy(own_ref.at[:, pl.ds(odd * top, width)], far_ref, sems.at[1])
    far.start()
    near.start()
    far.wait()
    near.wait()


def inside_kernel(group, own_ref, rate_ref, edges, middle, faded, damp_ref, power_ref, *fields):
    layers = own_ref.shape[1]
    share = layers // group
    slices = lax.axis_size("tm")
    mine = lax.axis_index("tm")
    keep = (mine != 0).astype(jnp.float32)

    def fill(z, _):
        for c in range(3):
            for odd, value in enumerate(split_rows(own_ref, c, z)):
                fields[0][z, c, odd] = value
        return 0

    lax.fori_loop(0, layers, fill, 0, unroll=2)

    def save(stage, field):
        for j in range(3):
            store(edges, (stage, 0, j), load(field, stage + j))
            store(edges, (stage, 1, j), load(field, layers - 1 - stage - j))

    def sweep(stage, source, target, base, alpha, beta):
        def body(turn, carry):
            below, here = carry
            for k in range(2):
                z = stage + 2 * turn + k
                above = load(source, z + 1)
                new = advance(below, here, above, alpha)
                if beta is not None:
                    new = blend(new, beta, load(base, z))
                store(target, (z,), new)
                below, here = here, above
            return below, here

        first = (load(source, stage - 1), load(source, stage))
        lax.fori_loop(0, (layers - 2 * stage) // 2, body, first)

    save(0, fields[0])
    for stage in range(1, STAGES + 1):
        kind = (stage - 1) % 3
        source, base = fields[kind], fields[0]
        target = fields[(kind + 1) % 3]
        sweep(stage, source, target, base, *MIX[kind])
        if stage < STAGES:
            save(stage, target)

    def fade(z, odd):
        return jnp.exp(split_rows(rate_ref, z)[odd] * (-1.0 / slices)) * keep

    for z in range(layers):
        damp = [fade(z, odd) for odd in (0, 1)]
        for c in range(3):
            start = split_rows(own_ref, c, z)
            for odd in (0, 1):
                lost = damp[odd] * start[odd]
                if z < STAGES:
                    faded[0, z, c, odd] = lost
                elif z >= layers - STAGES:
                    faded[1, layers - 1 - z, c, odd] = lost
                else:
                    middle[z - STAGES, c, odd] = fields[0][z, c, odd] - lost

    place = lax.rem(mine, group)
    for z in range(share):
        for odd, r in enumerate(split_rows(rate_ref, place * share + z)):
            damp_ref[z, odd] = jnp.exp(r * (-1.0 / slices))
    turns = place.astype(jnp.float32) * (-1.0 / slices)
    for z in range(layers):
        for odd, r in enumerate(split_rows(rate_ref, z)):
            power_ref[z, odd] = jnp.exp(r * turns)


def border_kernel(group, far_ref, near_ref, edges, middle, faded, *refs):
    outs, strip, jumps = refs[:group], refs[group], refs[group + 1]
    width = STAGES
    odd_slab = lax.rem(lax.axis_index("gz"), 2)
    for ref, side in ((near_ref, 1 - odd_slab), (far_ref, odd_slab)):
        for slot in range(width):
            place = slot + side * (width - 1 - 2 * slot)
            for c in range(3):
                for odd, value in enumerate(split_rows(ref, c, place)):
                    strip[0, side, slot, c, odd] = value

    def at(stage, side, slot):
        if slot < width:
            return load(strip, stage, side, slot)
        return load(edges, stage, side, slot - width)

    def step(turn, _):
        for kind, (alpha, beta) in enumerate(MIX):
            stage = 3 * turn + kind
            for side in (0, 1):
                last, here = at(stage, side, 0), at(stage, side, 1)
                for slot in range(width):
                    ahead = at(stage, side, slot + 2)
                    pair = (last, ahead) if side == 0 else (ahead, last)
                    new = advance(pair[0], here, pair[1], alpha)
                    if beta is not None:
                        new = blend(new, beta, at(3 * turn, side, slot + 1 + kind))
                    store(strip, (stage + 1, side, slot), new)
                    last, here = here, ahead
        return 0

    lax.fori_loop(0, STEPS, step, 0)

    share = outs[0].shape[0]
    layers = share * group
    for z in range(layers):
        if z < width:
            side, slot = 0, z
        elif z >= layers - width:
            side, slot = 1, layers - 1 - z
        else:
            store(jumps, (z // share, z % share), load(middle, z - width))
            continue
        end, lost = load(strip, STAGES, side, slot), load(faded, side, slot)
        for c in range(3):
            for odd in (0, 1):
                jumps[z // share, z % share, c, odd] = end[c][odd] - lost[c][odd]
    place = lax.rem(lax.axis_index("tm"), group)
    for k, out in enumerate(outs):
        out[...] = jumps[lax.bitwise_xor(place, partner(group, k))]


def carry_kernel(group, *refs):
    jumps, damp_ref, out = refs[:group], refs[group], refs[group + 1]
    locals_, order = refs[group + 2 : -1], refs[-1]
    place = lax.rem(lax.axis_index("tm"), group)
    for k in range(group):
        order[lax.bitwise_xor(place, partner(group, k))] = jumps[k][...]
    damp = damp_ref[...][:, None]
    total = order[0]
    order[0] = jnp.zeros_like(total)
    for j in range(1, group):
        jump = order[j]
        order[j] = total
        total = damp * total + jump
    out[...] = total
    for k in range(group):
        locals_[k][...] = order[lax.bitwise_xor(place, partner(group, k))]


def finish_kernel(group, own_ref, power_ref, carry_ref, *refs):
    pieces, out = refs[:group], refs[group]
    share = pieces[0].shape[0]
    mine = lax.axis_index("tm")
    place = lax.rem(mine, group)

    @pl.when(mine == 0)
    def _():
        out[...] = own_ref[...]

    @pl.when(mine != 0)
    def _():
        for k, piece in enumerate(pieces):
            worker = lax.bitwise_xor(place, partner(group, k))
            for z in range(share):
                layer = worker * share + z
                for c in range(3):
                    pair = []
                    for odd in (0, 1):
                        first = jnp.where(mine < group, 0.0, carry_ref[worker, z, c, odd])
                        pair.append(power_ref[layer, odd] * first + piece[z, c, odd])
                    join_rows(out, (c, layer), pair)


def shards(states, rate):
    slices = lax.axis_size("tm")
    slabs = lax.axis_size("gz")
    group = 4 if slices % 4 == 0 else (2 if slices % 2 == 0 else 1)
    groups = slices // group
    own = states[0]
    layers, rows, width = own.shape[1:]
    share = layers // group
    tile = (3, 2, rows // 2, width)
    face = f32(3, STAGES, rows, width)
    team = lax.axis_index("tm") // group

    far, near = call(
        faces_kernel, [face, face], own,
        specs=[HBM], scratch=[pltpu.SemaphoreType.DMA((2,))], flops=0, moved=0,
    )
    far = lax.ppermute(far, "gz", [(i, (i + 1 if i % 2 else i - 1) % slabs) for i in range(slabs)])
    near = lax.ppermute(near, "gz", [(i, i ^ 1) for i in range(slabs)])
    edges, middle, faded, damp, power = call(
        functools.partial(inside_kernel, group),
        [
            f32(STAGES, 2, 3, *tile),
            f32(layers - 2 * STAGES, *tile),
            f32(2, STAGES, *tile),
            f32(share, *tile[1:]),
            f32(layers, *tile[1:]),
        ],
        own, rate,
        scratch=[pltpu.VMEM((layers, *tile), jnp.float32)] * 3,
        flops=1 << 26,
    )
    piece = f32(share, *tile)
    jumps = call(
        functools.partial(border_kernel, group),
        [piece] * group,
        far, near, edges, middle, faded,
        scratch=[
            pltpu.VMEM((STAGES + 1, 2, STAGES, *tile), jnp.float32),
            pltpu.VMEM((group, *piece.shape), jnp.float32),
        ],
    )

    def swap(parts):
        return [parts[0]] + [
            lax.ppermute(parts[k], "tm", [(i, i ^ partner(group, k)) for i in range(slices)])
            for k in range(1, group)
        ]

    def onward(value, distance):
        step = distance * group
        return lax.ppermute(value, "tm", [(i, (i + step) % slices) for i in range(slices)])

    total, *before = call(
        functools.partial(carry_kernel, group),
        [piece] * (1 + group),
        *swap(jumps), damp,
        scratch=[pltpu.VMEM((group, *piece.shape), jnp.float32)],
    )
    carry = onward(total, 1)
    distance, factor = 1, (damp**group)[:, None]
    if groups > 2:
        carry = jnp.where(team < 1, 0.0, carry)
    while distance < groups - 1:
        carry = carry + jnp.where(team < distance, 0.0, factor * onward(carry, distance))
        distance, factor = 2 * distance, factor * factor
    carry, before = lax.optimization_barrier((carry, swap(before)))
    teams = [[g * group + k for k in range(group)] for g in range(groups)]
    carry = lax.all_gather(carry, "tm", axis_index_groups=teams)
    updated = call(
        functools.partial(finish_kernel, group), f32(*own.shape), own, power, carry, *before
    )
    return updated[None]


def solution(mesh):
    return jax.shard_map(
        shards,
        mesh=mesh,
        in_specs=(P("tm", None, "gz", None, None), P("gz", None, None)),
        out_specs=P("tm", None, "gz", None, None),
        check_vma=False,
    )
```

```python
import functools

import jax
import jax.numpy as jnp
from jax import lax
from jax.experimental import pallas as pl
from jax.experimental.pallas import tpu as pltpu
from jax.sharding import PartitionSpec as P

STEPS = 2
STAGES = 3 * STEPS
GROUP = 4
VISCOSITY = 0.05
TIME_STEP = 0.2
MIX = ((1.0, None), (0.25, 0.75), (2.0 / 3.0, 1.0 / 3.0))
VMEM = pl.BlockSpec(memory_space=pltpu.VMEM)
PARAMS = pltpu.CompilerParams(vmem_limit_bytes=16 * 1024 * 1024)


def call(kernel, out_shape, *args, scratch=(), flops=None):
    cost = None
    if flops is not None:
        cost = pl.CostEstimate(flops=flops, bytes_accessed=1 << 20, transcendentals=0)
    return pl.pallas_call(
        kernel,
        out_shape=out_shape,
        in_specs=[VMEM] * len(args),
        out_specs=jax.tree.map(lambda _: VMEM, out_shape),
        scratch_shapes=list(scratch),
        compiler_params=PARAMS,
        cost_estimate=cost,
    )(*args)


def f32(*shape):
    return jax.ShapeDtypeStruct(shape, jnp.float32)


def place():
    spot = lax.rem(lax.axis_index("tm"), GROUP)
    odd = lax.rem(lax.axis_index("gz"), 2)
    bits = (spot % 2, spot // 2)
    first = jnp.where(odd == 1, bits[1], bits[0])
    second = jnp.where(odd == 1, bits[0], bits[1])
    return spot, 1 + odd, 2 - odd, first, second


def split_rows(ref, *lead):
    half = ref.shape[-2] // 2
    return [ref[(*lead, pl.ds(odd, half, stride=2), slice(None))] for odd in (0, 1)]


def join_rows(ref, lead, pair):
    half = ref.shape[-2] // 2
    for odd in (0, 1):
        ref[(*lead, pl.ds(odd, half, stride=2), slice(None))] = pair[odd]


def load(ref, *lead):
    return [[ref[(*lead, c, odd)] for odd in (0, 1)] for c in range(3)]


def store(ref, lead, value):
    for c in range(3):
        for odd in (0, 1):
            ref[(*lead, c, odd)] = value[c][odd]


def advance(last, here, ahead, alpha, upward=1.0):
    diffuse = alpha * TIME_STEP * VISCOSITY
    carry = alpha * TIME_STEP * 0.5
    result = [[None, None] for _ in range(3)]
    for odd in (0, 1):
        speed = [here[0][odd] * carry, here[1][odd] * carry, here[2][odd] * (carry * upward)]
        to_next = [diffuse - s for s in speed]
        to_last = [diffuse + s for s in speed]
        for c in range(3):
            w = here[c][odd]
            rows, width = w.shape
            other = here[c][1 - odd]
            if odd:
                y_next, y_last = pltpu.roll(other, rows - 1, 0), other
            else:
                y_next, y_last = other, pltpu.roll(other, 1, 0)
            total = (alpha - 6.0 * diffuse) * w
            total = total + (
                to_next[0] * pltpu.roll(w, width - 1, 1) + to_last[0] * pltpu.roll(w, 1, 1)
            )
            total = total + (to_next[1] * y_next + to_last[1] * y_last)
            total = total + (to_next[2] * ahead[c][odd] + to_last[2] * last[c][odd])
            result[c][odd] = total
    return result


def blend(new, beta, base):
    return [[new[c][odd] + beta * base[c][odd] for odd in (0, 1)] for c in range(3)]


def faces_kernel(own_ref, far_ref, near_ref):
    layers, width = own_ref.shape[1], near_ref.shape[1]
    odd = lax.rem(lax.axis_index("gz"), 2)
    top = layers - width
    far_ref[...] = own_ref[:, pl.ds(odd * top, width)]
    near_ref[...] = own_ref[:, pl.ds((1 - odd) * top, width)]


def inside_kernel(own_ref, rate_ref, edges, middle, faded, damp_ref, damps, *fields):
    layers = own_ref.shape[1]
    half = layers // 2
    slices = lax.axis_size("tm")
    keep = (lax.axis_index("tm") != 0).astype(jnp.float32)

    def fill(z, _):
        for c in range(3):
            for odd, value in enumerate(split_rows(own_ref, c, z)):
                fields[0][z, c, odd] = value
        return 0

    lax.fori_loop(0, layers, fill, 0, unroll=2)

    def save(stage, field):
        for j in range(3):
            store(edges, (stage, 0, j), load(field, stage + j))
            store(edges, (stage, 1, j), load(field, layers - 1 - stage - j))

    def sweep(stage, source, target, base, alpha, beta):
        def body(turn, carry):
            below, here = carry
            for k in range(2):
                z = stage + 2 * turn + k
                above = load(source, z + 1)
                new = advance(below, here, above, alpha)
                if beta is not None:
                    new = blend(new, beta, load(base, z))
                store(target, (z,), new)
                below, here = here, above
            return below, here

        first = (load(source, stage - 1), load(source, stage))
        lax.fori_loop(0, (layers - 2 * stage) // 2, body, first)

    save(0, fields[0])
    for stage in range(1, STAGES + 1):
        kind = (stage - 1) % 3
        target = fields[(kind + 1) % 3]
        sweep(stage, fields[kind], target, fields[0], *MIX[kind])
        if stage < STAGES:
            save(stage, target)

    for z in range(layers):
        side, slot = (0, z) if z < half else (1, layers - 1 - z)
        damp = [jnp.exp(r * (-1.0 / slices)) for r in split_rows(rate_ref, z)]
        for odd in (0, 1):
            damps[side, slot, odd] = damp[odd]
        for c in range(3):
            start = split_rows(own_ref, c, z)
            for odd in (0, 1):
                lost = damp[odd] * keep * start[odd]
                if slot < STAGES:
                    faded[side, slot, c, odd] = lost
                else:
                    middle[side, slot - STAGES, c, odd] = fields[0][z, c, odd] - lost

    _, _, _, first, second = place()
    quarter = damp_ref.shape[1]
    for side in (0, 1):
        damp_ref[side] = damps[side, pl.ds((2 * first + second) * quarter, quarter)]


def border_kernel(far, face_ref, edges, middle, faded, kept, sent, strip, jumps):
    width = STAGES
    odd_slab = lax.rem(lax.axis_index("gz"), 2)
    side = odd_slab if far else 1 - odd_slab
    upward = 1.0 - 2.0 * side.astype(jnp.float32)
    for slot in range(width):
        layer = slot + side * (width - 1 - 2 * slot)
        for c in range(3):
            for odd, value in enumerate(split_rows(face_ref, c, layer)):
                strip[0, slot, c, odd] = value

    def at(stage, slot):
        if slot < width:
            return load(strip, stage, slot)
        return load(edges, stage, side, slot - width)

    def step(turn, _):
        for kind, (alpha, beta) in enumerate(MIX):
            stage = 3 * turn + kind
            last, here = at(stage, 0), at(stage, 1)
            for slot in range(width):
                ahead = at(stage, slot + 2)
                new = advance(last, here, ahead, alpha, upward)
                if beta is not None:
                    new = blend(new, beta, at(3 * turn, slot + 1 + kind))
                store(strip, (stage + 1, slot), new)
                last, here = here, ahead
        return 0

    lax.fori_loop(0, STEPS, step, 0)
    for slot in range(jumps.shape[0]):
        if slot < width:
            end, lost = load(strip, STAGES, slot), load(faded, side, slot)
            store(jumps, (slot,), [[end[c][odd] - lost[c][odd] for odd in (0, 1)] for c in range(3)])
        else:
            store(jumps, (slot,), load(middle, side, slot - width))
    _, _, _, first, _ = place()
    half = kept.shape[0]
    kept[...] = jumps[pl.ds(first * half, half)]
    sent[...] = jumps[pl.ds((1 - first) * half, half)]


def second_kernel(kept, other, sent):
    _, _, _, _, second = place()
    quarter = sent.shape[1]
    sent[0] = kept[pl.ds((1 - second) * quarter, quarter)]
    sent[1] = other[pl.ds((1 - second) * quarter, quarter)]


def in_order(kept, other, rest, order):
    spot, one, two, _, second = place()
    quarter = rest.shape[1]
    order[spot] = kept[pl.ds(second * quarter, quarter)]
    order[lax.bitwise_xor(spot, one)] = other[pl.ds(second * quarter, quarter)]
    order[lax.bitwise_xor(spot, two)] = rest[0]
    order[lax.bitwise_xor(spot, 3)] = rest[1]


def total_kernel(far, kept, other, rest, damp_ref, out, order):
    odd_slab = lax.rem(lax.axis_index("gz"), 2)
    in_order(kept, other, rest, order)
    damp = damp_ref[odd_slab if far else 1 - odd_slab][:, None]
    total = order[0]
    for j in range(1, GROUP):
        total = damp * total + order[j]
    out[...] = total


def spread_kernel(far, kept, other, rest, damp_ref, carry_ref, mine, sent, order):
    odd_slab = lax.rem(lax.axis_index("gz"), 2)
    spot, one, two, _, _ = place()
    in_order(kept, other, rest, order)
    damp = damp_ref[odd_slab if far else 1 - odd_slab][:, None]
    total = jnp.where(lax.axis_index("tm") < GROUP, 0.0, carry_ref[...])
    for j in range(GROUP):
        jump = order[j]
        order[j] = total
        total = damp * total + jump
    mine[0] = order[spot]
    mine[1] = order[lax.bitwise_xor(spot, one)]
    sent[0] = order[lax.bitwise_xor(spot, two)]
    sent[1] = order[lax.bitwise_xor(spot, 3)]


def last_kernel(mine, back, sent):
    _, _, _, _, second = place()
    quarter = mine.shape[1]
    sent[pl.ds(second * quarter, quarter)] = mine[1]
    sent[pl.ds((1 - second) * quarter, quarter)] = back[1]


def finish_kernel(own_ref, *refs):
    out = refs[-1]
    layers = out.shape[1]
    half = layers // 2
    odd_slab = lax.rem(lax.axis_index("gz"), 2)
    first_slice = lax.axis_index("tm") == 0

    @pl.when(first_slice)
    def _():
        out[...] = own_ref[...]

    @pl.when(jnp.logical_not(first_slice))
    def _():
        _, _, _, first, second = place()
        for stream, side in enumerate((odd_slab, 1 - odd_slab)):
            mine, back, rest = refs[3 * stream : 3 * stream + 3]
            quarter = mine.shape[1]

            def put(slot, ref, *lead):
                layer = slot + side * (layers - 1 - 2 * slot)
                for c in range(3):
                    join_rows(out, (c, layer), [ref[(*lead, c, odd)] for odd in (0, 1)])

            for j in range(quarter):
                put((2 * first + second) * quarter + j, mine, 0, j)
                put((2 * first + 1 - second) * quarter + j, back, 0, j)
            for j in range(2 * quarter):
                put((1 - first) * 2 * quarter + j, rest, j)


def shards(states, rate):
    slices = lax.axis_size("tm")
    slabs = lax.axis_size("gz")
    groups = slices // GROUP
    own = states[0]
    layers, rows, width = own.shape[1:]
    half = layers // 2
    quarter = half // 4
    tile = (3, 2, rows // 2, width)
    face = f32(3, STAGES, rows, width)
    team = lax.axis_index("tm") // GROUP

    def swap(value, turn):
        pairs = [
            (i * slabs + g, (i ^ (1 + (g + turn) % 2)) * slabs + g)
            for i in range(slices)
            for g in range(slabs)
        ]
        return lax.ppermute(value, ("tm", "gz"), pairs)

    def onward(value, distance):
        step = distance * GROUP
        return lax.ppermute(value, "tm", [(i, (i + step) % slices) for i in range(slices)])

    far_face, near_face = call(faces_kernel, [face, face], own)
    far_face = lax.ppermute(
        far_face, "gz", [(i, (i + 1 if i % 2 else i - 1) % slabs) for i in range(slabs)]
    )
    near_face = lax.ppermute(near_face, "gz", [(i, i ^ 1) for i in range(slabs)])
    edges, middle, faded, damp = call(
        inside_kernel,
        [
            f32(STAGES, 2, 3, *tile),
            f32(2, half - STAGES, *tile),
            f32(2, STAGES, *tile),
            f32(2, quarter, *tile[1:]),
        ],
        own, rate,
        scratch=[pltpu.VMEM((2, half, *tile[1:]), jnp.float32)]
        + [pltpu.VMEM((layers, *tile), jnp.float32)] * 3,
        flops=1 << 26,
    )
    order = pltpu.VMEM((GROUP, quarter, *tile), jnp.float32)

    def jumps(far, face):
        return call(
            functools.partial(border_kernel, far),
            [f32(2 * quarter, *tile)] * 2,
            face, edges, middle, faded,
            scratch=[
                pltpu.VMEM((STAGES + 1, STAGES, *tile), jnp.float32),
                pltpu.VMEM((half, *tile), jnp.float32),
            ],
            flops=1 << 24,
        )

    streams = []
    kept = None
    for far, face in ((False, near_face), (True, far_face)):
        if kept is not None:
            face, _ = lax.optimization_barrier((face, kept))
        kept, sent = jumps(far, face)
        other = swap(sent, 0)
        streams.append([far, kept, other])
    for stream in streams:
        _, kept, other = stream
        stream.append(swap(call(second_kernel, f32(2, quarter, *tile), kept, other), 1))
    for stream in streams:
        total = call(
            functools.partial(total_kernel, stream[0]), f32(quarter, *tile), *stream[1:], damp,
            scratch=[order],
        )
        carry = onward(total, 1)
        if groups > 2:
            side = lax.axis_index("gz") % 2
            fade = damp[side if stream[0] else 1 - side][:, None] ** GROUP
            carry = jnp.where(team < 1, 0.0, carry)
            distance = 1
            while distance < groups - 1:
                carry = carry + jnp.where(team < distance, 0.0, fade * onward(carry, distance))
                distance, fade = 2 * distance, fade * fade
        stream.append(carry)
    results = []
    for far, kept, other, rest, carry in streams:
        mine, sent = call(
            functools.partial(spread_kernel, far), [f32(2, quarter, *tile)] * 2,
            kept, other, rest, damp, carry,
            scratch=[order],
        )
        results.append((mine, swap(sent, 1)))
    pieces = []
    for mine, back in results:
        sent = call(last_kernel, f32(2 * quarter, *tile), mine, back)
        pieces = [mine, back, swap(sent, 0)] + pieces
    updated = call(finish_kernel, f32(*own.shape), own, *pieces)
    return updated[None]


def solution(mesh):
    return jax.shard_map(
        shards,
        mesh=mesh,
        in_specs=(P("tm", None, "gz", None, None), P("gz", None, None)),
        out_specs=P("tm", None, "gz", None, None),
        check_vma=False,
    )
```

```python
import functools

import jax
import jax.numpy as jnp
from jax import lax
from jax.experimental import pallas as pl
from jax.experimental.pallas import tpu as pltpu
from jax.sharding import PartitionSpec as P

STEPS = 2
STAGES = 3 * STEPS
GROUP = 4
VISCOSITY = 0.05
TIME_STEP = 0.2
MIX = ((1.0, None), (0.25, 0.75), (2.0 / 3.0, 1.0 / 3.0))
VMEM = pl.BlockSpec(memory_space=pltpu.VMEM)
PARAMS = pltpu.CompilerParams(vmem_limit_bytes=16 * 1024 * 1024)


def call(kernel, out_shape, *args, scratch=(), flops=None):
    cost = None
    if flops is not None:
        cost = pl.CostEstimate(flops=flops, bytes_accessed=1 << 20, transcendentals=0)
    return pl.pallas_call(
        kernel,
        out_shape=out_shape,
        in_specs=[VMEM] * len(args),
        out_specs=jax.tree.map(lambda _: VMEM, out_shape),
        scratch_shapes=list(scratch),
        compiler_params=PARAMS,
        cost_estimate=cost,
    )(*args)


def f32(*shape):
    return jax.ShapeDtypeStruct(shape, jnp.float32)


def partner(k):
    return (GROUP - k) % GROUP


def spot():
    return lax.rem(lax.axis_index("tm"), GROUP)


def near_side():
    return 1 - lax.rem(lax.axis_index("gz"), 2)


def is_late():
    return lax.rem((lax.axis_index("gz") + 1) // 2, 2) == 1


def split_rows(ref, *lead):
    half = ref.shape[-2] // 2
    return [ref[(*lead, pl.ds(odd, half, stride=2), slice(None))] for odd in (0, 1)]


def join_rows(ref, lead, pair):
    half = ref.shape[-2] // 2
    for odd in (0, 1):
        ref[(*lead, pl.ds(odd, half, stride=2), slice(None))] = pair[odd]


def load(ref, *lead):
    return [[ref[(*lead, c, odd)] for odd in (0, 1)] for c in range(3)]


def store(ref, lead, value):
    for c in range(3):
        for odd in (0, 1):
            ref[(*lead, c, odd)] = value[c][odd]


def advance(last, here, ahead, alpha, upward=1.0):
    diffuse = alpha * TIME_STEP * VISCOSITY
    carry = alpha * TIME_STEP * 0.5
    result = [[None, None] for _ in range(3)]
    for odd in (0, 1):
        speed = [here[0][odd] * carry, here[1][odd] * carry, here[2][odd] * (carry * upward)]
        to_next = [diffuse - s for s in speed]
        to_last = [diffuse + s for s in speed]
        for c in range(3):
            w = here[c][odd]
            rows, width = w.shape
            other = here[c][1 - odd]
            if odd:
                y_next, y_last = pltpu.roll(other, rows - 1, 0), other
            else:
                y_next, y_last = other, pltpu.roll(other, 1, 0)
            total = (alpha - 6.0 * diffuse) * w
            total = total + (
                to_next[0] * pltpu.roll(w, width - 1, 1) + to_last[0] * pltpu.roll(w, 1, 1)
            )
            total = total + (to_next[1] * y_next + to_last[1] * y_last)
            total = total + (to_next[2] * ahead[c][odd] + to_last[2] * last[c][odd])
            result[c][odd] = total
    return result


def blend(new, beta, base):
    return [[new[c][odd] + beta * base[c][odd] for odd in (0, 1)] for c in range(3)]


def faces_kernel(own_ref, far_ref, near_ref):
    layers, width = own_ref.shape[1], near_ref.shape[1]
    near = near_side()
    top = layers - width
    far_ref[...] = own_ref[:, pl.ds((1 - near) * top, width)]
    near_ref[...] = own_ref[:, pl.ds(near * top, width)]


def inside(own_ref, rate_ref, edges, middle, faded, damp_ref, damps, *fields):
    layers = own_ref.shape[1]
    half = layers // 2
    slices = lax.axis_size("tm")
    keep = (lax.axis_index("tm") != 0).astype(jnp.float32)

    def fill(z, _):
        for c in range(3):
            for odd, value in enumerate(split_rows(own_ref, c, z)):
                fields[0][z, c, odd] = value
        return 0

    lax.fori_loop(0, layers, fill, 0, unroll=2)

    def save(stage, field):
        for j in range(3):
            store(edges, (stage, 0, j), load(field, stage + j))
            store(edges, (stage, 1, j), load(field, layers - 1 - stage - j))

    def sweep(stage, source, target, base, alpha, beta):
        def body(turn, carry):
            below, here = carry
            for k in range(2):
                z = stage + 2 * turn + k
                above = load(source, z + 1)
                new = advance(below, here, above, alpha)
                if beta is not None:
                    new = blend(new, beta, load(base, z))
                store(target, (z,), new)
                below, here = here, above
            return below, here

        first = (load(source, stage - 1), load(source, stage))
        lax.fori_loop(0, (layers - 2 * stage) // 2, body, first)

    save(0, fields[0])
    for stage in range(1, STAGES + 1):
        kind = (stage - 1) % 3
        target = fields[(kind + 1) % 3]
        sweep(stage, fields[kind], target, fields[0], *MIX[kind])
        if stage < STAGES:
            save(stage, target)

    for z in range(layers):
        side, slot = (0, z) if z < half else (1, layers - 1 - z)
        damp = [jnp.exp(r * (-1.0 / slices)) for r in split_rows(rate_ref, z)]
        for odd in (0, 1):
            damps[side, slot, odd] = damp[odd]
        for c in range(3):
            start = split_rows(own_ref, c, z)
            for odd in (0, 1):
                lost = damp[odd] * keep * start[odd]
                if slot < STAGES:
                    faded[side, slot, c, odd] = lost
                else:
                    middle[side, slot - STAGES, c, odd] = fields[0][z, c, odd] - lost

    share = layers // GROUP
    place, near = spot(), near_side()
    side = jnp.where(place < GROUP // 2, near, 1 - near)
    damp_ref[...] = damps[side, pl.ds(lax.rem(place, 2) * share, share)]


def inside_kernel(late, *refs):
    @pl.when(is_late() == late)
    def _():
        inside(*refs)


def border(side, face_ref, edges, middle, faded, jumps, strip):
    width = STAGES
    upward = 1.0 - 2.0 * side.astype(jnp.float32)
    for slot in range(width):
        layer = slot + side * (width - 1 - 2 * slot)
        for c in range(3):
            for odd, value in enumerate(split_rows(face_ref, c, layer)):
                strip[0, slot, c, odd] = value

    def at(stage, slot):
        if slot < width:
            return load(strip, stage, slot)
        return load(edges, stage, side, slot - width)

    def step(turn, _):
        for kind, (alpha, beta) in enumerate(MIX):
            stage = 3 * turn + kind
            last, here = at(stage, 0), at(stage, 1)
            for slot in range(width):
                ahead = at(stage, slot + 2)
                new = advance(last, here, ahead, alpha, upward)
                if beta is not None:
                    new = blend(new, beta, at(3 * turn, slot + 1 + kind))
                store(strip, (stage + 1, slot), new)
                last, here = here, ahead
        return 0

    lax.fori_loop(0, STEPS, step, 0)
    for slot in range(jumps.shape[0]):
        if slot < width:
            end, lost = load(strip, STAGES, slot), load(faded, side, slot)
            store(jumps, (slot,), [[end[c][odd] - lost[c][odd] for odd in (0, 1)] for c in range(3)])
        else:
            store(jumps, (slot,), load(middle, side, slot - width))


def near_kernel(face_ref, early, late, jumps, strip):
    for flag, refs in ((False, early), (True, late)):

        @pl.when(is_late() == flag)
        def _():
            border(near_side(), face_ref, *refs[:3], jumps, strip)


def far_kernel(face_ref, early, late, near_jumps, outs, strip, jumps):
    for flag, refs in ((False, early), (True, late)):

        @pl.when(is_late() == flag)
        def _():
            border(1 - near_side(), face_ref, *refs[:3], jumps.at[1], strip)

    jumps[0] = near_jumps[...]
    share = outs[0].shape[0]
    for k, out in enumerate(outs):
        chunk = lax.bitwise_xor(spot(), partner(k))
        out[...] = jumps[chunk // 2, pl.ds(lax.rem(chunk, 2) * share, share)]


def damp_of(early, late):
    return jnp.where(is_late(), late[3][...], early[3][...])[:, None]


def total_kernel(jumps, early, late, out, order):
    for k in range(GROUP):
        order[lax.bitwise_xor(spot(), partner(k))] = jumps[k][...]
    damp = damp_of(early, late)
    total = order[0]
    for j in range(1, GROUP):
        total = damp * total + order[j]
    out[...] = total


def spread_kernel(jumps, early, late, carry_ref, outs, order):
    for k in range(GROUP):
        order[lax.bitwise_xor(spot(), partner(k))] = jumps[k][...]
    damp = damp_of(early, late)
    total = jnp.where(lax.axis_index("tm") < GROUP, 0.0, carry_ref[...])
    for j in range(GROUP):
        jump = order[j]
        order[j] = total
        total = damp * total + jump
    for k in range(GROUP):
        outs[k][...] = order[lax.bitwise_xor(spot(), partner(k))]


def finish_kernel(own_ref, pieces, out):
    layers = out.shape[1]
    share = layers // GROUP
    first_slice = lax.axis_index("tm") == 0

    @pl.when(first_slice)
    def _():
        out[...] = own_ref[...]

    @pl.when(jnp.logical_not(first_slice))
    def _():
        near = near_side()
        for k, piece in enumerate(pieces):
            chunk = lax.bitwise_xor(spot(), partner(k))
            side = jnp.where(chunk < GROUP // 2, near, 1 - near)
            for j in range(share):
                slot = lax.rem(chunk, 2) * share + j
                layer = slot + side * (layers - 1 - 2 * slot)
                for c in range(3):
                    join_rows(out, (c, layer), [piece[j, c, odd] for odd in (0, 1)])


def shards(states, rate):
    slices = lax.axis_size("tm")
    slabs = lax.axis_size("gz")
    groups = slices // GROUP
    own = states[0]
    layers, rows, width = own.shape[1:]
    half, share = layers // 2, layers // GROUP
    tile = (3, 2, rows // 2, width)
    face = f32(3, STAGES, rows, width)
    piece = f32(share, *tile)
    team = lax.axis_index("tm") // GROUP

    def halo(value, pairs):
        return lax.ppermute(value, "gz", [(i, j % slabs) for i, j in pairs])

    def swap(parts):
        return [parts[0]] + [
            lax.ppermute(parts[k], "tm", [(i, i ^ partner(k)) for i in range(slices)])
            for k in range(1, GROUP)
        ]

    def onward(value, distance):
        step = distance * GROUP
        return lax.ppermute(value, "tm", [(i, (i + step) % slices) for i in range(slices)])

    def inner(late, flops):
        return call(
            functools.partial(inside_kernel, late),
            [
                f32(STAGES, 2, 3, *tile),
                f32(2, half - STAGES, *tile),
                f32(2, STAGES, *tile),
                f32(share, *tile[1:]),
            ],
            own, rate,
            scratch=[pltpu.VMEM((2, half, *tile[1:]), jnp.float32)]
            + [pltpu.VMEM((layers, *tile), jnp.float32)] * 3,
            flops=flops,
        )

    def step(kernel, out_shape, *args, scratch=(), flops=None):
        leaves, tree = jax.tree.flatten((args, out_shape))
        inputs = jax.tree.leaves(args)

        def flat(*refs):
            count = len(leaves)
            nested = jax.tree.unflatten(tree, refs[:count])
            kernel(*nested[0], nested[1], *refs[count:])

        return call(flat, out_shape, *inputs, scratch=scratch, flops=flops)

    far_face, near_face = call(faces_kernel, [face, face], own)
    near_face = halo(near_face, [(i, i ^ 1) for i in range(slabs)])
    late = inner(True, 1 << 34)
    far_face, _ = lax.optimization_barrier((far_face, late[3]))
    far_face = halo(far_face, [(i, i + 1 if i % 2 else i - 1 + slabs) for i in range(slabs)])
    early = inner(False, 1 << 20)
    strip = pltpu.VMEM((STAGES + 1, STAGES, *tile), jnp.float32)
    near_jumps = step(near_kernel, f32(half, *tile), near_face, early, late, scratch=[strip])
    far_face, near_jumps = lax.optimization_barrier((far_face, near_jumps))
    jumps = step(
        far_kernel, [piece] * GROUP, far_face, early, late, near_jumps,
        scratch=[strip, pltpu.VMEM((2, half, *tile), jnp.float32)],
    )
    jumps = swap(jumps)
    order = pltpu.VMEM((GROUP, *piece.shape), jnp.float32)
    if groups > 1:
        carry = onward(step(total_kernel, piece, jumps, early, late, scratch=[order]), 1)
        if groups > 2:
            turn = lax.rem((lax.axis_index("gz") + 1) // 2, 2) == 1
            fade = jnp.where(turn, late[3], early[3])[:, None] ** GROUP
            carry = jnp.where(team < 1, 0.0, carry)
            distance = 1
            while distance < groups - 1:
                carry = carry + jnp.where(team < distance, 0.0, fade * onward(carry, distance))
                distance, fade = 2 * distance, fade * fade
    else:
        carry = jnp.zeros(piece.shape, jnp.float32)
    news = step(spread_kernel, [piece] * GROUP, jumps, early, late, carry, scratch=[order])
    updated = step(finish_kernel, f32(*own.shape), own, swap(news))
    return updated[None]


def solution(mesh):
    return jax.shard_map(
        shards,
        mesh=mesh,
        in_specs=(P("tm", None, "gz", None, None), P("gz", None, None)),
        out_specs=P("tm", None, "gz", None, None),
        check_vma=False,
    )
```

```python
import functools

import jax
import jax.numpy as jnp
from jax import lax
from jax.experimental import pallas as pl
from jax.experimental.pallas import tpu as pltpu
from jax.sharding import PartitionSpec as P

STEPS = 2
STAGES = 3 * STEPS
GROUP = 4
VISCOSITY = 0.05
TIME_STEP = 0.2
MIX = ((1.0, None), (0.25, 0.75), (2.0 / 3.0, 1.0 / 3.0))
VMEM = pl.BlockSpec(memory_space=pltpu.VMEM)
PARAMS = pltpu.CompilerParams(vmem_limit_bytes=16 * 1024 * 1024)


def call(kernel, out_shape, *args, scratch=(), flops=None):
    cost = None
    if flops is not None:
        cost = pl.CostEstimate(flops=flops, bytes_accessed=1 << 20, transcendentals=0)
    return pl.pallas_call(
        kernel,
        out_shape=out_shape,
        in_specs=[VMEM] * len(args),
        out_specs=jax.tree.map(lambda _: VMEM, out_shape),
        scratch_shapes=list(scratch),
        compiler_params=PARAMS,
        cost_estimate=cost,
    )(*args)


def f32(*shape):
    return jax.ShapeDtypeStruct(shape, jnp.float32)


def partner(k):
    return (GROUP - k) % GROUP


def spot():
    return lax.rem(lax.axis_index("tm"), GROUP)


def near_side():
    return 1 - lax.rem(lax.axis_index("gz"), 2)


def split_rows(ref, *lead):
    half = ref.shape[-2] // 2
    return [ref[(*lead, pl.ds(odd, half, stride=2), slice(None))] for odd in (0, 1)]


def join_rows(ref, lead, pair):
    half = ref.shape[-2] // 2
    for odd in (0, 1):
        ref[(*lead, pl.ds(odd, half, stride=2), slice(None))] = pair[odd]


def load(ref, *lead):
    return [[ref[(*lead, c, odd)] for odd in (0, 1)] for c in range(3)]


def store(ref, lead, value):
    for c in range(3):
        for odd in (0, 1):
            ref[(*lead, c, odd)] = value[c][odd]


def advance(last, here, ahead, alpha, upward=1.0):
    diffuse = alpha * TIME_STEP * VISCOSITY
    carry = alpha * TIME_STEP * 0.5
    result = [[None, None] for _ in range(3)]
    for odd in (0, 1):
        speed = [here[0][odd] * carry, here[1][odd] * carry, here[2][odd] * (carry * upward)]
        to_next = [diffuse - s for s in speed]
        to_last = [diffuse + s for s in speed]
        for c in range(3):
            w = here[c][odd]
            rows, width = w.shape
            other = here[c][1 - odd]
            if odd:
                y_next, y_last = pltpu.roll(other, rows - 1, 0), other
            else:
                y_next, y_last = other, pltpu.roll(other, 1, 0)
            total = (alpha - 6.0 * diffuse) * w
            total = total + (
                to_next[0] * pltpu.roll(w, width - 1, 1) + to_last[0] * pltpu.roll(w, 1, 1)
            )
            total = total + (to_next[1] * y_next + to_last[1] * y_last)
            total = total + (to_next[2] * ahead[c][odd] + to_last[2] * last[c][odd])
            result[c][odd] = total
    return result


def blend(new, beta, base):
    return [[new[c][odd] + beta * base[c][odd] for odd in (0, 1)] for c in range(3)]


def faces_kernel(own_ref, far_ref, near_ref):
    layers, width = own_ref.shape[1], near_ref.shape[1]
    near = near_side()
    top = layers - width
    far_ref[...] = own_ref[:, pl.ds((1 - near) * top, width)]
    near_ref[...] = own_ref[:, pl.ds(near * top, width)]


def inside_kernel(own_ref, rate_ref, edges, middle, faded, damp_ref, damps, *fields):
    layers = own_ref.shape[1]
    half = layers // 2
    slices = lax.axis_size("tm")
    keep = (lax.axis_index("tm") != 0).astype(jnp.float32)

    def fill(z, _):
        for c in range(3):
            for odd, value in enumerate(split_rows(own_ref, c, z)):
                fields[0][z, c, odd] = value
        return 0

    lax.fori_loop(0, layers, fill, 0, unroll=2)

    def save(stage, field):
        for j in range(3):
            store(edges, (stage, 0, j), load(field, stage + j))
            store(edges, (stage, 1, j), load(field, layers - 1 - stage - j))

    def sweep(stage, source, target, base, alpha, beta):
        def body(turn, carry):
            below, here = carry
            for k in range(2):
                z = stage + 2 * turn + k
                above = load(source, z + 1)
                new = advance(below, here, above, alpha)
                if beta is not None:
                    new = blend(new, beta, load(base, z))
                store(target, (z,), new)
                below, here = here, above
            return below, here

        first = (load(source, stage - 1), load(source, stage))
        lax.fori_loop(0, (layers - 2 * stage) // 2, body, first)

    save(0, fields[0])
    for stage in range(1, STAGES + 1):
        kind = (stage - 1) % 3
        target = fields[(kind + 1) % 3]
        sweep(stage, fields[kind], target, fields[0], *MIX[kind])
        if stage < STAGES:
            save(stage, target)

    for z in range(layers):
        side, slot = (0, z) if z < half else (1, layers - 1 - z)
        damp = [jnp.exp(r * (-1.0 / slices)) for r in split_rows(rate_ref, z)]
        for odd in (0, 1):
            damps[side, slot, odd] = damp[odd]
        for c in range(3):
            start = split_rows(own_ref, c, z)
            for odd in (0, 1):
                lost = damp[odd] * keep * start[odd]
                if slot < STAGES:
                    faded[side, slot, c, odd] = lost
                else:
                    middle[side, slot - STAGES, c, odd] = fields[0][z, c, odd] - lost

    share = layers // GROUP
    place, near = spot(), near_side()
    side = jnp.where(place < GROUP // 2, near, 1 - near)
    damp_ref[...] = damps[side, pl.ds(lax.rem(place, 2) * share, share)]


def border(side, face_ref, edges, middle, faded, jumps, strip):
    width = STAGES
    upward = 1.0 - 2.0 * side.astype(jnp.float32)
    for slot in range(width):
        layer = slot + side * (width - 1 - 2 * slot)
        for c in range(3):
            for odd, value in enumerate(split_rows(face_ref, c, layer)):
                strip[0, slot, c, odd] = value

    def at(stage, slot):
        if slot < width:
            return load(strip, stage, slot)
        return load(edges, stage, side, slot - width)

    def step(turn, _):
        for kind, (alpha, beta) in enumerate(MIX):
            stage = 3 * turn + kind
            last, here = at(stage, 0), at(stage, 1)
            for slot in range(width):
                ahead = at(stage, slot + 2)
                new = advance(last, here, ahead, alpha, upward)
                if beta is not None:
                    new = blend(new, beta, at(3 * turn, slot + 1 + kind))
                store(strip, (stage + 1, slot), new)
                last, here = here, ahead
        return 0

    lax.fori_loop(0, STEPS, step, 0)
    for slot in range(jumps.shape[0]):
        if slot < width:
            end, lost = load(strip, STAGES, slot), load(faded, side, slot)
            store(jumps, (slot,), [[end[c][odd] - lost[c][odd] for odd in (0, 1)] for c in range(3)])
        else:
            store(jumps, (slot,), load(middle, side, slot - width))


def near_kernel(face_ref, edges, middle, faded, jumps, strip):
    border(near_side(), face_ref, edges, middle, faded, jumps, strip)


def far_kernel(face_ref, edges, middle, faded, near_jumps, *refs):
    outs, strip, jumps = refs[:GROUP], refs[GROUP], refs[GROUP + 1]
    border(1 - near_side(), face_ref, edges, middle, faded, jumps.at[1], strip)
    jumps[0] = near_jumps[...]
    share = outs[0].shape[0]
    for k, out in enumerate(outs):
        chunk = lax.bitwise_xor(spot(), partner(k))
        out[...] = jumps[chunk // 2, pl.ds(lax.rem(chunk, 2) * share, share)]


def sort_in(jumps, order):
    for k in range(GROUP):
        order[lax.bitwise_xor(spot(), partner(k))] = jumps[k][...]


def sort_out(order, outs):
    for k in range(GROUP):
        outs[k][...] = order[lax.bitwise_xor(spot(), partner(k))]


def run(order, damp, total):
    for j in range(GROUP):
        jump = order[j]
        order[j] = total
        total = damp * total + jump
    return total


def total_kernel(*refs):
    jumps, damp_ref, out, order = refs[:GROUP], refs[GROUP], refs[GROUP + 1], refs[GROUP + 2]
    sort_in(jumps, order)
    out[...] = run(order, damp_ref[...][:, None], jnp.zeros(out.shape, jnp.float32))


def spread_kernel(*refs):
    carry_ref, jumps, damp_ref = refs[0], refs[1 : 1 + GROUP], refs[1 + GROUP]
    outs, order = refs[GROUP + 2 : -1], refs[-1]
    sort_in(jumps, order)
    run(order, damp_ref[...][:, None], jnp.where(lax.axis_index("tm") < GROUP, 0.0, carry_ref[...]))
    sort_out(order, outs)


def lead_kernel(*refs):
    jumps, damp_ref, out = refs[:GROUP], refs[GROUP], refs[GROUP + 1]
    outs, order = refs[GROUP + 2 : -1], refs[-1]
    leading = lax.axis_index("tm") < GROUP

    @pl.when(leading)
    def _():
        sort_in(jumps, order)
        out[...] = run(order, damp_ref[...][:, None], jnp.zeros(out.shape, jnp.float32))
        sort_out(order, outs)

    @pl.when(jnp.logical_not(leading))
    def _():
        out[...] = jnp.zeros_like(out)
        for k in range(GROUP):
            outs[k][...] = jumps[k][...]


def finish_kernel(own_ref, *refs):
    out, whole, sems = refs[-3], refs[-2], refs[-1]
    others, leading = refs[:GROUP], refs[-3 - GROUP : -3]
    layers = own_ref.shape[1]
    share = layers // GROUP
    mine = lax.axis_index("tm")
    near = near_side()

    def place(k):
        chunk = lax.bitwise_xor(spot(), partner(k))
        side = jnp.where(chunk < GROUP // 2, near, 1 - near)
        return side, lax.rem(chunk, 2) * share

    def copy(k):
        side, slot = place(k)
        span = pl.ds(slot + side * (layers - share - 2 * slot), share)
        return pltpu.make_async_copy(whole.at[:, span], out.at[:, span], sems.at[k])

    def join(pieces):
        for k, piece in enumerate(pieces):
            side, slot = place(k)
            for j in range(share):
                layer = slot + j + side * (layers - 1 - 2 * (slot + j))
                for c in range(3):
                    join_rows(whole, (c, layer), [piece[j, c, odd] for odd in (0, 1)])
            copy(k).start()

    @pl.when(mine == 0)
    def _():
        whole[...] = own_ref[...]
        for k in range(GROUP):
            copy(k).start()

    @pl.when(jnp.logical_and(mine > 0, mine < GROUP))
    def _():
        join(leading)

    @pl.when(mine >= GROUP)
    def _():
        join(others)

    for k in range(GROUP):
        copy(k).wait()


def shards(states, rate):
    slices = lax.axis_size("tm")
    slabs = lax.axis_size("gz")
    groups = slices // GROUP
    own = states[0]
    layers, rows, width = own.shape[1:]
    half, share = layers // 2, layers // GROUP
    tile = (3, 2, rows // 2, width)
    face = f32(3, STAGES, rows, width)
    piece = f32(share, *tile)

    def halo(value, pairs):
        return lax.ppermute(value, "gz", [(i, j % slabs) for i, j in pairs])

    def swap(parts, active):
        return [parts[0]] + [
            lax.ppermute(
                parts[k], "tm", [(i, i ^ partner(k) if active(i) else i) for i in range(slices)]
            )
            for k in range(1, GROUP)
        ]

    def onward(value, distance):
        step = distance * GROUP
        return lax.ppermute(value, "tm", [(i, i + step) for i in range(slices - step)])

    far_face, near_face = call(faces_kernel, [face, face], own)
    near_face = halo(near_face, [(i, i ^ 1) for i in range(slabs)])
    far_face = halo(far_face, [(i, i + 1 if i % 2 else i - 1 + slabs) for i in range(slabs)])
    edges, middle, faded, damp = call(
        inside_kernel,
        [
            f32(STAGES, 2, 3, *tile),
            f32(2, half - STAGES, *tile),
            f32(2, STAGES, *tile),
            f32(share, *tile[1:]),
        ],
        own, rate,
        scratch=[pltpu.VMEM((2, half, *tile[1:]), jnp.float32)]
        + [pltpu.VMEM((layers, *tile), jnp.float32)] * 3,
        flops=1 << 26,
    )
    strip = pltpu.VMEM((STAGES + 1, STAGES, *tile), jnp.float32)
    near_jumps = call(
        near_kernel, f32(half, *tile), near_face, edges, middle, faded, scratch=[strip], flops=1 << 24
    )
    jumps = call(
        far_kernel, [piece] * GROUP, far_face, edges, middle, faded, near_jumps,
        scratch=[strip, pltpu.VMEM((2, half, *tile), jnp.float32)],
    )
    order = pltpu.VMEM((GROUP, *piece.shape), jnp.float32)
    if groups == 2:
        jumps = swap(jumps, lambda i: i < GROUP)
        total, *parts = call(lead_kernel, [piece] * (1 + GROUP), *jumps, damp, scratch=[order])
        carry = onward(total, 1)
        jumps = swap(parts, lambda i: True)
        news = call(spread_kernel, [piece] * GROUP, carry, *jumps, damp, scratch=[order])
        pieces = [*swap(news, lambda i: i >= GROUP), *jumps]
    else:
        jumps = swap(jumps, lambda i: True)
        total = call(total_kernel, piece, *jumps, damp, scratch=[order])
        carry, fade, distance = onward(total, 1), damp[:, None] ** GROUP, 1
        while distance < groups - 1:
            carry = carry + fade * onward(carry, distance)
            distance, fade = 2 * distance, fade * fade
        news = call(spread_kernel, [piece] * GROUP, carry, *jumps, damp, scratch=[order])
        pieces = swap(news, lambda i: True)
    updated = pl.pallas_call(
        finish_kernel,
        out_shape=f32(*own.shape),
        in_specs=[VMEM] * (1 + len(pieces)),
        out_specs=pl.BlockSpec(memory_space=pl.ANY),
        scratch_shapes=[pltpu.VMEM(own.shape, jnp.float32), pltpu.SemaphoreType.DMA((GROUP,))],
        compiler_params=PARAMS,
    )(own, *pieces)
    return updated[None]


def solution(mesh):
    return jax.shard_map(
        shards,
        mesh=mesh,
        in_specs=(P("tm", None, "gz", None, None), P("gz", None, None)),
        out_specs=P("tm", None, "gz", None, None),
        check_vma=False,
    )
```

```python
import functools

import jax
import jax.numpy as jnp
from jax import lax
from jax.experimental import pallas as pl
from jax.experimental.pallas import tpu as pltpu
from jax.sharding import PartitionSpec as P

STEPS = 2
STAGES = 3 * STEPS
GROUP = 4
VISCOSITY = 0.05
TIME_STEP = 0.2
MIX = ((1.0, None), (0.25, 0.75), (2.0 / 3.0, 1.0 / 3.0))
VMEM = pl.BlockSpec(memory_space=pltpu.VMEM)
PARAMS = pltpu.CompilerParams(vmem_limit_bytes=16 * 1024 * 1024)


def call(kernel, out_shape, *args, scratch=(), flops=None):
    cost = None
    if flops is not None:
        cost = pl.CostEstimate(flops=flops, bytes_accessed=1 << 20, transcendentals=0)
    return pl.pallas_call(
        kernel,
        out_shape=out_shape,
        in_specs=[VMEM] * len(args),
        out_specs=jax.tree.map(lambda _: VMEM, out_shape),
        scratch_shapes=list(scratch),
        compiler_params=PARAMS,
        cost_estimate=cost,
    )(*args)


def f32(*shape):
    return jax.ShapeDtypeStruct(shape, jnp.float32)


def partner(k):
    return (GROUP - k) % GROUP


def spot():
    return lax.rem(lax.axis_index("tm"), GROUP)


def chunk_of(k):
    flip = 2 * lax.rem(lax.axis_index("tm") // GROUP, 2)
    return lax.bitwise_xor(lax.bitwise_xor(spot(), flip), partner(k))


def near_side():
    return 1 - lax.rem(lax.axis_index("gz"), 2)


def split_rows(ref, *lead):
    half = ref.shape[-2] // 2
    return [ref[(*lead, pl.ds(odd, half, stride=2), slice(None))] for odd in (0, 1)]


def join_rows(ref, lead, pair):
    half = ref.shape[-2] // 2
    for odd in (0, 1):
        ref[(*lead, pl.ds(odd, half, stride=2), slice(None))] = pair[odd]


def load(ref, *lead):
    return [[ref[(*lead, c, odd)] for odd in (0, 1)] for c in range(3)]


def store(ref, lead, value):
    for c in range(3):
        for odd in (0, 1):
            ref[(*lead, c, odd)] = value[c][odd]


def advance(last, here, ahead, alpha, upward=1.0):
    diffuse = alpha * TIME_STEP * VISCOSITY
    carry = alpha * TIME_STEP * 0.5
    result = [[None, None] for _ in range(3)]
    for odd in (0, 1):
        speed = [here[0][odd] * carry, here[1][odd] * carry, here[2][odd] * (carry * upward)]
        to_next = [diffuse - s for s in speed]
        to_last = [diffuse + s for s in speed]
        for c in range(3):
            w = here[c][odd]
            rows, width = w.shape
            other = here[c][1 - odd]
            if odd:
                y_next, y_last = pltpu.roll(other, rows - 1, 0), other
            else:
                y_next, y_last = other, pltpu.roll(other, 1, 0)
            total = (alpha - 6.0 * diffuse) * w
            total = total + (
                to_next[0] * pltpu.roll(w, width - 1, 1) + to_last[0] * pltpu.roll(w, 1, 1)
            )
            total = total + (to_next[1] * y_next + to_last[1] * y_last)
            total = total + (to_next[2] * ahead[c][odd] + to_last[2] * last[c][odd])
            result[c][odd] = total
    return result


def blend(new, beta, base):
    return [[new[c][odd] + beta * base[c][odd] for odd in (0, 1)] for c in range(3)]


def faces_kernel(own_ref, far_ref, near_ref):
    layers, width = own_ref.shape[1], near_ref.shape[1]
    near = near_side()
    top = layers - width
    far_ref[...] = own_ref[:, pl.ds((1 - near) * top, width)]
    near_ref[...] = own_ref[:, pl.ds(near * top, width)]


def inside_kernel(own_ref, rate_ref, edges, middle, faded, damp_ref, damps, *fields):
    layers = own_ref.shape[1]
    half = layers // 2
    slices = lax.axis_size("tm")
    keep = (lax.axis_index("tm") != 0).astype(jnp.float32)

    def fill(z, _):
        for c in range(3):
            for odd, value in enumerate(split_rows(own_ref, c, z)):
                fields[0][z, c, odd] = value
        return 0

    lax.fori_loop(0, layers, fill, 0, unroll=2)

    def save(stage, field):
        for j in range(3):
            store(edges, (stage, 0, j), load(field, stage + j))
            store(edges, (stage, 1, j), load(field, layers - 1 - stage - j))

    def sweep(stage, source, target, base, alpha, beta):
        def body(turn, carry):
            below, here = carry
            for k in range(2):
                z = stage + 2 * turn + k
                above = load(source, z + 1)
                new = advance(below, here, above, alpha)
                if beta is not None:
                    new = blend(new, beta, load(base, z))
                store(target, (z,), new)
                below, here = here, above
            return below, here

        first = (load(source, stage - 1), load(source, stage))
        lax.fori_loop(0, (layers - 2 * stage) // 2, body, first)

    save(0, fields[0])
    for stage in range(1, STAGES + 1):
        kind = (stage - 1) % 3
        target = fields[(kind + 1) % 3]
        sweep(stage, fields[kind], target, fields[0], *MIX[kind])
        if stage < STAGES:
            save(stage, target)

    for z in range(layers):
        side, slot = (0, z) if z < half else (1, layers - 1 - z)
        damp = [jnp.exp(r * (-1.0 / slices)) for r in split_rows(rate_ref, z)]
        for odd in (0, 1):
            damps[side, slot, odd] = damp[odd]
        for c in range(3):
            start = split_rows(own_ref, c, z)
            for odd in (0, 1):
                lost = damp[odd] * keep * start[odd]
                if slot < STAGES:
                    faded[side, slot, c, odd] = lost
                else:
                    middle[side, slot - STAGES, c, odd] = fields[0][z, c, odd] - lost

    share = layers // GROUP
    chunk, near = chunk_of(0), near_side()
    side = jnp.where(chunk < GROUP // 2, near, 1 - near)
    damp_ref[...] = damps[side, pl.ds(lax.rem(chunk, 2) * share, share)]


def border(side, face_ref, edges, middle, faded, jumps, strip):
    width = STAGES
    upward = 1.0 - 2.0 * side.astype(jnp.float32)
    for slot in range(width):
        layer = slot + side * (width - 1 - 2 * slot)
        for c in range(3):
            for odd, value in enumerate(split_rows(face_ref, c, layer)):
                strip[0, slot, c, odd] = value

    def at(stage, slot):
        if slot < width:
            return load(strip, stage, slot)
        return load(edges, stage, side, slot - width)

    def step(turn, _):
        for kind, (alpha, beta) in enumerate(MIX):
            stage = 3 * turn + kind
            last, here = at(stage, 0), at(stage, 1)
            for slot in range(width):
                ahead = at(stage, slot + 2)
                new = advance(last, here, ahead, alpha, upward)
                if beta is not None:
                    new = blend(new, beta, at(3 * turn, slot + 1 + kind))
                store(strip, (stage + 1, slot), new)
                last, here = here, ahead
        return 0

    lax.fori_loop(0, STEPS, step, 0)
    for slot in range(jumps.shape[0]):
        if slot < width:
            end, lost = load(strip, STAGES, slot), load(faded, side, slot)
            store(jumps, (slot,), [[end[c][odd] - lost[c][odd] for odd in (0, 1)] for c in range(3)])
        else:
            store(jumps, (slot,), load(middle, side, slot - width))


def near_kernel(face_ref, edges, middle, faded, jumps, strip):
    border(near_side(), face_ref, edges, middle, faded, jumps, strip)


def far_kernel(face_ref, edges, middle, faded, near_jumps, *refs):
    outs, strip, jumps = refs[:GROUP], refs[GROUP], refs[GROUP + 1]
    border(1 - near_side(), face_ref, edges, middle, faded, jumps.at[1], strip)
    jumps[0] = near_jumps[...]
    share = outs[0].shape[0]
    for k, out in enumerate(outs):
        chunk = chunk_of(k)
        out[...] = jumps[chunk // 2, pl.ds(lax.rem(chunk, 2) * share, share)]


def sort_in(jumps, order):
    for k in range(GROUP):
        order[lax.bitwise_xor(spot(), partner(k))] = jumps[k][...]


def sort_out(order, outs):
    for k in range(GROUP):
        outs[k][...] = order[lax.bitwise_xor(spot(), partner(k))]


def run(order, damp, total):
    for j in range(GROUP):
        jump = order[j]
        order[j] = total
        total = damp * total + jump
    return total


def total_kernel(*refs):
    jumps, damp_ref, out, order = refs[:GROUP], refs[GROUP], refs[GROUP + 1], refs[GROUP + 2]
    sort_in(jumps, order)
    out[...] = run(order, damp_ref[...][:, None], jnp.zeros(out.shape, jnp.float32))


def spread_kernel(*refs):
    carry_ref, jumps, damp_ref = refs[0], refs[1 : 1 + GROUP], refs[1 + GROUP]
    outs, order = refs[GROUP + 2 : -1], refs[-1]
    sort_in(jumps, order)
    run(order, damp_ref[...][:, None], jnp.where(lax.axis_index("tm") < GROUP, 0.0, carry_ref[...]))
    sort_out(order, outs)


def finish_kernel(own_ref, *refs):
    pieces, out = refs[:GROUP], refs[GROUP]
    layers = out.shape[1]
    share = layers // GROUP
    first_slice = lax.axis_index("tm") == 0

    @pl.when(first_slice)
    def _():
        out[...] = own_ref[...]

    @pl.when(jnp.logical_not(first_slice))
    def _():
        near = near_side()
        for k, piece in enumerate(pieces):
            chunk = chunk_of(k)
            side = jnp.where(chunk < GROUP // 2, near, 1 - near)
            for j in range(share):
                slot = lax.rem(chunk, 2) * share + j
                layer = slot + side * (layers - 1 - 2 * slot)
                for c in range(3):
                    join_rows(out, (c, layer), [piece[j, c, odd] for odd in (0, 1)])


def shards(states, rate):
    slices = lax.axis_size("tm")
    slabs = lax.axis_size("gz")
    groups = slices // GROUP
    own = states[0]
    layers, rows, width = own.shape[1:]
    half, share = layers // 2, layers // GROUP
    tile = (3, 2, rows // 2, width)
    face = f32(3, STAGES, rows, width)
    piece = f32(share, *tile)
    team = lax.axis_index("tm") // GROUP

    def halo(value, pairs):
        return lax.ppermute(value, "gz", [(i, j % slabs) for i, j in pairs])

    def swap(parts):
        return [parts[0]] + [
            lax.ppermute(parts[k], "tm", [(i, i ^ partner(k)) for i in range(slices)])
            for k in range(1, GROUP)
        ]

    def onward(value, distance):
        flip = 2 * (distance % 2)
        pairs = [(i, ((i ^ flip) + distance * GROUP) % slices) for i in range(slices)]
        return lax.ppermute(value, "tm", pairs)

    far_face, near_face = call(faces_kernel, [face, face], own)
    near_face = halo(near_face, [(i, i ^ 1) for i in range(slabs)])
    far_face = halo(far_face, [(i, i + 1 if i % 2 else i - 1 + slabs) for i in range(slabs)])
    edges, middle, faded, damp = call(
        inside_kernel,
        [
            f32(STAGES, 2, 3, *tile),
            f32(2, half - STAGES, *tile),
            f32(2, STAGES, *tile),
            f32(share, *tile[1:]),
        ],
        own, rate,
        scratch=[pltpu.VMEM((2, half, *tile[1:]), jnp.float32)]
        + [pltpu.VMEM((layers, *tile), jnp.float32)] * 3,
        flops=1 << 26,
    )
    strip = pltpu.VMEM((STAGES + 1, STAGES, *tile), jnp.float32)
    near_jumps = call(
        near_kernel, f32(half, *tile), near_face, edges, middle, faded, scratch=[strip], flops=1 << 24
    )
    jumps = call(
        far_kernel, [piece] * GROUP, far_face, edges, middle, faded, near_jumps,
        scratch=[strip, pltpu.VMEM((2, half, *tile), jnp.float32)],
    )
    order = pltpu.VMEM((GROUP, *piece.shape), jnp.float32)
    jumps = swap(jumps)
    if groups > 1:
        total = call(total_kernel, piece, *jumps, damp, scratch=[order])
        carry = onward(total, 1)
        if groups > 2:
            carry = jnp.where(team < 1, 0.0, carry)
            fade, distance = damp[:, None] ** GROUP, 1
            while distance < groups - 1:
                carry = carry + jnp.where(team < distance, 0.0, fade * onward(carry, distance))
                distance, fade = 2 * distance, fade * fade
    else:
        carry = jnp.zeros(piece.shape, jnp.float32)
    news = call(spread_kernel, [piece] * GROUP, carry, *jumps, damp, scratch=[order])
    updated = call(finish_kernel, f32(*own.shape), own, *swap(news))
    return updated[None]


def solution(mesh):
    return jax.shard_map(
        shards,
        mesh=mesh,
        in_specs=(P("tm", None, "gz", None, None), P("gz", None, None)),
        out_specs=P("tm", None, "gz", None, None),
        check_vma=False,
    )
```

```python
import functools

import jax
import jax.numpy as jnp
from jax import lax
from jax.experimental import pallas as pl
from jax.experimental.pallas import tpu as pltpu
from jax.sharding import PartitionSpec as P

STEPS = 2
STAGES = 3 * STEPS
GROUP = 4
VISCOSITY = 0.05
TIME_STEP = 0.2
MIX = ((1.0, None), (0.25, 0.75), (2.0 / 3.0, 1.0 / 3.0))
VMEM = pl.BlockSpec(memory_space=pltpu.VMEM)
PARAMS = pltpu.CompilerParams(vmem_limit_bytes=16 * 1024 * 1024)


def call(kernel, out_shape, *args, scratch=(), flops=None):
    cost = None
    if flops is not None:
        cost = pl.CostEstimate(flops=flops, bytes_accessed=1 << 20, transcendentals=0)
    return pl.pallas_call(
        kernel,
        out_shape=out_shape,
        in_specs=[VMEM] * len(args),
        out_specs=jax.tree.map(lambda _: VMEM, out_shape),
        scratch_shapes=list(scratch),
        compiler_params=PARAMS,
        cost_estimate=cost,
    )(*args)


def f32(*shape):
    return jax.ShapeDtypeStruct(shape, jnp.float32)


def partner(k):
    return (GROUP - k) % GROUP


def spot():
    return lax.rem(lax.axis_index("tm"), GROUP)


def chunk_of(k):
    flip = 2 * lax.rem(lax.axis_index("tm") // GROUP, 2)
    return lax.bitwise_xor(lax.bitwise_xor(spot(), flip), partner(k))


def near_side():
    return 1 - lax.rem(lax.axis_index("gz"), 2)


def split_rows(ref, *lead):
    half = ref.shape[-2] // 2
    return [ref[(*lead, pl.ds(odd, half, stride=2), slice(None))] for odd in (0, 1)]


def join_rows(ref, lead, pair):
    half = ref.shape[-2] // 2
    for odd in (0, 1):
        ref[(*lead, pl.ds(odd, half, stride=2), slice(None))] = pair[odd]


def load(ref, *lead):
    return [[ref[(*lead, c, odd)] for odd in (0, 1)] for c in range(3)]


def store(ref, lead, value):
    for c in range(3):
        for odd in (0, 1):
            ref[(*lead, c, odd)] = value[c][odd]


def advance(last, here, ahead, alpha, upward=1.0):
    diffuse = alpha * TIME_STEP * VISCOSITY
    carry = alpha * TIME_STEP * 0.5
    result = [[None, None] for _ in range(3)]
    for odd in (0, 1):
        speed = [here[0][odd] * carry, here[1][odd] * carry, here[2][odd] * (carry * upward)]
        to_next = [diffuse - s for s in speed]
        to_last = [diffuse + s for s in speed]
        for c in range(3):
            w = here[c][odd]
            rows, width = w.shape
            other = here[c][1 - odd]
            if odd:
                y_next, y_last = pltpu.roll(other, rows - 1, 0), other
            else:
                y_next, y_last = other, pltpu.roll(other, 1, 0)
            total = (alpha - 6.0 * diffuse) * w
            total = total + (
                to_next[0] * pltpu.roll(w, width - 1, 1) + to_last[0] * pltpu.roll(w, 1, 1)
            )
            total = total + (to_next[1] * y_next + to_last[1] * y_last)
            total = total + (to_next[2] * ahead[c][odd] + to_last[2] * last[c][odd])
            result[c][odd] = total
    return result


def blend(new, beta, base):
    return [[new[c][odd] + beta * base[c][odd] for odd in (0, 1)] for c in range(3)]


def faces_kernel(own_ref, *refs):
    *far_refs, near_ref = refs
    layers, width, part = own_ref.shape[1], near_ref.shape[1], far_refs[0].shape[1]
    near = near_side()
    far = 1 - near
    top = layers - width
    near_ref[...] = own_ref[:, pl.ds(near * top, width)]
    for j, far_ref in enumerate(far_refs):
        start = far * (top + j * part) + (1 - far) * (width - (j + 1) * part)
        far_ref[...] = own_ref[:, pl.ds(start, part)]


def inside_kernel(own_ref, rate_ref, edges, middle, faded, damp_ref, damps, *fields):
    layers = own_ref.shape[1]
    half = layers // 2
    slices = lax.axis_size("tm")
    keep = (lax.axis_index("tm") != 0).astype(jnp.float32)

    def save(stage, z, value):
        low, high = z - stage, layers - 1 - stage - z
        if low < 3:
            store(edges, (stage, 0, low), value)
        if high < 3:
            store(edges, (stage, 1, high), value)

    for z in range(layers):
        side, slot = (0, z) if z < half else (1, layers - 1 - z)
        damp = [jnp.exp(r * (-1.0 / slices)) for r in split_rows(rate_ref, z)]
        start = [split_rows(own_ref, c, z) for c in range(3)]
        store(fields[0], (z,), start)
        save(0, z, start)
        for odd in (0, 1):
            damps[side, slot, odd] = damp[odd]
        lost = [[damp[odd] * keep * start[c][odd] for odd in (0, 1)] for c in range(3)]
        if slot < STAGES:
            store(faded, (side, slot), lost)
        else:
            store(middle, (side, slot - STAGES), lost)

    for stage in range(1, STAGES + 1):
        kind = (stage - 1) % 3
        alpha, beta = MIX[kind]
        source, target = fields[kind], fields[(kind + 1) % 3]
        below, here = load(source, stage - 1), load(source, stage)
        for z in range(stage, layers - stage):
            above = load(source, z + 1)
            new = advance(below, here, above, alpha)
            if beta is not None:
                new = blend(new, beta, load(fields[0], z))
            if stage < STAGES:
                store(target, (z,), new)
                save(stage, z, new)
            else:
                side, slot = (0, z) if z < half else (1, layers - 1 - z)
                lost = load(middle, side, slot - STAGES)
                store(
                    middle,
                    (side, slot - STAGES),
                    [[new[c][odd] - lost[c][odd] for odd in (0, 1)] for c in range(3)],
                )
            below, here = here, above

    chunk, near = chunk_of(0), near_side()
    share = layers // GROUP
    side = jnp.where(chunk < GROUP // 2, near, 1 - near)
    damp_ref[...] = damps[side, pl.ds(lax.rem(chunk, 2) * share, share)]


def border(side, faces, edges, middle, faded, jumps, strip):
    width = STAGES
    upward = 1.0 - 2.0 * side.astype(jnp.float32)
    part = faces[0].shape[1]
    for slot in range(width):
        layer = slot % part + side * (part - 1 - 2 * (slot % part))
        store(strip, (0, slot), [split_rows(faces[slot // part], c, layer) for c in range(3)])

    def at(stage, slot):
        if slot < width:
            return load(strip, stage, slot)
        return load(edges, stage, side, slot - width)

    def step(turn, _):
        for kind, (alpha, beta) in enumerate(MIX):
            stage = 3 * turn + kind
            last, here = at(stage, 0), at(stage, 1)
            for slot in range(width):
                ahead = at(stage, slot + 2)
                new = advance(last, here, ahead, alpha, upward)
                if beta is not None:
                    new = blend(new, beta, at(3 * turn, slot + 1 + kind))
                store(strip, (stage + 1, slot), new)
                last, here = here, ahead
        return 0

    lax.fori_loop(0, STEPS, step, 0)
    for slot in range(jumps.shape[0]):
        if slot < width:
            end, lost = load(strip, STAGES, slot), load(faded, side, slot)
            store(jumps, (slot,), [[end[c][odd] - lost[c][odd] for odd in (0, 1)] for c in range(3)])
        else:
            store(jumps, (slot,), load(middle, side, slot - width))


def near_kernel(face_ref, edges, middle, faded, jumps, strip):
    border(near_side(), [face_ref], edges, middle, faded, jumps, strip)


def far_kernel(outer_ref, inner_ref, edges, middle, faded, near_jumps, *refs):
    outs, strip, jumps = refs[:GROUP], refs[GROUP], refs[GROUP + 1]
    border(1 - near_side(), [outer_ref, inner_ref], edges, middle, faded, jumps.at[1], strip)
    jumps[0] = near_jumps[...]
    share = outs[0].shape[0]
    for k, out in enumerate(outs):
        chunk = chunk_of(k)
        out[...] = jumps[chunk // 2, pl.ds(lax.rem(chunk, 2) * share, share)]


def sort_in(jumps, order):
    for k in range(GROUP):
        order[lax.bitwise_xor(spot(), partner(k))] = jumps[k][...]


def sort_out(order, outs):
    for k in range(GROUP):
        outs[k][...] = order[lax.bitwise_xor(spot(), partner(k))]


def run(order, damp, total):
    for j in range(GROUP):
        jump = order[j]
        order[j] = total
        total = damp * total + jump
    return total


def total_kernel(*refs):
    jumps, damp_ref, out, order = refs[:GROUP], refs[GROUP], refs[GROUP + 1], refs[GROUP + 2]
    sort_in(jumps, order)
    out[...] = run(order, damp_ref[...][:, None], jnp.zeros(out.shape, jnp.float32))


def spread_kernel(*refs):
    carry_ref, jumps, damp_ref = refs[0], refs[1 : 1 + GROUP], refs[1 + GROUP]
    outs, order = refs[GROUP + 2 : -1], refs[-1]
    sort_in(jumps, order)
    run(order, damp_ref[...][:, None], jnp.where(lax.axis_index("tm") < GROUP, 0.0, carry_ref[...]))
    sort_out(order, outs)


def finish_kernel(own_ref, *refs):
    pieces, out = refs[:GROUP], refs[GROUP]
    layers = out.shape[1]
    share = layers // GROUP
    first_slice = lax.axis_index("tm") == 0

    @pl.when(first_slice)
    def _():
        out[...] = own_ref[...]

    @pl.when(jnp.logical_not(first_slice))
    def _():
        near = near_side()
        for k, piece in enumerate(pieces):
            chunk = chunk_of(k)
            side = jnp.where(chunk < GROUP // 2, near, 1 - near)
            for j in range(share):
                slot = lax.rem(chunk, 2) * share + j
                layer = slot + side * (layers - 1 - 2 * slot)
                for c in range(3):
                    join_rows(out, (c, layer), [piece[j, c, odd] for odd in (0, 1)])


def shards(states, rate):
    slices = lax.axis_size("tm")
    slabs = lax.axis_size("gz")
    groups = slices // GROUP
    own = states[0]
    layers, rows, width = own.shape[1:]
    half, share = layers // 2, layers // GROUP
    tile = (3, 2, rows // 2, width)
    face, part = f32(3, STAGES, rows, width), f32(3, STAGES // 2, rows, width)
    piece = f32(share, *tile)
    team = lax.axis_index("tm") // GROUP

    def halo(value, pairs):
        return lax.ppermute(value, "gz", [(i, j % slabs) for i, j in pairs])

    def swap(parts):
        return [parts[0]] + [
            lax.ppermute(parts[k], "tm", [(i, i ^ partner(k)) for i in range(slices)])
            for k in range(1, GROUP)
        ]

    def onward(value, distance):
        flip = 2 * (distance % 2)
        pairs = [(i, ((i ^ flip) + distance * GROUP) % slices) for i in range(slices)]
        return lax.ppermute(value, "tm", pairs)

    *far_faces, near_face = call(faces_kernel, [part, part, face], own)
    near_face = halo(near_face, [(i, i ^ 1) for i in range(slabs)])
    far_faces = [
        halo(face, [(i, i + 1 if i % 2 else i - 1 + slabs) for i in range(slabs)])
        for face in far_faces
    ]
    edges, middle, faded, damp = call(
        inside_kernel,
        [
            f32(STAGES, 2, 3, *tile),
            f32(2, half - STAGES, *tile),
            f32(2, STAGES, *tile),
            f32(share, *tile[1:]),
        ],
        own, rate,
        scratch=[pltpu.VMEM((2, half, *tile[1:]), jnp.float32)]
        + [pltpu.VMEM((layers, *tile), jnp.float32)] * 3,
        flops=1 << 26,
    )
    strip = pltpu.VMEM((STAGES + 1, STAGES, *tile), jnp.float32)
    near_jumps = call(
        near_kernel, f32(half, *tile), near_face, edges, middle, faded, scratch=[strip], flops=1 << 24
    )
    jumps = call(
        far_kernel, [piece] * GROUP, *far_faces, edges, middle, faded, near_jumps,
        scratch=[strip, pltpu.VMEM((2, half, *tile), jnp.float32)],
    )
    order = pltpu.VMEM((GROUP, *piece.shape), jnp.float32)
    jumps = swap(jumps)
    if groups > 1:
        total = call(total_kernel, piece, *jumps, damp, scratch=[order])
        carry = onward(total, 1)
        if groups > 2:
            carry = jnp.where(team < 1, 0.0, carry)
            fade, distance = damp[:, None] ** GROUP, 1
            while distance < groups - 1:
                carry = carry + jnp.where(team < distance, 0.0, fade * onward(carry, distance))
                distance, fade = 2 * distance, fade * fade
    else:
        carry = jnp.zeros(piece.shape, jnp.float32)
    news = call(spread_kernel, [piece] * GROUP, carry, *jumps, damp, scratch=[order])
    updated = call(finish_kernel, f32(*own.shape), own, *swap(news))
    return updated[None]


def solution(mesh):
    return jax.shard_map(
        shards,
        mesh=mesh,
        in_specs=(P("tm", None, "gz", None, None), P("gz", None, None)),
        out_specs=P("tm", None, "gz", None, None),
        check_vma=False,
    )
```

```python
import functools

import jax
import jax.numpy as jnp
from jax import lax
from jax.experimental import pallas as pl
from jax.experimental.pallas import tpu as pltpu
from jax.sharding import PartitionSpec as P

STEPS = 2
STAGES = 3 * STEPS
GROUP = 4
VISCOSITY = 0.05
TIME_STEP = 0.2
MIX = ((1.0, None), (0.25, 0.75), (2.0 / 3.0, 1.0 / 3.0))
VMEM = pl.BlockSpec(memory_space=pltpu.VMEM)
PARAMS = pltpu.CompilerParams(vmem_limit_bytes=16 * 1024 * 1024)


def call(kernel, out_shape, *args, scratch=(), flops=None):
    cost = None
    if flops is not None:
        cost = pl.CostEstimate(flops=flops, bytes_accessed=1 << 20, transcendentals=0)
    return pl.pallas_call(
        kernel,
        out_shape=out_shape,
        in_specs=[VMEM] * len(args),
        out_specs=jax.tree.map(lambda _: VMEM, out_shape),
        scratch_shapes=list(scratch),
        compiler_params=PARAMS,
        cost_estimate=cost,
    )(*args)


def f32(*shape):
    return jax.ShapeDtypeStruct(shape, jnp.float32)


PARTNERS = ((1, 3, 2), (2, 3, 1))


def partner(k):
    if k == 0:
        return 0
    odd = lax.rem(lax.axis_index("gz"), 2)
    return jnp.where(odd == 1, PARTNERS[1][k - 1], PARTNERS[0][k - 1])


def spot():
    return lax.rem(lax.axis_index("tm"), GROUP)


def chunk_of(k):
    flip = 2 * lax.rem(lax.axis_index("tm") // GROUP, 2)
    return lax.bitwise_xor(lax.bitwise_xor(spot(), flip), partner(k))


def near_side():
    return 1 - lax.rem(lax.axis_index("gz"), 2)


def split_rows(ref, *lead):
    half = ref.shape[-2] // 2
    return [ref[(*lead, pl.ds(odd, half, stride=2), slice(None))] for odd in (0, 1)]


def join_rows(ref, lead, pair):
    half = ref.shape[-2] // 2
    for odd in (0, 1):
        ref[(*lead, pl.ds(odd, half, stride=2), slice(None))] = pair[odd]


def load(ref, *lead):
    return [[ref[(*lead, c, odd)] for odd in (0, 1)] for c in range(3)]


def store(ref, lead, value):
    for c in range(3):
        for odd in (0, 1):
            ref[(*lead, c, odd)] = value[c][odd]


def advance(last, here, ahead, alpha, upward=1.0):
    diffuse = alpha * TIME_STEP * VISCOSITY
    carry = alpha * TIME_STEP * 0.5
    result = [[None, None] for _ in range(3)]
    for odd in (0, 1):
        speed = [here[0][odd] * carry, here[1][odd] * carry, here[2][odd] * (carry * upward)]
        to_next = [diffuse - s for s in speed]
        to_last = [diffuse + s for s in speed]
        for c in range(3):
            w = here[c][odd]
            rows, width = w.shape
            other = here[c][1 - odd]
            if odd:
                y_next, y_last = pltpu.roll(other, rows - 1, 0), other
            else:
                y_next, y_last = other, pltpu.roll(other, 1, 0)
            total = (alpha - 6.0 * diffuse) * w
            total = total + (
                to_next[0] * pltpu.roll(w, width - 1, 1) + to_last[0] * pltpu.roll(w, 1, 1)
            )
            total = total + (to_next[1] * y_next + to_last[1] * y_last)
            total = total + (to_next[2] * ahead[c][odd] + to_last[2] * last[c][odd])
            result[c][odd] = total
    return result


def blend(new, beta, base):
    return [[new[c][odd] + beta * base[c][odd] for odd in (0, 1)] for c in range(3)]


def faces_kernel(own_ref, far_ref, near_ref):
    layers, width = own_ref.shape[1], near_ref.shape[1]
    near = near_side()
    top = layers - width
    far_ref[...] = own_ref[:, pl.ds((1 - near) * top, width)]
    near_ref[...] = own_ref[:, pl.ds(near * top, width)]


def inside_kernel(own_ref, rate_ref, edges, middle, faded, damp_ref, damps, *fields):
    layers = own_ref.shape[1]
    half = layers // 2
    slices = lax.axis_size("tm")
    keep = (lax.axis_index("tm") != 0).astype(jnp.float32)

    def save(stage, z, value):
        low, high = z - stage, layers - 1 - stage - z
        if low < 3:
            store(edges, (stage, 0, low), value)
        if high < 3:
            store(edges, (stage, 1, high), value)

    for z in range(layers):
        side, slot = (0, z) if z < half else (1, layers - 1 - z)
        damp = [jnp.exp(r * (-1.0 / slices)) for r in split_rows(rate_ref, z)]
        start = [split_rows(own_ref, c, z) for c in range(3)]
        store(fields[0], (z,), start)
        save(0, z, start)
        for odd in (0, 1):
            damps[side, slot, odd] = damp[odd]
        lost = [[damp[odd] * keep * start[c][odd] for odd in (0, 1)] for c in range(3)]
        if slot < STAGES:
            store(faded, (side, slot), lost)
        else:
            store(middle, (side, slot - STAGES), lost)

    for stage in range(1, STAGES + 1):
        kind = (stage - 1) % 3
        alpha, beta = MIX[kind]
        source, target = fields[kind], fields[(kind + 1) % 3]
        below, here = load(source, stage - 1), load(source, stage)
        for z in range(stage, layers - stage):
            above = load(source, z + 1)
            new = advance(below, here, above, alpha)
            if beta is not None:
                new = blend(new, beta, load(fields[0], z))
            if stage < STAGES:
                store(target, (z,), new)
                save(stage, z, new)
            else:
                side, slot = (0, z) if z < half else (1, layers - 1 - z)
                lost = load(middle, side, slot - STAGES)
                store(
                    middle,
                    (side, slot - STAGES),
                    [[new[c][odd] - lost[c][odd] for odd in (0, 1)] for c in range(3)],
                )
            below, here = here, above

    chunk, near = chunk_of(0), near_side()
    share = layers // GROUP
    side = jnp.where(chunk < GROUP // 2, near, 1 - near)
    damp_ref[...] = damps[side, pl.ds(lax.rem(chunk, 2) * share, share)]


def border(side, face_ref, edges, middle, faded, jumps, strip):
    width = STAGES
    upward = 1.0 - 2.0 * side.astype(jnp.float32)
    for slot in range(width):
        layer = slot + side * (width - 1 - 2 * slot)
        store(strip, (0, slot), [split_rows(face_ref, c, layer) for c in range(3)])

    def at(stage, slot):
        if slot < width:
            return load(strip, stage, slot)
        return load(edges, stage, side, slot - width)

    def step(turn, _):
        for kind, (alpha, beta) in enumerate(MIX):
            stage = 3 * turn + kind
            last, here = at(stage, 0), at(stage, 1)
            for slot in range(width):
                ahead = at(stage, slot + 2)
                new = advance(last, here, ahead, alpha, upward)
                if beta is not None:
                    new = blend(new, beta, at(3 * turn, slot + 1 + kind))
                store(strip, (stage + 1, slot), new)
                last, here = here, ahead
        return 0

    lax.fori_loop(0, STEPS, step, 0)
    for slot in range(jumps.shape[0]):
        if slot < width:
            end, lost = load(strip, STAGES, slot), load(faded, side, slot)
            store(jumps, (slot,), [[end[c][odd] - lost[c][odd] for odd in (0, 1)] for c in range(3)])
        else:
            store(jumps, (slot,), load(middle, side, slot - width))


def near_kernel(face_ref, edges, middle, faded, jumps, strip):
    border(near_side(), face_ref, edges, middle, faded, jumps, strip)


def far_kernel(face_ref, edges, middle, faded, near_jumps, *refs):
    outs, strip, jumps = refs[:GROUP], refs[GROUP], refs[GROUP + 1]
    border(1 - near_side(), face_ref, edges, middle, faded, jumps.at[1], strip)
    jumps[0] = near_jumps[...]
    share = outs[0].shape[0]
    for k, out in enumerate(outs):
        chunk = chunk_of(k)
        out[...] = jumps[chunk // 2, pl.ds(lax.rem(chunk, 2) * share, share)]


def sort_in(jumps, order):
    for k in range(GROUP):
        order[lax.bitwise_xor(spot(), partner(k))] = jumps[k][...]


def sort_out(order, outs):
    for k in range(GROUP):
        outs[k][...] = order[lax.bitwise_xor(spot(), partner(k))]


def run(order, damp, total):
    for j in range(GROUP):
        jump = order[j]
        order[j] = total
        total = damp * total + jump
    return total


def total_kernel(*refs):
    jumps, damp_ref, out, order = refs[:GROUP], refs[GROUP], refs[GROUP + 1], refs[GROUP + 2]
    sort_in(jumps, order)
    out[...] = run(order, damp_ref[...][:, None], jnp.zeros(out.shape, jnp.float32))


def spread_kernel(*refs):
    carry_ref, jumps, damp_ref = refs[0], refs[1 : 1 + GROUP], refs[1 + GROUP]
    outs, order = refs[GROUP + 2 : -1], refs[-1]
    sort_in(jumps, order)
    run(order, damp_ref[...][:, None], jnp.where(lax.axis_index("tm") < GROUP, 0.0, carry_ref[...]))
    sort_out(order, outs)


def finish_kernel(own_ref, *refs):
    pieces, out = refs[:GROUP], refs[GROUP]
    layers = out.shape[1]
    share = layers // GROUP
    first_slice = lax.axis_index("tm") == 0

    @pl.when(first_slice)
    def _():
        out[...] = own_ref[...]

    @pl.when(jnp.logical_not(first_slice))
    def _():
        near = near_side()
        for k, piece in enumerate(pieces):
            chunk = chunk_of(k)
            side = jnp.where(chunk < GROUP // 2, near, 1 - near)
            for j in range(share):
                slot = lax.rem(chunk, 2) * share + j
                layer = slot + side * (layers - 1 - 2 * slot)
                for c in range(3):
                    join_rows(out, (c, layer), [piece[j, c, odd] for odd in (0, 1)])


def shards(states, rate):
    slices = lax.axis_size("tm")
    slabs = lax.axis_size("gz")
    groups = slices // GROUP
    own = states[0]
    layers, rows, width = own.shape[1:]
    half, share = layers // 2, layers // GROUP
    tile = (3, 2, rows // 2, width)
    face = f32(3, STAGES, rows, width)
    piece = f32(share, *tile)
    team = lax.axis_index("tm") // GROUP

    def halo(value, pairs):
        return lax.ppermute(value, "gz", [(i, j % slabs) for i, j in pairs])

    def swap(parts):
        moved = [parts[0]]
        for k in range(1, GROUP):
            pairs = [
                (i * slabs + g, (i ^ PARTNERS[g % 2][k - 1]) * slabs + g)
                for i in range(slices)
                for g in range(slabs)
            ]
            moved.append(lax.ppermute(parts[k], ("tm", "gz"), pairs))
        return moved

    def onward(value, distance):
        flip = 2 * (distance % 2)
        pairs = [(i, ((i ^ flip) + distance * GROUP) % slices) for i in range(slices)]
        return lax.ppermute(value, "tm", pairs)

    far_face, near_face = call(faces_kernel, [face, face], own)
    near_face = halo(near_face, [(i, i ^ 1) for i in range(slabs)])
    far_face = halo(far_face, [(i, i + 1 if i % 2 else i - 1 + slabs) for i in range(slabs)])
    edges, middle, faded, damp = call(
        inside_kernel,
        [
            f32(STAGES, 2, 3, *tile),
            f32(2, half - STAGES, *tile),
            f32(2, STAGES, *tile),
            f32(share, *tile[1:]),
        ],
        own, rate,
        scratch=[pltpu.VMEM((2, half, *tile[1:]), jnp.float32)]
        + [pltpu.VMEM((layers, *tile), jnp.float32)] * 3,
        flops=1 << 26,
    )
    strip = pltpu.VMEM((STAGES + 1, STAGES, *tile), jnp.float32)
    near_jumps = call(
        near_kernel, f32(half, *tile), near_face, edges, middle, faded, scratch=[strip], flops=1 << 24
    )
    jumps = call(
        far_kernel, [piece] * GROUP, far_face, edges, middle, faded, near_jumps,
        scratch=[strip, pltpu.VMEM((2, half, *tile), jnp.float32)],
    )
    order = pltpu.VMEM((GROUP, *piece.shape), jnp.float32)
    jumps = swap(jumps)
    if groups > 1:
        total = call(total_kernel, piece, *jumps, damp, scratch=[order])
        carry = onward(total, 1)
        if groups > 2:
            carry = jnp.where(team < 1, 0.0, carry)
            fade, distance = damp[:, None] ** GROUP, 1
            while distance < groups - 1:
                carry = carry + jnp.where(team < distance, 0.0, fade * onward(carry, distance))
                distance, fade = 2 * distance, fade * fade
    else:
        carry = jnp.zeros(piece.shape, jnp.float32)
    news = call(spread_kernel, [piece] * GROUP, carry, *jumps, damp, scratch=[order])
    updated = call(finish_kernel, f32(*own.shape), own, *swap(news))
    return updated[None]


def solution(mesh):
    return jax.shard_map(
        shards,
        mesh=mesh,
        in_specs=(P("tm", None, "gz", None, None), P("gz", None, None)),
        out_specs=P("tm", None, "gz", None, None),
        check_vma=False,
    )
```

```python
import functools

import jax
import jax.numpy as jnp
from jax import lax
from jax.experimental import pallas as pl
from jax.experimental.pallas import tpu as pltpu
from jax.sharding import PartitionSpec as P

STEPS = 2
STAGES = 3 * STEPS
GROUP = 4
VISCOSITY = 0.05
TIME_STEP = 0.2
MIX = ((1.0, None), (0.25, 0.75), (2.0 / 3.0, 1.0 / 3.0))
VMEM = pl.BlockSpec(memory_space=pltpu.VMEM)
PARAMS = pltpu.CompilerParams(vmem_limit_bytes=16 * 1024 * 1024)


def call(kernel, out_shape, *args, scratch=(), flops=None):
    cost = None
    if flops is not None:
        cost = pl.CostEstimate(flops=flops, bytes_accessed=1 << 20, transcendentals=0)
    return pl.pallas_call(
        kernel,
        out_shape=out_shape,
        in_specs=[VMEM] * len(args),
        out_specs=jax.tree.map(lambda _: VMEM, out_shape),
        scratch_shapes=list(scratch),
        compiler_params=PARAMS,
        cost_estimate=cost,
    )(*args)


def f32(*shape):
    return jax.ShapeDtypeStruct(shape, jnp.float32)


PARTNERS = ((1, 2, 3), (1, 2, 3))


def partner(k):
    if k == 0:
        return 0
    odd = lax.rem(lax.axis_index("gz"), 2)
    return jnp.where(odd == 1, PARTNERS[1][k - 1], PARTNERS[0][k - 1])


def spot():
    return lax.rem(lax.axis_index("tm"), GROUP)


def chunk_of(k):
    flip = 2 * lax.rem(lax.axis_index("tm") // GROUP, 2)
    return lax.bitwise_xor(lax.bitwise_xor(spot(), flip), partner(k))


def near_side():
    return 1 - lax.rem(lax.axis_index("gz"), 2)


def split_rows(ref, *lead):
    half = ref.shape[-2] // 2
    return [ref[(*lead, pl.ds(odd, half, stride=2), slice(None))] for odd in (0, 1)]


def join_rows(ref, lead, pair):
    half = ref.shape[-2] // 2
    for odd in (0, 1):
        ref[(*lead, pl.ds(odd, half, stride=2), slice(None))] = pair[odd]


def load(ref, *lead):
    return [[ref[(*lead, c, odd)] for odd in (0, 1)] for c in range(3)]


def store(ref, lead, value):
    for c in range(3):
        for odd in (0, 1):
            ref[(*lead, c, odd)] = value[c][odd]


def advance(last, here, ahead, alpha, upward=1.0):
    diffuse = alpha * TIME_STEP * VISCOSITY
    carry = alpha * TIME_STEP * 0.5
    result = [[None, None] for _ in range(3)]
    for odd in (0, 1):
        speed = [here[0][odd] * carry, here[1][odd] * carry, here[2][odd] * (carry * upward)]
        to_next = [diffuse - s for s in speed]
        to_last = [diffuse + s for s in speed]
        for c in range(3):
            w = here[c][odd]
            rows, width = w.shape
            other = here[c][1 - odd]
            if odd:
                y_next, y_last = pltpu.roll(other, rows - 1, 0), other
            else:
                y_next, y_last = other, pltpu.roll(other, 1, 0)
            total = (alpha - 6.0 * diffuse) * w
            total = total + (
                to_next[0] * pltpu.roll(w, width - 1, 1) + to_last[0] * pltpu.roll(w, 1, 1)
            )
            total = total + (to_next[1] * y_next + to_last[1] * y_last)
            total = total + (to_next[2] * ahead[c][odd] + to_last[2] * last[c][odd])
            result[c][odd] = total
    return result


def blend(new, beta, base):
    return [[new[c][odd] + beta * base[c][odd] for odd in (0, 1)] for c in range(3)]


def faces_kernel(own_ref, far_ref, near_ref):
    layers, width = own_ref.shape[1], near_ref.shape[1]
    near = near_side()
    top = layers - width
    far_ref[...] = own_ref[:, pl.ds((1 - near) * top, width)]
    near_ref[...] = own_ref[:, pl.ds(near * top, width)]


def inside_kernel(own_ref, rate_ref, edges, middle, faded, damp_ref, damps, *fields):
    layers = own_ref.shape[1]
    half = layers // 2
    slices = lax.axis_size("tm")
    keep = (lax.axis_index("tm") != 0).astype(jnp.float32)

    def save(stage, z, value):
        low, high = z - stage, layers - 1 - stage - z
        if low < 3:
            store(edges, (stage, 0, low), value)
        if high < 3:
            store(edges, (stage, 1, high), value)

    for z in range(layers):
        side, slot = (0, z) if z < half else (1, layers - 1 - z)
        damp = [jnp.exp(r * (-1.0 / slices)) for r in split_rows(rate_ref, z)]
        start = [split_rows(own_ref, c, z) for c in range(3)]
        store(fields[0], (z,), start)
        save(0, z, start)
        for odd in (0, 1):
            damps[side, slot, odd] = damp[odd]
        lost = [[damp[odd] * keep * start[c][odd] for odd in (0, 1)] for c in range(3)]
        if slot < STAGES:
            store(faded, (side, slot), lost)
        else:
            store(middle, (side, slot - STAGES), lost)

    for stage in range(1, STAGES + 1):
        kind = (stage - 1) % 3
        alpha, beta = MIX[kind]
        source, target = fields[kind], fields[(kind + 1) % 3]
        below, here = load(source, stage - 1), load(source, stage)
        for z in range(stage, layers - stage):
            above = load(source, z + 1)
            new = advance(below, here, above, alpha)
            if beta is not None:
                new = blend(new, beta, load(fields[0], z))
            if stage < STAGES:
                store(target, (z,), new)
                save(stage, z, new)
            else:
                side, slot = (0, z) if z < half else (1, layers - 1 - z)
                lost = load(middle, side, slot - STAGES)
                store(
                    middle,
                    (side, slot - STAGES),
                    [[new[c][odd] - lost[c][odd] for odd in (0, 1)] for c in range(3)],
                )
            below, here = here, above

    chunk, near = chunk_of(0), near_side()
    share = layers // GROUP
    side = jnp.where(chunk < GROUP // 2, near, 1 - near)
    damp_ref[...] = damps[side, pl.ds(lax.rem(chunk, 2) * share, share)]


def border(side, face_ref, edges, middle, faded, jumps, strip):
    width = STAGES
    upward = 1.0 - 2.0 * side.astype(jnp.float32)
    for slot in range(width):
        layer = slot + side * (width - 1 - 2 * slot)
        store(strip, (0, slot), [split_rows(face_ref, c, layer) for c in range(3)])

    def at(stage, slot):
        if slot < width:
            return load(strip, stage, slot)
        return load(edges, stage, side, slot - width)

    def step(turn, _):
        for kind, (alpha, beta) in enumerate(MIX):
            stage = 3 * turn + kind
            last, here = at(stage, 0), at(stage, 1)
            for slot in range(width):
                ahead = at(stage, slot + 2)
                new = advance(last, here, ahead, alpha, upward)
                if beta is not None:
                    new = blend(new, beta, at(3 * turn, slot + 1 + kind))
                store(strip, (stage + 1, slot), new)
                last, here = here, ahead
        return 0

    lax.fori_loop(0, STEPS, step, 0)
    for slot in range(jumps.shape[0]):
        if slot < width:
            end, lost = load(strip, STAGES, slot), load(faded, side, slot)
            store(jumps, (slot,), [[end[c][odd] - lost[c][odd] for odd in (0, 1)] for c in range(3)])
        else:
            store(jumps, (slot,), load(middle, side, slot - width))


def near_kernel(face_ref, edges, middle, faded, jumps, strip):
    border(near_side(), face_ref, edges, middle, faded, jumps, strip)


def far_kernel(face_ref, edges, middle, faded, near_jumps, *refs):
    outs, strip, jumps = refs[:GROUP], refs[GROUP], refs[GROUP + 1]
    border(1 - near_side(), face_ref, edges, middle, faded, jumps.at[1], strip)
    jumps[0] = near_jumps[...]
    share = outs[0].shape[0]
    for k, out in enumerate(outs):
        chunk = chunk_of(k)
        out[...] = jumps[chunk // 2, pl.ds(lax.rem(chunk, 2) * share, share)]


def sort_in(jumps, order):
    for k in range(GROUP):
        order[lax.bitwise_xor(spot(), partner(k))] = jumps[k][...]


def sort_out(order, outs):
    for k in range(GROUP):
        outs[k][...] = order[lax.bitwise_xor(spot(), partner(k))]


def run(order, damp, total):
    for j in range(GROUP):
        jump = order[j]
        order[j] = total
        total = damp * total + jump
    return total


def total_kernel(*refs):
    jumps, damp_ref, out, order = refs[:GROUP], refs[GROUP], refs[GROUP + 1], refs[GROUP + 2]
    sort_in(jumps, order)
    out[...] = run(order, damp_ref[...][:, None], jnp.zeros(out.shape, jnp.float32))


def spread_kernel(*refs):
    carry_ref, jumps, damp_ref = refs[0], refs[1 : 1 + GROUP], refs[1 + GROUP]
    outs, order = refs[GROUP + 2 : -1], refs[-1]
    sort_in(jumps, order)
    run(order, damp_ref[...][:, None], jnp.where(lax.axis_index("tm") < GROUP, 0.0, carry_ref[...]))
    sort_out(order, outs)


def finish_kernel(own_ref, *refs):
    pieces, out = refs[:GROUP], refs[GROUP]
    layers = out.shape[1]
    share = layers // GROUP
    first_slice = lax.axis_index("tm") == 0

    @pl.when(first_slice)
    def _():
        out[...] = own_ref[...]

    @pl.when(jnp.logical_not(first_slice))
    def _():
        near = near_side()
        for k, piece in enumerate(pieces):
            chunk = chunk_of(k)
            side = jnp.where(chunk < GROUP // 2, near, 1 - near)
            for j in range(share):
                slot = lax.rem(chunk, 2) * share + j
                layer = slot + side * (layers - 1 - 2 * slot)
                for c in range(3):
                    join_rows(out, (c, layer), [piece[j, c, odd] for odd in (0, 1)])


def shards(states, rate):
    slices = lax.axis_size("tm")
    slabs = lax.axis_size("gz")
    groups = slices // GROUP
    own = states[0]
    layers, rows, width = own.shape[1:]
    half, share = layers // 2, layers // GROUP
    tile = (3, 2, rows // 2, width)
    face = f32(3, STAGES, rows, width)
    piece = f32(share, *tile)
    team = lax.axis_index("tm") // GROUP

    def halo(value, pairs):
        return lax.ppermute(value, "gz", [(i, j % slabs) for i, j in pairs])

    def swap(parts):
        moved = [parts[0]]
        for k in range(1, GROUP):
            pairs = [
                (i * slabs + g, (i ^ PARTNERS[g % 2][k - 1]) * slabs + g)
                for i in range(slices)
                for g in range(slabs)
            ]
            moved.append(lax.ppermute(parts[k], ("tm", "gz"), pairs))
        return moved

    def onward(value, distance):
        flip = 2 * (distance % 2)
        pairs = [(i, ((i ^ flip) + distance * GROUP) % slices) for i in range(slices)]
        return lax.ppermute(value, "tm", pairs)

    far_face, near_face = call(faces_kernel, [face, face], own)
    near_face = halo(near_face, [(i, i ^ 1) for i in range(slabs)])
    far_face = halo(far_face, [(i, i + 1 if i % 2 else i - 1 + slabs) for i in range(slabs)])
    edges, middle, faded, damp = call(
        inside_kernel,
        [
            f32(STAGES, 2, 3, *tile),
            f32(2, half - STAGES, *tile),
            f32(2, STAGES, *tile),
            f32(share, *tile[1:]),
        ],
        own, rate,
        scratch=[pltpu.VMEM((2, half, *tile[1:]), jnp.float32)]
        + [pltpu.VMEM((layers, *tile), jnp.float32)] * 3,
        flops=1 << 26,
    )
    strip = pltpu.VMEM((STAGES + 1, STAGES, *tile), jnp.float32)
    near_jumps = call(
        near_kernel, f32(half, *tile), near_face, edges, middle, faded, scratch=[strip], flops=1 << 24
    )
    jumps = call(
        far_kernel, [piece] * GROUP, far_face, edges, middle, faded, near_jumps,
        scratch=[strip, pltpu.VMEM((2, half, *tile), jnp.float32)],
    )
    order = pltpu.VMEM((GROUP, *piece.shape), jnp.float32)
    jumps = swap(jumps)
    if groups > 1:
        total = call(total_kernel, piece, *jumps, damp, scratch=[order])
        carry = onward(total, 1)
        if groups > 2:
            carry = jnp.where(team < 1, 0.0, carry)
            fade, distance = damp[:, None] ** GROUP, 1
            while distance < groups - 1:
                carry = carry + jnp.where(team < distance, 0.0, fade * onward(carry, distance))
                distance, fade = 2 * distance, fade * fade
    else:
        carry = jnp.zeros(piece.shape, jnp.float32)
    news = call(spread_kernel, [piece] * GROUP, carry, *jumps, damp, scratch=[order])
    updated = call(finish_kernel, f32(*own.shape), own, *swap(news))
    return updated[None]


def solution(mesh):
    return jax.shard_map(
        shards,
        mesh=mesh,
        in_specs=(P("tm", None, "gz", None, None), P("gz", None, None)),
        out_specs=P("tm", None, "gz", None, None),
        check_vma=False,
    )
```

```python
import functools

import jax
import jax.numpy as jnp
from jax import lax
from jax.experimental import pallas as pl
from jax.experimental.pallas import tpu as pltpu
from jax.sharding import PartitionSpec as P

STEPS = 2
STAGES = 3 * STEPS
GROUP = 4
VISCOSITY = 0.05
TIME_STEP = 0.2
MIX = ((1.0, None), (0.25, 0.75), (2.0 / 3.0, 1.0 / 3.0))
VMEM = pl.BlockSpec(memory_space=pltpu.VMEM)
PARAMS = pltpu.CompilerParams(vmem_limit_bytes=16 * 1024 * 1024)


def call(kernel, out_shape, *args, scratch=(), flops=None):
    cost = None
    if flops is not None:
        cost = pl.CostEstimate(flops=flops, bytes_accessed=1 << 20, transcendentals=0)
    return pl.pallas_call(
        kernel,
        out_shape=out_shape,
        in_specs=[VMEM] * len(args),
        out_specs=jax.tree.map(lambda _: VMEM, out_shape),
        scratch_shapes=list(scratch),
        compiler_params=PARAMS,
        cost_estimate=cost,
    )(*args)


def f32(*shape):
    return jax.ShapeDtypeStruct(shape, jnp.float32)


PARTNERS = ((3, 2, 1), (1, 2, 3))


def partner(k):
    if k == 0:
        return 0
    odd = lax.rem(lax.axis_index("gz"), 2)
    return jnp.where(odd == 1, PARTNERS[1][k - 1], PARTNERS[0][k - 1])


def spot():
    return lax.rem(lax.axis_index("tm"), GROUP)


def chunk_of(k):
    flip = 2 * lax.rem(lax.axis_index("tm") // GROUP, 2)
    return lax.bitwise_xor(lax.bitwise_xor(spot(), flip), partner(k))


def near_side():
    return 1 - lax.rem(lax.axis_index("gz"), 2)


def split_rows(ref, *lead):
    half = ref.shape[-2] // 2
    return [ref[(*lead, pl.ds(odd, half, stride=2), slice(None))] for odd in (0, 1)]


def join_rows(ref, lead, pair):
    half = ref.shape[-2] // 2
    for odd in (0, 1):
        ref[(*lead, pl.ds(odd, half, stride=2), slice(None))] = pair[odd]


def load(ref, *lead):
    return [[ref[(*lead, c, odd)] for odd in (0, 1)] for c in range(3)]


def store(ref, lead, value):
    for c in range(3):
        for odd in (0, 1):
            ref[(*lead, c, odd)] = value[c][odd]


def advance(last, here, ahead, alpha, upward=1.0):
    diffuse = alpha * TIME_STEP * VISCOSITY
    carry = alpha * TIME_STEP * 0.5
    result = [[None, None] for _ in range(3)]
    for odd in (0, 1):
        speed = [here[0][odd] * carry, here[1][odd] * carry, here[2][odd] * (carry * upward)]
        to_next = [diffuse - s for s in speed]
        to_last = [diffuse + s for s in speed]
        for c in range(3):
            w = here[c][odd]
            rows, width = w.shape
            other = here[c][1 - odd]
            if odd:
                y_next, y_last = pltpu.roll(other, rows - 1, 0), other
            else:
                y_next, y_last = other, pltpu.roll(other, 1, 0)
            total = (alpha - 6.0 * diffuse) * w
            total = total + (
                to_next[0] * pltpu.roll(w, width - 1, 1) + to_last[0] * pltpu.roll(w, 1, 1)
            )
            total = total + (to_next[1] * y_next + to_last[1] * y_last)
            total = total + (to_next[2] * ahead[c][odd] + to_last[2] * last[c][odd])
            result[c][odd] = total
    return result


def blend(new, beta, base):
    return [[new[c][odd] + beta * base[c][odd] for odd in (0, 1)] for c in range(3)]


def faces_kernel(own_ref, far_ref, near_ref):
    layers, width = own_ref.shape[1], near_ref.shape[1]
    near = near_side()
    top = layers - width
    far_ref[...] = own_ref[:, pl.ds((1 - near) * top, width)]
    near_ref[...] = own_ref[:, pl.ds(near * top, width)]


def inside_kernel(own_ref, rate_ref, edges, middle, faded, damp_ref, damps, *fields):
    layers = own_ref.shape[1]
    half = layers // 2
    slices = lax.axis_size("tm")
    keep = (lax.axis_index("tm") != 0).astype(jnp.float32)

    def save(stage, z, value):
        low, high = z - stage, layers - 1 - stage - z
        if low < 3:
            store(edges, (stage, 0, low), value)
        if high < 3:
            store(edges, (stage, 1, high), value)

    for z in range(layers):
        side, slot = (0, z) if z < half else (1, layers - 1 - z)
        damp = [jnp.exp(r * (-1.0 / slices)) for r in split_rows(rate_ref, z)]
        start = [split_rows(own_ref, c, z) for c in range(3)]
        store(fields[0], (z,), start)
        save(0, z, start)
        for odd in (0, 1):
            damps[side, slot, odd] = damp[odd]
        lost = [[damp[odd] * keep * start[c][odd] for odd in (0, 1)] for c in range(3)]
        if slot < STAGES:
            store(faded, (side, slot), lost)
        else:
            store(middle, (side, slot - STAGES), lost)

    for stage in range(1, STAGES + 1):
        kind = (stage - 1) % 3
        alpha, beta = MIX[kind]
        source, target = fields[kind], fields[(kind + 1) % 3]
        below, here = load(source, stage - 1), load(source, stage)
        for z in range(stage, layers - stage):
            above = load(source, z + 1)
            new = advance(below, here, above, alpha)
            if beta is not None:
                new = blend(new, beta, load(fields[0], z))
            if stage < STAGES:
                store(target, (z,), new)
                save(stage, z, new)
            else:
                side, slot = (0, z) if z < half else (1, layers - 1 - z)
                lost = load(middle, side, slot - STAGES)
                store(
                    middle,
                    (side, slot - STAGES),
                    [[new[c][odd] - lost[c][odd] for odd in (0, 1)] for c in range(3)],
                )
            below, here = here, above

    chunk, near = chunk_of(0), near_side()
    share = layers // GROUP
    side = jnp.where(chunk < GROUP // 2, near, 1 - near)
    damp_ref[...] = damps[side, pl.ds(lax.rem(chunk, 2) * share, share)]


def border(side, face_ref, edges, middle, faded, jumps, strip):
    width = STAGES
    upward = 1.0 - 2.0 * side.astype(jnp.float32)
    for slot in range(width):
        layer = slot + side * (width - 1 - 2 * slot)
        store(strip, (0, slot), [split_rows(face_ref, c, layer) for c in range(3)])

    def at(stage, slot):
        if slot < width:
            return load(strip, stage, slot)
        return load(edges, stage, side, slot - width)

    def step(turn, _):
        for kind, (alpha, beta) in enumerate(MIX):
            stage = 3 * turn + kind
            last, here = at(stage, 0), at(stage, 1)
            for slot in range(width):
                ahead = at(stage, slot + 2)
                new = advance(last, here, ahead, alpha, upward)
                if beta is not None:
                    new = blend(new, beta, at(3 * turn, slot + 1 + kind))
                store(strip, (stage + 1, slot), new)
                last, here = here, ahead
        return 0

    lax.fori_loop(0, STEPS, step, 0)
    for slot in range(jumps.shape[0]):
        if slot < width:
            end, lost = load(strip, STAGES, slot), load(faded, side, slot)
            store(jumps, (slot,), [[end[c][odd] - lost[c][odd] for odd in (0, 1)] for c in range(3)])
        else:
            store(jumps, (slot,), load(middle, side, slot - width))


def near_kernel(face_ref, edges, middle, faded, jumps, strip):
    border(near_side(), face_ref, edges, middle, faded, jumps, strip)


def far_kernel(face_ref, edges, middle, faded, near_jumps, *refs):
    outs, strip, jumps = refs[:GROUP], refs[GROUP], refs[GROUP + 1]
    border(1 - near_side(), face_ref, edges, middle, faded, jumps.at[1], strip)
    jumps[0] = near_jumps[...]
    share = outs[0].shape[0]
    for k, out in enumerate(outs):
        chunk = chunk_of(k)
        out[...] = jumps[chunk // 2, pl.ds(lax.rem(chunk, 2) * share, share)]


def sort_in(jumps, order):
    for k in range(GROUP):
        order[lax.bitwise_xor(spot(), partner(k))] = jumps[k][...]


def sort_out(order, outs):
    for k in range(GROUP):
        outs[k][...] = order[lax.bitwise_xor(spot(), partner(k))]


def run(order, damp, total):
    for j in range(GROUP):
        jump = order[j]
        order[j] = total
        total = damp * total + jump
    return total


def total_kernel(*refs):
    jumps, damp_ref, out, order = refs[:GROUP], refs[GROUP], refs[GROUP + 1], refs[GROUP + 2]
    sort_in(jumps, order)
    out[...] = run(order, damp_ref[...][:, None], jnp.zeros(out.shape, jnp.float32))


def spread_kernel(*refs):
    carry_ref, jumps, damp_ref = refs[0], refs[1 : 1 + GROUP], refs[1 + GROUP]
    outs, order = refs[GROUP + 2 : -1], refs[-1]
    sort_in(jumps, order)
    run(order, damp_ref[...][:, None], jnp.where(lax.axis_index("tm") < GROUP, 0.0, carry_ref[...]))
    sort_out(order, outs)


def finish_kernel(own_ref, *refs):
    pieces, out = refs[:GROUP], refs[GROUP]
    layers = out.shape[1]
    share = layers // GROUP
    first_slice = lax.axis_index("tm") == 0

    @pl.when(first_slice)
    def _():
        out[...] = own_ref[...]

    @pl.when(jnp.logical_not(first_slice))
    def _():
        near = near_side()
        for k, piece in enumerate(pieces):
            chunk = chunk_of(k)
            side = jnp.where(chunk < GROUP // 2, near, 1 - near)
            for j in range(share):
                slot = lax.rem(chunk, 2) * share + j
                layer = slot + side * (layers - 1 - 2 * slot)
                for c in range(3):
                    join_rows(out, (c, layer), [piece[j, c, odd] for odd in (0, 1)])


def shards(states, rate):
    slices = lax.axis_size("tm")
    slabs = lax.axis_size("gz")
    groups = slices // GROUP
    own = states[0]
    layers, rows, width = own.shape[1:]
    half, share = layers // 2, layers // GROUP
    tile = (3, 2, rows // 2, width)
    face = f32(3, STAGES, rows, width)
    piece = f32(share, *tile)
    team = lax.axis_index("tm") // GROUP

    def halo(value, pairs):
        return lax.ppermute(value, "gz", [(i, j % slabs) for i, j in pairs])

    def swap(parts):
        moved = [parts[0]]
        for k in range(1, GROUP):
            pairs = [
                (i * slabs + g, (i ^ PARTNERS[g % 2][k - 1]) * slabs + g)
                for i in range(slices)
                for g in range(slabs)
            ]
            moved.append(lax.ppermute(parts[k], ("tm", "gz"), pairs))
        return moved

    def onward(value, distance):
        flip = 2 * (distance % 2)
        pairs = [(i, ((i ^ flip) + distance * GROUP) % slices) for i in range(slices)]
        return lax.ppermute(value, "tm", pairs)

    far_face, near_face = call(faces_kernel, [face, face], own)
    near_face = halo(near_face, [(i, i ^ 1) for i in range(slabs)])
    far_face = halo(far_face, [(i, i + 1 if i % 2 else i - 1 + slabs) for i in range(slabs)])
    edges, middle, faded, damp = call(
        inside_kernel,
        [
            f32(STAGES, 2, 3, *tile),
            f32(2, half - STAGES, *tile),
            f32(2, STAGES, *tile),
            f32(share, *tile[1:]),
        ],
        own, rate,
        scratch=[pltpu.VMEM((2, half, *tile[1:]), jnp.float32)]
        + [pltpu.VMEM((layers, *tile), jnp.float32)] * 3,
        flops=1 << 26,
    )
    strip = pltpu.VMEM((STAGES + 1, STAGES, *tile), jnp.float32)
    near_jumps = call(
        near_kernel, f32(half, *tile), near_face, edges, middle, faded, scratch=[strip], flops=1 << 24
    )
    jumps = call(
        far_kernel, [piece] * GROUP, far_face, edges, middle, faded, near_jumps,
        scratch=[strip, pltpu.VMEM((2, half, *tile), jnp.float32)],
    )
    order = pltpu.VMEM((GROUP, *piece.shape), jnp.float32)
    jumps = swap(jumps)
    if groups > 1:
        total = call(total_kernel, piece, *jumps, damp, scratch=[order])
        carry = onward(total, 1)
        if groups > 2:
            carry = jnp.where(team < 1, 0.0, carry)
            fade, distance = damp[:, None] ** GROUP, 1
            while distance < groups - 1:
                carry = carry + jnp.where(team < distance, 0.0, fade * onward(carry, distance))
                distance, fade = 2 * distance, fade * fade
    else:
        carry = jnp.zeros(piece.shape, jnp.float32)
    news = call(spread_kernel, [piece] * GROUP, carry, *jumps, damp, scratch=[order])
    updated = call(finish_kernel, f32(*own.shape), own, *swap(news))
    return updated[None]


def solution(mesh):
    return jax.shard_map(
        shards,
        mesh=mesh,
        in_specs=(P("tm", None, "gz", None, None), P("gz", None, None)),
        out_specs=P("tm", None, "gz", None, None),
        check_vma=False,
    )
```

```python
import functools

import jax
import jax.numpy as jnp
from jax import lax
from jax.experimental import pallas as pl
from jax.experimental.pallas import tpu as pltpu
from jax.sharding import PartitionSpec as P

STEPS = 2
STAGES = 3 * STEPS
GROUP = 4
VISCOSITY = 0.05
TIME_STEP = 0.2
MIX = ((1.0, None), (0.25, 0.75), (2.0 / 3.0, 1.0 / 3.0))
VMEM = pl.BlockSpec(memory_space=pltpu.VMEM)
PARAMS = pltpu.CompilerParams(vmem_limit_bytes=16 * 1024 * 1024)


def call(kernel, out_shape, *args, scratch=(), flops=None):
    cost = None
    if flops is not None:
        cost = pl.CostEstimate(flops=flops, bytes_accessed=1 << 20, transcendentals=0)
    return pl.pallas_call(
        kernel,
        out_shape=out_shape,
        in_specs=[VMEM] * len(args),
        out_specs=jax.tree.map(lambda _: VMEM, out_shape),
        scratch_shapes=list(scratch),
        compiler_params=PARAMS,
        cost_estimate=cost,
    )(*args)


def f32(*shape):
    return jax.ShapeDtypeStruct(shape, jnp.float32)


def partner(k):
    return (GROUP - k) % GROUP


def spot():
    return lax.rem(lax.axis_index("tm"), GROUP)


def chunk_of(k):
    flip = 2 * lax.rem(lax.axis_index("tm") // GROUP, 2)
    return lax.bitwise_xor(lax.bitwise_xor(spot(), flip), partner(k))


def near_side():
    return 1 - lax.rem(lax.axis_index("gz"), 2)


def split_rows(ref, *lead):
    half = ref.shape[-2] // 2
    return [ref[(*lead, pl.ds(odd, half, stride=2), slice(None))] for odd in (0, 1)]


def join_rows(ref, lead, pair):
    half = ref.shape[-2] // 2
    for odd in (0, 1):
        ref[(*lead, pl.ds(odd, half, stride=2), slice(None))] = pair[odd]


def load(ref, *lead):
    return [[ref[(*lead, c, odd)] for odd in (0, 1)] for c in range(3)]


def store(ref, lead, value):
    for c in range(3):
        for odd in (0, 1):
            ref[(*lead, c, odd)] = value[c][odd]


def advance(last, here, ahead, alpha, upward=1.0):
    diffuse = alpha * TIME_STEP * VISCOSITY
    carry = alpha * TIME_STEP * 0.5
    result = [[None, None] for _ in range(3)]
    for odd in (0, 1):
        speed = [here[0][odd] * carry, here[1][odd] * carry, here[2][odd] * (carry * upward)]
        to_next = [diffuse - s for s in speed]
        to_last = [diffuse + s for s in speed]
        for c in range(3):
            w = here[c][odd]
            rows, width = w.shape
            other = here[c][1 - odd]
            if odd:
                y_next, y_last = pltpu.roll(other, rows - 1, 0), other
            else:
                y_next, y_last = other, pltpu.roll(other, 1, 0)
            total = (alpha - 6.0 * diffuse) * w
            total = total + (
                to_next[0] * pltpu.roll(w, width - 1, 1) + to_last[0] * pltpu.roll(w, 1, 1)
            )
            total = total + (to_next[1] * y_next + to_last[1] * y_last)
            total = total + (to_next[2] * ahead[c][odd] + to_last[2] * last[c][odd])
            result[c][odd] = total
    return result


def blend(new, beta, base):
    return [[new[c][odd] + beta * base[c][odd] for odd in (0, 1)] for c in range(3)]


def faces_kernel(own_ref, far_ref, near_ref):
    layers, width = own_ref.shape[1], near_ref.shape[1]
    near = near_side()
    top = layers - width
    far_ref[...] = own_ref[:, pl.ds((1 - near) * top, width)]
    near_ref[...] = own_ref[:, pl.ds(near * top, width)]


def inside_kernel(own_ref, rate_ref, edges, middle, faded, damp_ref, kept, damps, *fields):
    layers = own_ref.shape[1]
    half = layers // 2
    slices = lax.axis_size("tm")
    keep = (lax.axis_index("tm") != 0).astype(jnp.float32)

    def save(stage, z, value):
        low, high = z - stage, layers - 1 - stage - z
        if low < 3:
            store(edges, (stage, 0, low), value)
        if high < 3:
            store(edges, (stage, 1, high), value)

    for z in range(layers):
        side, slot = (0, z) if z < half else (1, layers - 1 - z)
        damp = [jnp.exp(r * (-1.0 / slices)) for r in split_rows(rate_ref, z)]
        start = [split_rows(own_ref, c, z) for c in range(3)]
        store(fields[0], (z,), start)
        store(kept, (side, slot), start)
        save(0, z, start)
        for odd in (0, 1):
            damps[side, slot, odd] = damp[odd]
        lost = [[damp[odd] * keep * start[c][odd] for odd in (0, 1)] for c in range(3)]
        if slot < STAGES:
            store(faded, (side, slot), lost)
        else:
            store(middle, (side, slot - STAGES), lost)

    for stage in range(1, STAGES + 1):
        kind = (stage - 1) % 3
        alpha, beta = MIX[kind]
        source, target = fields[kind], fields[(kind + 1) % 3]
        below, here = load(source, stage - 1), load(source, stage)
        for z in range(stage, layers - stage):
            above = load(source, z + 1)
            new = advance(below, here, above, alpha)
            if beta is not None:
                new = blend(new, beta, load(fields[0], z))
            if stage < STAGES:
                store(target, (z,), new)
                save(stage, z, new)
            else:
                side, slot = (0, z) if z < half else (1, layers - 1 - z)
                lost = load(middle, side, slot - STAGES)
                store(
                    middle,
                    (side, slot - STAGES),
                    [[new[c][odd] - lost[c][odd] for odd in (0, 1)] for c in range(3)],
                )
            below, here = here, above

    chunk, near = chunk_of(0), near_side()
    share = layers // GROUP
    side = jnp.where(chunk < GROUP // 2, near, 1 - near)
    damp_ref[...] = damps[side, pl.ds(lax.rem(chunk, 2) * share, share)]


def border(side, face_ref, edges, middle, faded, jumps, strip):
    width = STAGES
    upward = 1.0 - 2.0 * side.astype(jnp.float32)
    for slot in range(width):
        layer = slot + side * (width - 1 - 2 * slot)
        store(strip, (0, slot), [split_rows(face_ref, c, layer) for c in range(3)])

    def at(stage, slot):
        if slot < width:
            return load(strip, stage, slot)
        return load(edges, stage, side, slot - width)

    def step(turn, _):
        for kind, (alpha, beta) in enumerate(MIX):
            stage = 3 * turn + kind
            last, here = at(stage, 0), at(stage, 1)
            for slot in range(width):
                ahead = at(stage, slot + 2)
                new = advance(last, here, ahead, alpha, upward)
                if beta is not None:
                    new = blend(new, beta, at(3 * turn, slot + 1 + kind))
                store(strip, (stage + 1, slot), new)
                last, here = here, ahead
        return 0

    lax.fori_loop(0, STEPS, step, 0)
    for slot in range(jumps.shape[0]):
        if slot < width:
            end, lost = load(strip, STAGES, slot), load(faded, side, slot)
            store(jumps, (slot,), [[end[c][odd] - lost[c][odd] for odd in (0, 1)] for c in range(3)])
        else:
            store(jumps, (slot,), load(middle, side, slot - width))


def near_kernel(face_ref, edges, middle, faded, jumps, strip):
    border(near_side(), face_ref, edges, middle, faded, jumps, strip)


def far_kernel(face_ref, edges, middle, faded, near_jumps, *refs):
    outs, strip, jumps = refs[:GROUP], refs[GROUP], refs[GROUP + 1]
    border(1 - near_side(), face_ref, edges, middle, faded, jumps.at[1], strip)
    jumps[0] = near_jumps[...]
    share = outs[0].shape[0]
    for k, out in enumerate(outs):
        chunk = chunk_of(k)
        out[...] = jumps[chunk // 2, pl.ds(lax.rem(chunk, 2) * share, share)]


def sort_in(jumps, order):
    for k in range(GROUP):
        order[lax.bitwise_xor(spot(), partner(k))] = jumps[k][...]


def sort_out(order, outs):
    for k in range(GROUP):
        outs[k][...] = order[lax.bitwise_xor(spot(), partner(k))]


def run(order, damp, total):
    for j in range(GROUP):
        jump = order[j]
        order[j] = total
        total = damp * total + jump
    return total


def total_kernel(*refs):
    jumps, damp_ref, out, order = refs[:GROUP], refs[GROUP], refs[GROUP + 1], refs[GROUP + 2]
    sort_in(jumps, order)
    out[...] = run(order, damp_ref[...][:, None], jnp.zeros(out.shape, jnp.float32))


def spread_kernel(*refs):
    carry_ref, jumps, damp_ref = refs[0], refs[1 : 1 + GROUP], refs[1 + GROUP]
    outs, order = refs[GROUP + 2 : -1], refs[-1]
    sort_in(jumps, order)
    run(order, damp_ref[...][:, None], jnp.where(lax.axis_index("tm") < GROUP, 0.0, carry_ref[...]))
    sort_out(order, outs)


def finish_kernel(kept, *refs):
    pieces, out = refs[:GROUP], refs[GROUP]
    layers = out.shape[1]
    share = layers // GROUP
    first_slice = lax.axis_index("tm") == 0
    near = near_side()

    def put(side, slot, layer_of):
        layer = slot + side * (layers - 1 - 2 * slot)
        for c in range(3):
            join_rows(out, (c, layer), layer_of[c])

    @pl.when(first_slice)
    def _():
        for side in (0, 1):
            for slot in range(layers // 2):
                put(side, slot, load(kept, side, slot))

    @pl.when(jnp.logical_not(first_slice))
    def _():
        for k, piece in enumerate(pieces):
            chunk = chunk_of(k)
            side = jnp.where(chunk < GROUP // 2, near, 1 - near)
            for j in range(share):
                put(side, lax.rem(chunk, 2) * share + j, load(piece, j))


def shards(states, rate):
    slices = lax.axis_size("tm")
    slabs = lax.axis_size("gz")
    groups = slices // GROUP
    own = states[0]
    layers, rows, width = own.shape[1:]
    half, share = layers // 2, layers // GROUP
    tile = (3, 2, rows // 2, width)
    face = f32(3, STAGES, rows, width)
    piece = f32(share, *tile)
    team = lax.axis_index("tm") // GROUP

    def halo(value, pairs):
        return lax.ppermute(value, "gz", [(i, j % slabs) for i, j in pairs])

    def swap(parts):
        return [parts[0]] + [
            lax.ppermute(parts[k], "tm", [(i, i ^ partner(k)) for i in range(slices)])
            for k in range(1, GROUP)
        ]

    def onward(value, distance):
        flip = 2 * (distance % 2)
        pairs = [(i, ((i ^ flip) + distance * GROUP) % slices) for i in range(slices)]
        return lax.ppermute(value, "tm", pairs)

    far_face, near_face = call(faces_kernel, [face, face], own)
    near_face = halo(near_face, [(i, i ^ 1) for i in range(slabs)])
    far_face = halo(far_face, [(i, i + 1 if i % 2 else i - 1 + slabs) for i in range(slabs)])
    edges, middle, faded, damp, kept = call(
        inside_kernel,
        [
            f32(STAGES, 2, 3, *tile),
            f32(2, half - STAGES, *tile),
            f32(2, STAGES, *tile),
            f32(share, *tile[1:]),
            f32(2, half, *tile),
        ],
        own, rate,
        scratch=[pltpu.VMEM((2, half, *tile[1:]), jnp.float32)]
        + [pltpu.VMEM((layers, *tile), jnp.float32)] * 3,
        flops=1 << 26,
    )
    strip = pltpu.VMEM((STAGES + 1, STAGES, *tile), jnp.float32)
    near_jumps = call(
        near_kernel, f32(half, *tile), near_face, edges, middle, faded, scratch=[strip], flops=1 << 24
    )
    jumps = call(
        far_kernel, [piece] * GROUP, far_face, edges, middle, faded, near_jumps,
        scratch=[strip, pltpu.VMEM((2, half, *tile), jnp.float32)],
    )
    order = pltpu.VMEM((GROUP, *piece.shape), jnp.float32)
    jumps = swap(jumps)
    if groups > 1:
        total = call(total_kernel, piece, *jumps, damp, scratch=[order])
        carry = onward(total, 1)
        if groups > 2:
            carry = jnp.where(team < 1, 0.0, carry)
            fade, distance = damp[:, None] ** GROUP, 1
            while distance < groups - 1:
                carry = carry + jnp.where(team < distance, 0.0, fade * onward(carry, distance))
                distance, fade = 2 * distance, fade * fade
    else:
        carry = jnp.zeros(piece.shape, jnp.float32)
    news = call(spread_kernel, [piece] * GROUP, carry, *jumps, damp, scratch=[order])
    updated = call(finish_kernel, f32(*own.shape), kept, *swap(news))
    return updated[None]


def solution(mesh):
    return jax.shard_map(
        shards,
        mesh=mesh,
        in_specs=(P("tm", None, "gz", None, None), P("gz", None, None)),
        out_specs=P("tm", None, "gz", None, None),
        check_vma=False,
    )
```

```python
import functools

import jax
import jax.numpy as jnp
from jax import lax
from jax.experimental import pallas as pl
from jax.experimental.pallas import tpu as pltpu
from jax.sharding import PartitionSpec as P

STEPS = 2
STAGES = 3 * STEPS
GROUP = 4
VISCOSITY = 0.05
TIME_STEP = 0.2
MIX = ((1.0, None), (0.25, 0.75), (2.0 / 3.0, 1.0 / 3.0))
VMEM = pl.BlockSpec(memory_space=pltpu.VMEM)
PARAMS = pltpu.CompilerParams(vmem_limit_bytes=16 * 1024 * 1024)


def call(kernel, out_shape, *args, scratch=(), flops=None):
    cost = None
    if flops is not None:
        cost = pl.CostEstimate(flops=flops, bytes_accessed=1 << 20, transcendentals=0)
    return pl.pallas_call(
        kernel,
        out_shape=out_shape,
        in_specs=[VMEM] * len(args),
        out_specs=jax.tree.map(lambda _: VMEM, out_shape),
        scratch_shapes=list(scratch),
        compiler_params=PARAMS,
        cost_estimate=cost,
    )(*args)


def f32(*shape):
    return jax.ShapeDtypeStruct(shape, jnp.float32)


def partner(k):
    return (GROUP - k) % GROUP


def spot():
    return lax.rem(lax.axis_index("tm"), GROUP)


def chunk_of(k):
    flip = 2 * lax.rem(lax.axis_index("tm") // GROUP, 2)
    return lax.bitwise_xor(lax.bitwise_xor(spot(), flip), partner(k))


def near_side():
    return 1 - lax.rem(lax.axis_index("gz"), 2)


def split_rows(ref, *lead):
    half = ref.shape[-2] // 2
    return [ref[(*lead, pl.ds(odd, half, stride=2), slice(None))] for odd in (0, 1)]


def join_rows(ref, lead, pair):
    half = ref.shape[-2] // 2
    for odd in (0, 1):
        ref[(*lead, pl.ds(odd, half, stride=2), slice(None))] = pair[odd]


def load(ref, *lead):
    return [[ref[(*lead, c, odd)] for odd in (0, 1)] for c in range(3)]


def store(ref, lead, value):
    for c in range(3):
        for odd in (0, 1):
            ref[(*lead, c, odd)] = value[c][odd]


def advance(last, here, ahead, alpha, upward=1.0):
    diffuse = alpha * TIME_STEP * VISCOSITY
    carry = alpha * TIME_STEP * 0.5
    result = [[None, None] for _ in range(3)]
    for odd in (0, 1):
        speed = [here[0][odd] * carry, here[1][odd] * carry, here[2][odd] * (carry * upward)]
        to_next = [diffuse - s for s in speed]
        to_last = [diffuse + s for s in speed]
        for c in range(3):
            w = here[c][odd]
            rows, width = w.shape
            other = here[c][1 - odd]
            if odd:
                y_next, y_last = pltpu.roll(other, rows - 1, 0), other
            else:
                y_next, y_last = other, pltpu.roll(other, 1, 0)
            total = (alpha - 6.0 * diffuse) * w
            total = total + (
                to_next[0] * pltpu.roll(w, width - 1, 1) + to_last[0] * pltpu.roll(w, 1, 1)
            )
            total = total + (to_next[1] * y_next + to_last[1] * y_last)
            total = total + (to_next[2] * ahead[c][odd] + to_last[2] * last[c][odd])
            result[c][odd] = total
    return result


def blend(new, beta, base):
    return [[new[c][odd] + beta * base[c][odd] for odd in (0, 1)] for c in range(3)]


def faces_kernel(own_ref, far_ref, near_ref):
    layers, width = own_ref.shape[1], near_ref.shape[1]
    near = near_side()
    top = layers - width
    far_ref[...] = own_ref[:, pl.ds((1 - near) * top, width)]
    near_ref[...] = own_ref[:, pl.ds(near * top, width)]


def inside_kernel(own_ref, rate_ref, edges, middle, faded, damp_ref, kept, damps, *fields):
    layers = own_ref.shape[1]
    half = layers // 2
    slices = lax.axis_size("tm")
    keep = (lax.axis_index("tm") != 0).astype(jnp.float32)

    def save(stage, z, value):
        low, high = z - stage, layers - 1 - stage - z
        if low < 3:
            store(edges, (stage, 0, low), value)
        if high < 3:
            store(edges, (stage, 1, high), value)

    for z in range(layers):
        side, slot = (0, z) if z < half else (1, layers - 1 - z)
        damp = [jnp.exp(r * (-1.0 / slices)) for r in split_rows(rate_ref, z)]
        start = [split_rows(own_ref, c, z) for c in range(3)]
        store(fields[0], (z,), start)
        store(kept, (side, slot), start)
        save(0, z, start)
        for odd in (0, 1):
            damps[side, slot, odd] = damp[odd]
        lost = [[damp[odd] * keep * start[c][odd] for odd in (0, 1)] for c in range(3)]
        if slot < STAGES:
            store(faded, (side, slot), lost)
        else:
            store(middle, (side, slot - STAGES), lost)

    for stage in range(1, STAGES + 1):
        kind = (stage - 1) % 3
        alpha, beta = MIX[kind]
        source, target = fields[kind], fields[(kind + 1) % 3]
        below, here = load(source, stage - 1), load(source, stage)
        for z in range(stage, layers - stage):
            above = load(source, z + 1)
            new = advance(below, here, above, alpha)
            if beta is not None:
                new = blend(new, beta, load(fields[0], z))
            if stage < STAGES:
                store(target, (z,), new)
                save(stage, z, new)
            else:
                side, slot = (0, z) if z < half else (1, layers - 1 - z)
                lost = load(middle, side, slot - STAGES)
                store(
                    middle,
                    (side, slot - STAGES),
                    [[new[c][odd] - lost[c][odd] for odd in (0, 1)] for c in range(3)],
                )
            below, here = here, above

    share = half // GROUP
    for far in (0, 1):
        side = far + (1 - 2 * far) * near_side()
        damp_ref[far] = damps[side, pl.ds(chunk_of(0) * share, share)]


def border(side, face_ref, edges, middle, faded, jumps, strip):
    width = STAGES
    upward = 1.0 - 2.0 * side.astype(jnp.float32)
    for slot in range(width):
        layer = slot + side * (width - 1 - 2 * slot)
        store(strip, (0, slot), [split_rows(face_ref, c, layer) for c in range(3)])

    def at(stage, slot):
        if slot < width:
            return load(strip, stage, slot)
        return load(edges, stage, side, slot - width)

    def step(turn, _):
        for kind, (alpha, beta) in enumerate(MIX):
            stage = 3 * turn + kind
            last, here = at(stage, 0), at(stage, 1)
            for slot in range(width):
                ahead = at(stage, slot + 2)
                new = advance(last, here, ahead, alpha, upward)
                if beta is not None:
                    new = blend(new, beta, at(3 * turn, slot + 1 + kind))
                store(strip, (stage + 1, slot), new)
                last, here = here, ahead
        return 0

    lax.fori_loop(0, STEPS, step, 0)
    for slot in range(jumps.shape[0]):
        if slot < width:
            end, lost = load(strip, STAGES, slot), load(faded, side, slot)
            store(jumps, (slot,), [[end[c][odd] - lost[c][odd] for odd in (0, 1)] for c in range(3)])
        else:
            store(jumps, (slot,), load(middle, side, slot - width))


def jumps_kernel(far, face_ref, edges, middle, faded, *refs):
    outs, strip, jumps = refs[:GROUP], refs[-2], refs[-1]
    side = far + (1 - 2 * far) * near_side()
    border(side, face_ref, edges, middle, faded, jumps, strip)
    share = outs[0].shape[0]
    for k, out in enumerate(outs):
        out[...] = jumps[pl.ds(chunk_of(k) * share, share)]


def sort_in(jumps, order):
    for k in range(GROUP):
        order[lax.bitwise_xor(spot(), partner(k))] = jumps[k][...]


def sort_out(order, outs):
    for k in range(GROUP):
        outs[k][...] = order[lax.bitwise_xor(spot(), partner(k))]


def run(order, damp, total):
    for j in range(GROUP):
        jump = order[j]
        order[j] = total
        total = damp * total + jump
    return total


def total_kernel(far, *refs):
    jumps, damp_ref, out, order = refs[:GROUP], refs[GROUP], refs[GROUP + 1], refs[GROUP + 2]
    sort_in(jumps, order)
    out[...] = run(order, damp_ref[far][:, None], jnp.zeros(out.shape, jnp.float32))


def spread_kernel(far, *refs):
    carry_ref, jumps, damp_ref = refs[0], refs[1 : 1 + GROUP], refs[1 + GROUP]
    outs, order = refs[GROUP + 2 : -1], refs[-1]
    sort_in(jumps, order)
    run(order, damp_ref[far][:, None], jnp.where(lax.axis_index("tm") < GROUP, 0.0, carry_ref[...]))
    sort_out(order, outs)


def finish_kernel(kept, *refs):
    out = refs[-1]
    layers = out.shape[1]
    half = layers // 2
    share = half // GROUP
    first_slice = lax.axis_index("tm") == 0

    def put(side, slot, layer_of):
        layer = slot + side * (layers - 1 - 2 * slot)
        for c in range(3):
            join_rows(out, (c, layer), layer_of[c])

    @pl.when(first_slice)
    def _():
        for side in (0, 1):
            for slot in range(half):
                put(side, slot, load(kept, side, slot))

    @pl.when(jnp.logical_not(first_slice))
    def _():
        for far in (0, 1):
            side = far + (1 - 2 * far) * near_side()
            for k in range(GROUP):
                for j in range(share):
                    put(side, chunk_of(k) * share + j, load(refs[(1 - far) * GROUP + k], j))


def shards(states, rate):
    slices = lax.axis_size("tm")
    slabs = lax.axis_size("gz")
    groups = slices // GROUP
    own = states[0]
    layers, rows, width = own.shape[1:]
    half, share = layers // 2, layers // 2 // GROUP
    tile = (3, 2, rows // 2, width)
    face = f32(3, STAGES, rows, width)
    piece = f32(share, *tile)
    team = lax.axis_index("tm") // GROUP

    def halo(value, pairs):
        return lax.ppermute(value, "gz", [(i, j % slabs) for i, j in pairs])

    def swap(parts):
        return [parts[0]] + [
            lax.ppermute(parts[k], "tm", [(i, i ^ partner(k)) for i in range(slices)])
            for k in range(1, GROUP)
        ]

    def onward(value, distance):
        flip = 2 * (distance % 2)
        pairs = [(i, ((i ^ flip) + distance * GROUP) % slices) for i in range(slices)]
        return lax.ppermute(value, "tm", pairs)

    far_face, near_face = call(faces_kernel, [face, face], own)
    near_face = halo(near_face, [(i, i ^ 1) for i in range(slabs)])
    far_face = halo(far_face, [(i, i + 1 if i % 2 else i - 1 + slabs) for i in range(slabs)])
    edges, middle, faded, damp, kept = call(
        inside_kernel,
        [
            f32(STAGES, 2, 3, *tile),
            f32(2, half - STAGES, *tile),
            f32(2, STAGES, *tile),
            f32(2, share, *tile[1:]),
            f32(2, half, *tile),
        ],
        own, rate,
        scratch=[pltpu.VMEM((2, half, *tile[1:]), jnp.float32)]
        + [pltpu.VMEM((layers, *tile), jnp.float32)] * 3,
        flops=1 << 26,
    )
    strip = pltpu.VMEM((STAGES + 1, STAGES, *tile), jnp.float32)
    order = pltpu.VMEM((GROUP, *piece.shape), jnp.float32)

    def after(value, earlier):
        return lax.optimization_barrier((value, earlier))[0]

    halves = []
    for far, face_ref in enumerate((near_face, far_face)):
        jumps = call(
            functools.partial(jumps_kernel, far), [piece] * GROUP, face_ref, edges, middle, faded,
            scratch=[strip, pltpu.VMEM((half, *tile), jnp.float32)],
            flops=1 << 32,
        )
        halves.append(swap(jumps))

    carries, total = [], None
    for far, jumps in enumerate(halves):
        if far:
            jumps[0] = after(jumps[0], total)
        total = call(
            functools.partial(total_kernel, far), piece, *jumps, damp, scratch=[order]
        )
        carry = onward(total, 1)
        if groups > 2:
            carry = jnp.where(team < 1, 0.0, carry)
            fade, distance = damp[far][:, None] ** GROUP, 1
            while distance < groups - 1:
                carry = carry + jnp.where(team < distance, 0.0, fade * onward(carry, distance))
                distance, fade = 2 * distance, fade * fade
        carries.append(carry)

    pieces, news = [], None
    for far, (jumps, carry) in enumerate(zip(halves, carries)):
        if far:
            jumps[0] = after(jumps[0], news[0])
        news = call(
            functools.partial(spread_kernel, far), [piece] * GROUP, carry, *jumps, damp,
            scratch=[order],
            flops=1 << 32,
        )
        pieces = swap(news) + pieces
    updated = call(finish_kernel, f32(*own.shape), kept, *pieces)
    return updated[None]


def solution(mesh):
    return jax.shard_map(
        shards,
        mesh=mesh,
        in_specs=(P("tm", None, "gz", None, None), P("gz", None, None)),
        out_specs=P("tm", None, "gz", None, None),
        check_vma=False,
    )
```

```python
import functools

import jax
import jax.numpy as jnp
from jax import lax
from jax.experimental import pallas as pl
from jax.experimental.pallas import tpu as pltpu
from jax.sharding import PartitionSpec as P

STEPS = 2
STAGES = 3 * STEPS
GROUP = 4
VISCOSITY = 0.05
TIME_STEP = 0.2
MIX = ((1.0, None), (0.25, 0.75), (2.0 / 3.0, 1.0 / 3.0))
VMEM = pl.BlockSpec(memory_space=pltpu.VMEM)
PARAMS = pltpu.CompilerParams(vmem_limit_bytes=16 * 1024 * 1024)


def call(kernel, out_shape, *args, scratch=(), flops=None):
    cost = None
    if flops is not None:
        cost = pl.CostEstimate(flops=flops, bytes_accessed=1 << 20, transcendentals=0)
    return pl.pallas_call(
        kernel,
        out_shape=out_shape,
        in_specs=[VMEM] * len(args),
        out_specs=jax.tree.map(lambda _: VMEM, out_shape),
        scratch_shapes=list(scratch),
        compiler_params=PARAMS,
        cost_estimate=cost,
    )(*args)


def f32(*shape):
    return jax.ShapeDtypeStruct(shape, jnp.float32)


def partner(k):
    return (GROUP - k) % GROUP


def spot():
    return lax.rem(lax.axis_index("tm"), GROUP)


def chunk_of(k):
    return lax.bitwise_xor(spot(), partner(k))


def near_side():
    return 1 - lax.rem(lax.axis_index("gz"), 2)


def split_rows(ref, *lead):
    half = ref.shape[-2] // 2
    return [ref[(*lead, pl.ds(odd, half, stride=2), slice(None))] for odd in (0, 1)]


def join_rows(ref, lead, pair):
    half = ref.shape[-2] // 2
    for odd in (0, 1):
        ref[(*lead, pl.ds(odd, half, stride=2), slice(None))] = pair[odd]


def load(ref, *lead):
    return [[ref[(*lead, c, odd)] for odd in (0, 1)] for c in range(3)]


def store(ref, lead, value):
    for c in range(3):
        for odd in (0, 1):
            ref[(*lead, c, odd)] = value[c][odd]


def advance(last, here, ahead, alpha, upward=1.0):
    diffuse = alpha * TIME_STEP * VISCOSITY
    carry = alpha * TIME_STEP * 0.5
    result = [[None, None] for _ in range(3)]
    for odd in (0, 1):
        speed = [here[0][odd] * carry, here[1][odd] * carry, here[2][odd] * (carry * upward)]
        to_next = [diffuse - s for s in speed]
        to_last = [diffuse + s for s in speed]
        for c in range(3):
            w = here[c][odd]
            rows, width = w.shape
            other = here[c][1 - odd]
            if odd:
                y_next, y_last = pltpu.roll(other, rows - 1, 0), other
            else:
                y_next, y_last = other, pltpu.roll(other, 1, 0)
            total = (alpha - 6.0 * diffuse) * w
            total = total + (
                to_next[0] * pltpu.roll(w, width - 1, 1) + to_last[0] * pltpu.roll(w, 1, 1)
            )
            total = total + (to_next[1] * y_next + to_last[1] * y_last)
            total = total + (to_next[2] * ahead[c][odd] + to_last[2] * last[c][odd])
            result[c][odd] = total
    return result


def blend(new, beta, base):
    return [[new[c][odd] + beta * base[c][odd] for odd in (0, 1)] for c in range(3)]


def faces_kernel(own_ref, far_ref, near_ref):
    layers, width = own_ref.shape[1], near_ref.shape[1]
    near = near_side()
    top = layers - width
    far_ref[...] = own_ref[:, pl.ds((1 - near) * top, width)]
    near_ref[...] = own_ref[:, pl.ds(near * top, width)]


def inside_kernel(own_ref, rate_ref, edges, middle, faded, damp_ref, kept, damps, *fields):
    layers = own_ref.shape[1]
    half = layers // 2
    slices = lax.axis_size("tm")
    keep = (lax.axis_index("tm") != 0).astype(jnp.float32)

    def save(stage, z, value):
        low, high = z - stage, layers - 1 - stage - z
        if low < 3:
            store(edges, (stage, 0, low), value)
        if high < 3:
            store(edges, (stage, 1, high), value)

    for z in range(layers):
        side, slot = (0, z) if z < half else (1, layers - 1 - z)
        damp = [jnp.exp(r * (-1.0 / slices)) for r in split_rows(rate_ref, z)]
        start = [split_rows(own_ref, c, z) for c in range(3)]
        store(fields[0], (z,), start)
        store(kept, (side, slot), start)
        save(0, z, start)
        for odd in (0, 1):
            damps[side, slot, odd] = damp[odd]
        lost = [[damp[odd] * keep * start[c][odd] for odd in (0, 1)] for c in range(3)]
        if slot < STAGES:
            store(faded, (side, slot), lost)
        else:
            store(middle, (side, slot - STAGES), lost)

    for stage in range(1, STAGES + 1):
        kind = (stage - 1) % 3
        alpha, beta = MIX[kind]
        source, target = fields[kind], fields[(kind + 1) % 3]
        below, here = load(source, stage - 1), load(source, stage)
        for z in range(stage, layers - stage):
            above = load(source, z + 1)
            new = advance(below, here, above, alpha)
            if beta is not None:
                new = blend(new, beta, load(fields[0], z))
            if stage < STAGES:
                store(target, (z,), new)
                save(stage, z, new)
            else:
                side, slot = (0, z) if z < half else (1, layers - 1 - z)
                lost = load(middle, side, slot - STAGES)
                store(
                    middle,
                    (side, slot - STAGES),
                    [[new[c][odd] - lost[c][odd] for odd in (0, 1)] for c in range(3)],
                )
            below, here = here, above

    share = half // GROUP
    for far in (0, 1):
        side = far + (1 - 2 * far) * near_side()
        damp_ref[far] = damps[side, pl.ds(chunk_of(0) * share, share)]


def border(side, face_ref, edges, middle, faded, jumps, strip):
    width = STAGES
    upward = 1.0 - 2.0 * side.astype(jnp.float32)
    for slot in range(width):
        layer = slot + side * (width - 1 - 2 * slot)
        store(strip, (0, slot), [split_rows(face_ref, c, layer) for c in range(3)])

    def at(stage, slot):
        if slot < width:
            return load(strip, stage, slot)
        return load(edges, stage, side, slot - width)

    def step(turn, _):
        for kind, (alpha, beta) in enumerate(MIX):
            stage = 3 * turn + kind
            last, here = at(stage, 0), at(stage, 1)
            for slot in range(width):
                ahead = at(stage, slot + 2)
                new = advance(last, here, ahead, alpha, upward)
                if beta is not None:
                    new = blend(new, beta, at(3 * turn, slot + 1 + kind))
                store(strip, (stage + 1, slot), new)
                last, here = here, ahead
        return 0

    lax.fori_loop(0, STEPS, step, 0)
    for slot in range(jumps.shape[0]):
        if slot < width:
            end, lost = load(strip, STAGES, slot), load(faded, side, slot)
            store(jumps, (slot,), [[end[c][odd] - lost[c][odd] for odd in (0, 1)] for c in range(3)])
        else:
            store(jumps, (slot,), load(middle, side, slot - width))


def jumps_kernel(far, face_ref, edges, middle, faded, *refs):
    outs, strip, jumps = refs[:GROUP], refs[-2], refs[-1]
    side = far + (1 - 2 * far) * near_side()
    border(side, face_ref, edges, middle, faded, jumps, strip)
    share = outs[0].shape[0]
    for k, out in enumerate(outs):
        out[...] = jumps[pl.ds(chunk_of(k) * share, share)]


def sort_in(jumps, order):
    for k in range(GROUP):
        order[lax.bitwise_xor(spot(), partner(k))] = jumps[k][...]


def sort_out(order, outs):
    for k in range(GROUP):
        outs[k][...] = order[lax.bitwise_xor(spot(), partner(k))]


def run(order, damp, total):
    for j in range(GROUP):
        jump = order[j]
        order[j] = total
        total = damp * total + jump
    return total


def total_kernel(far, *refs):
    jumps, damp_ref, out, order = refs[:GROUP], refs[GROUP], refs[GROUP + 1], refs[GROUP + 2]
    sort_in(jumps, order)
    out[...] = run(order, damp_ref[far][:, None], jnp.zeros(out.shape, jnp.float32))


def spread_kernel(far, *refs):
    carry_ref, jumps, damp_ref = refs[0], refs[1 : 1 + GROUP], refs[1 + GROUP]
    outs, order = refs[GROUP + 2 : -1], refs[-1]
    sort_in(jumps, order)
    run(order, damp_ref[far][:, None], jnp.where(lax.axis_index("tm") < GROUP, 0.0, carry_ref[...]))
    sort_out(order, outs)


def finish_kernel(kept, *refs):
    out = refs[-1]
    layers = out.shape[1]
    half = layers // 2
    share = half // GROUP
    first_slice = lax.axis_index("tm") == 0

    def put(side, slot, layer_of):
        layer = slot + side * (layers - 1 - 2 * slot)
        for c in range(3):
            join_rows(out, (c, layer), layer_of[c])

    @pl.when(first_slice)
    def _():
        for side in (0, 1):
            for slot in range(half):
                put(side, slot, load(kept, side, slot))

    @pl.when(jnp.logical_not(first_slice))
    def _():
        for far in (0, 1):
            side = far + (1 - 2 * far) * near_side()
            for k in range(GROUP):
                for j in range(share):
                    put(side, chunk_of(k) * share + j, load(refs[(1 - far) * GROUP + k], j))


def shards(states, rate):
    slices = lax.axis_size("tm")
    slabs = lax.axis_size("gz")
    groups = slices // GROUP
    own = states[0]
    layers, rows, width = own.shape[1:]
    half, share = layers // 2, layers // 2 // GROUP
    tile = (3, 2, rows // 2, width)
    face = f32(3, STAGES, rows, width)
    piece = f32(share, *tile)
    team = lax.axis_index("tm") // GROUP

    def halo(value, pairs):
        return lax.ppermute(value, "gz", [(i, j % slabs) for i, j in pairs])

    def swap(parts):
        return [parts[0]] + [
            lax.ppermute(parts[k], "tm", [(i, i ^ partner(k)) for i in range(slices)])
            for k in range(1, GROUP)
        ]

    def onward(value, distance):
        step = distance * GROUP
        return lax.ppermute(value, "tm", [(i, (i + step) % slices) for i in range(slices)])

    far_face, near_face = call(faces_kernel, [face, face], own)
    near_face = halo(near_face, [(i, i ^ 1) for i in range(slabs)])
    far_face = halo(far_face, [(i, i + 1 if i % 2 else i - 1 + slabs) for i in range(slabs)])
    edges, middle, faded, damp, kept = call(
        inside_kernel,
        [
            f32(STAGES, 2, 3, *tile),
            f32(2, half - STAGES, *tile),
            f32(2, STAGES, *tile),
            f32(2, share, *tile[1:]),
            f32(2, half, *tile),
        ],
        own, rate,
        scratch=[pltpu.VMEM((2, half, *tile[1:]), jnp.float32)]
        + [pltpu.VMEM((layers, *tile), jnp.float32)] * 3,
        flops=1 << 26,
    )
    strip = pltpu.VMEM((STAGES + 1, STAGES, *tile), jnp.float32)
    order = pltpu.VMEM((GROUP, *piece.shape), jnp.float32)

    def after(value, earlier):
        return lax.optimization_barrier((value, earlier))[0]

    halves = []
    for far, face_ref in enumerate((near_face, far_face)):
        jumps = call(
            functools.partial(jumps_kernel, far), [piece] * GROUP, face_ref, edges, middle, faded,
            scratch=[strip, pltpu.VMEM((half, *tile), jnp.float32)],
            flops=1 << 32,
        )
        halves.append(swap(jumps))

    carries, total = [], None
    for far, jumps in enumerate(halves):
        if far:
            jumps[0] = after(jumps[0], total)
        total = call(
            functools.partial(total_kernel, far), piece, *jumps, damp, scratch=[order]
        )
        carry = onward(total, 1)
        if groups > 2:
            carry = jnp.where(team < 1, 0.0, carry)
            fade, distance = damp[far][:, None] ** GROUP, 1
            while distance < groups - 1:
                carry = carry + jnp.where(team < distance, 0.0, fade * onward(carry, distance))
                distance, fade = 2 * distance, fade * fade
        carries.append(carry)

    pieces, news = [], None
    for far, (jumps, carry) in enumerate(zip(halves, carries)):
        if far:
            jumps[0] = after(jumps[0], news[0])
        news = call(
            functools.partial(spread_kernel, far), [piece] * GROUP, carry, *jumps, damp,
            scratch=[order],
            flops=1 << 32,
        )
        pieces = swap(news) + pieces
    updated = call(finish_kernel, f32(*own.shape), kept, *pieces)
    return updated[None]


def solution(mesh):
    return jax.shard_map(
        shards,
        mesh=mesh,
        in_specs=(P("tm", None, "gz", None, None), P("gz", None, None)),
        out_specs=P("tm", None, "gz", None, None),
        check_vma=False,
    )
```

```python
import functools

import jax
import jax.numpy as jnp
from jax import lax
from jax.experimental import pallas as pl
from jax.experimental.pallas import tpu as pltpu
from jax.sharding import PartitionSpec as P

STEPS = 2
STAGES = 3 * STEPS
BUSY = 1 << 32
GROUP = 4
VISCOSITY = 0.05
TIME_STEP = 0.2
MIX = ((1.0, None), (0.25, 0.75), (2.0 / 3.0, 1.0 / 3.0))
VMEM = pl.BlockSpec(memory_space=pltpu.VMEM)
ANY = pl.BlockSpec(memory_space=pl.ANY)
PARAMS = pltpu.CompilerParams(vmem_limit_bytes=16 * 1024 * 1024)


def call(kernel, out_shape, *args, scratch=(), flops=None):
    cost = None
    if flops is not None:
        cost = pl.CostEstimate(flops=flops, bytes_accessed=1 << 20, transcendentals=0)
    return pl.pallas_call(
        kernel,
        out_shape=out_shape,
        in_specs=[VMEM] * len(args),
        out_specs=jax.tree.map(lambda _: VMEM, out_shape),
        scratch_shapes=list(scratch),
        compiler_params=PARAMS,
        cost_estimate=cost,
    )(*args)


def f32(*shape):
    return jax.ShapeDtypeStruct(shape, jnp.float32)


def partner(k):
    return (GROUP - k) % GROUP


def spot():
    return lax.rem(lax.axis_index("tm"), GROUP)


def chunk_of(k):
    return lax.bitwise_xor(spot(), partner(k))


def share_of(ref, k, count):
    chunk = chunk_of(k)
    return ref[chunk // 2, pl.ds(lax.rem(chunk, 2) * count, count)]


def near_side():
    return 1 - lax.rem(lax.axis_index("gz"), 2)


def split_rows(ref, *lead):
    half = ref.shape[-2] // 2
    return [ref[(*lead, pl.ds(odd, half, stride=2), slice(None))] for odd in (0, 1)]


def join_rows(ref, lead, pair):
    half = ref.shape[-2] // 2
    for odd in (0, 1):
        ref[(*lead, pl.ds(odd, half, stride=2), slice(None))] = pair[odd]


def load(ref, *lead):
    return [[ref[(*lead, c, odd)] for odd in (0, 1)] for c in range(3)]


def store(ref, lead, value):
    for c in range(3):
        for odd in (0, 1):
            ref[(*lead, c, odd)] = value[c][odd]


def advance(last, here, ahead, alpha, upward=1.0):
    diffuse = alpha * TIME_STEP * VISCOSITY
    carry = alpha * TIME_STEP * 0.5
    result = [[None, None] for _ in range(3)]
    for odd in (0, 1):
        speed = [here[0][odd] * carry, here[1][odd] * carry, here[2][odd] * (carry * upward)]
        to_next = [diffuse - s for s in speed]
        to_last = [diffuse + s for s in speed]
        for c in range(3):
            w = here[c][odd]
            rows, width = w.shape
            other = here[c][1 - odd]
            if odd:
                y_next, y_last = pltpu.roll(other, rows - 1, 0), other
            else:
                y_next, y_last = other, pltpu.roll(other, 1, 0)
            total = (alpha - 6.0 * diffuse) * w
            total = total + (
                to_next[0] * pltpu.roll(w, width - 1, 1) + to_last[0] * pltpu.roll(w, 1, 1)
            )
            total = total + (to_next[1] * y_next + to_last[1] * y_last)
            total = total + (to_next[2] * ahead[c][odd] + to_last[2] * last[c][odd])
            result[c][odd] = total
    return result


def blend(new, beta, base):
    return [[new[c][odd] + beta * base[c][odd] for odd in (0, 1)] for c in range(3)]


def faces_kernel(own_ref, far_ref, near_ref):
    layers, width = own_ref.shape[1], near_ref.shape[1]
    near = near_side()
    top = layers - width
    far_ref[...] = own_ref[:, pl.ds((1 - near) * top, width)]
    near_ref[...] = own_ref[:, pl.ds(near * top, width)]


def inside_kernel(own_ref, rate_ref, edges, middle, faded, early_damp, late_damp, kept, damps, inner, *fields):
    layers = own_ref.shape[1]
    near = near_side()
    slices = lax.axis_size("tm")
    keep = (lax.axis_index("tm") != 0).astype(jnp.float32)

    def side_of(z):
        return (0, z) if z < layers - 1 - z else (1, layers - 1 - z)

    def from_near(z):
        return z - STAGES + near * (layers - 1 - 2 * z)

    def save(stage, z, value):
        low, high = z - stage, layers - 1 - stage - z
        if low < 3:
            store(edges, (stage, 0, low), value)
        if high < 3:
            store(edges, (stage, 1, high), value)

    for z in range(layers):
        side, slot = side_of(z)
        damp = [jnp.exp(r * (-1.0 / slices)) for r in split_rows(rate_ref, z)]
        start = [split_rows(own_ref, c, z) for c in range(3)]
        store(fields[0], (z,), start)
        store(kept, (z,), start)
        save(0, z, start)
        lost = [[damp[odd] * keep * start[c][odd] for odd in (0, 1)] for c in range(3)]
        if slot < STAGES:
            store(faded, (side, slot), lost)
            for odd in (0, 1):
                damps[side, odd, slot] = damp[odd]
        else:
            store(middle, (from_near(z),), lost)
            for odd in (0, 1):
                inner[odd, STAGES + from_near(z)] = damp[odd]

    for stage in range(1, STAGES + 1):
        kind = (stage - 1) % 3
        alpha, beta = MIX[kind]
        source, target = fields[kind], fields[(kind + 1) % 3]
        below, here = load(source, stage - 1), load(source, stage)
        for z in range(stage, layers - stage):
            above = load(source, z + 1)
            new = advance(below, here, above, alpha)
            if beta is not None:
                new = blend(new, beta, load(fields[0], z))
            if stage < STAGES:
                store(target, (z,), new)
                save(stage, z, new)
            else:
                lost = load(middle, from_near(z))
                store(
                    middle,
                    (from_near(z),),
                    [[new[c][odd] - lost[c][odd] for odd in (0, 1)] for c in range(3)],
                )
            below, here = here, above

    for odd in (0, 1):
        inner[odd, :STAGES] = damps[near, odd]
    early_damp[...] = share_of(inner, 0, early_damp.shape[0])
    late_damp[...] = share_of(damps.at[1 - near], 0, late_damp.shape[0])


def border(side, face_ref, edges, middle, faded, jumps, strip):
    width = STAGES
    upward = 1.0 - 2.0 * side.astype(jnp.float32)
    for slot in range(width):
        layer = slot + side * (width - 1 - 2 * slot)
        store(strip, (0, slot), [split_rows(face_ref, c, layer) for c in range(3)])

    def at(stage, slot):
        if slot < width:
            return load(strip, stage, slot)
        return load(edges, stage, side, slot - width)

    def step(turn, _):
        for kind, (alpha, beta) in enumerate(MIX):
            stage = 3 * turn + kind
            last, here = at(stage, 0), at(stage, 1)
            for slot in range(width):
                ahead = at(stage, slot + 2)
                new = advance(last, here, ahead, alpha, upward)
                if beta is not None:
                    new = blend(new, beta, at(3 * turn, slot + 1 + kind))
                store(strip, (stage + 1, slot), new)
                last, here = here, ahead
        return 0

    lax.fori_loop(0, STEPS, step, 0)
    for slot in range(jumps.shape[1]):
        if slot < width:
            end, lost = load(strip, STAGES, slot), load(faded, side, slot)
            jump = [[end[c][odd] - lost[c][odd] for odd in (0, 1)] for c in range(3)]
        else:
            jump = load(middle, slot - width)
        for odd in (0, 1):
            for c in range(3):
                jumps[odd, slot, c] = jump[c][odd]


def jumps_kernel(far, face_ref, edges, middle, faded, *refs):
    outs, strip, jumps = refs[:GROUP], refs[-2], refs[-1]
    side = far + (1 - 2 * far) * near_side()
    border(side, face_ref, edges, middle, faded, jumps, strip)
    for k, out in enumerate(outs):
        out[...] = share_of(jumps, k, out.shape[0])


def sort_in(jumps, order):
    for k in range(GROUP):
        order[lax.bitwise_xor(spot(), partner(k))] = jumps[k][...]


def sort_out(order, outs):
    for k in range(GROUP):
        outs[k][...] = order[lax.bitwise_xor(spot(), partner(k))]


def run(order, damp, total):
    for j in range(GROUP):
        jump = order[j]
        order[j] = total
        total = damp * total + jump
    return total


def total_kernel(*refs):
    jumps, damp_ref, out, order = refs[:GROUP], refs[GROUP], refs[GROUP + 1], refs[GROUP + 2]
    sort_in(jumps, order)
    out[...] = run(order, damp_ref[...][:, None], jnp.zeros(out.shape, jnp.float32))


def spread_kernel(*refs):
    carry_ref, jumps, damp_ref = refs[0], refs[1 : 1 + GROUP], refs[1 + GROUP]
    outs, order = refs[GROUP + 2 : -1], refs[-1]
    sort_in(jumps, order)
    run(order, damp_ref[...][:, None], jnp.where(lax.axis_index("tm") < GROUP, 0.0, carry_ref[...]))
    sort_out(order, outs)


def finish_kernel(far, kept, *refs):
    pieces, (out, part, sem) = refs[:GROUP], refs[-3:]
    layers, count = out.shape[1], part.shape[1]
    rows = out.shape[2] // 2
    down = far + (1 - 2 * far) * near_side()
    base = down * (layers - count)
    first_slice = lax.axis_index("tm") == 0

    @pl.when(first_slice)
    def _():
        for layer in range(count):
            pair = load(kept, base + layer)
            for c in range(3):
                join_rows(part, (c, layer), pair[c])

    @pl.when(jnp.logical_not(first_slice))
    def _():
        for k, piece in enumerate(pieces):
            chunk, share = chunk_of(k), piece.shape[0]
            for odd in (0, 1):

                @pl.when(chunk // 2 == odd)
                def _():
                    for j in range(share):
                        slot = lax.rem(chunk, 2) * share + j
                        layer = slot + down * (count - 1 - 2 * slot)
                        for c in range(3):
                            part[c, layer, pl.ds(odd, rows, stride=2), :] = piece[j, c]

    copy = pltpu.make_async_copy(part, out.at[:, pl.ds(base, count)], sem)
    copy.start()
    copy.wait()


def shards(states, rate):
    slices = lax.axis_size("tm")
    slabs = lax.axis_size("gz")
    groups = slices // GROUP
    own = states[0]
    layers, rows, width = own.shape[1:]
    middle_layers = layers - 2 * STAGES
    tile = (3, 2, rows // 2, width)
    face = f32(3, STAGES, rows, width)
    sizes = ((layers - STAGES) // 2, STAGES // 2)
    team = lax.axis_index("tm") // GROUP

    def halo(value, pairs):
        return lax.ppermute(value, "gz", [(i, j % slabs) for i, j in pairs])

    def swap(parts):
        return [parts[0]] + [
            lax.ppermute(parts[k], "tm", [(i, i ^ partner(k)) for i in range(slices)])
            for k in range(1, GROUP)
        ]

    def onward(value, distance):
        step = distance * GROUP
        return lax.ppermute(value, "tm", [(i, (i + step) % slices) for i in range(slices)])

    far_face, near_face = call(faces_kernel, [face, face], own)
    near_face = halo(near_face, [(i, i ^ 1) for i in range(slabs)])
    far_face = halo(far_face, [(i, i + 1 if i % 2 else i - 1 + slabs) for i in range(slabs)])
    row = (rows // 2, width)
    edges, middle, faded, *damps, kept = call(
        inside_kernel,
        [
            f32(STAGES, 2, 3, *tile),
            f32(middle_layers, *tile),
            f32(2, STAGES, *tile),
            *[f32(size, *row) for size in sizes],
            f32(layers, *tile),
        ],
        own, rate,
        scratch=[
            pltpu.VMEM((2, 2, STAGES, *row), jnp.float32),
            pltpu.VMEM((2, layers - STAGES, *row), jnp.float32),
        ]
        + [pltpu.VMEM((layers, *tile), jnp.float32)] * 3,
        flops=1 << 26,
    )
    strip = pltpu.VMEM((STAGES + 1, STAGES, *tile), jnp.float32)
    shares = [f32(size, 3, *row) for size in sizes]
    orders = [pltpu.VMEM((GROUP, *share.shape), jnp.float32) for share in shares]

    def after(value, earlier):
        return lax.optimization_barrier((value, earlier))[0]

    halves = []
    for far, face_ref in enumerate((near_face, far_face)):
        jumps = call(
            functools.partial(jumps_kernel, far), [shares[far]] * GROUP,
            face_ref, edges, middle, faded,
            scratch=[strip, pltpu.VMEM((2, 2 * sizes[far], 3, *row), jnp.float32)],
            flops=BUSY,
        )
        halves.append(swap(jumps))

    carries, total = [], halves[1][0]
    for far, jumps in enumerate(halves):
        jumps[0] = after(jumps[0], total)
        total = call(
            total_kernel, shares[far], *jumps, damps[far], scratch=[orders[far]], flops=BUSY
        )
        carry = onward(total, 1)
        if groups > 2:
            carry = jnp.where(team < 1, 0.0, carry)
            fade, distance = damps[far][:, None] ** GROUP, 1
            while distance < groups - 1:
                carry = carry + jnp.where(team < distance, 0.0, fade * onward(carry, distance))
                distance, fade = 2 * distance, fade * fade
        carries.append(carry)

    updated, news = None, None
    for far, (jumps, carry) in enumerate(zip(halves, carries)):
        if far:
            jumps[0] = after(jumps[0], news[0])
        news = call(
            spread_kernel, [shares[far]] * GROUP, carry, *jumps, damps[far],
            scratch=[orders[far]],
            flops=BUSY,
        )
        halves[far] = swap(news)
    for far, pieces in enumerate(halves):
        args = [kept, *pieces] + ([updated] if far else [])
        updated = pl.pallas_call(
            functools.partial(finish_kernel, far),
            out_shape=f32(*own.shape),
            in_specs=[VMEM] * (1 + GROUP) + [ANY] * far,
            out_specs=ANY,
            scratch_shapes=[
                pltpu.VMEM((3, 2 * sizes[far], rows, width), jnp.float32),
                pltpu.SemaphoreType.DMA,
            ],
            input_output_aliases={1 + GROUP: 0} if far else {},
            compiler_params=PARAMS,
            cost_estimate=pl.CostEstimate(flops=BUSY, bytes_accessed=1 << 20, transcendentals=0),
        )(*args)
    return updated[None]


def solution(mesh):
    return jax.shard_map(
        shards,
        mesh=mesh,
        in_specs=(P("tm", None, "gz", None, None), P("gz", None, None)),
        out_specs=P("tm", None, "gz", None, None),
        check_vma=False,
    )
```

```python
import functools

import jax
import jax.numpy as jnp
from jax import lax
from jax.experimental import pallas as pl
from jax.experimental.pallas import tpu as pltpu
from jax.sharding import PartitionSpec as P

STEPS = 2
STAGES = 3 * STEPS
BUSY = 1 << 32
GROUP = 4
VISCOSITY = 0.05
TIME_STEP = 0.2
MIX = ((1.0, None), (0.25, 0.75), (2.0 / 3.0, 1.0 / 3.0))
VMEM = pl.BlockSpec(memory_space=pltpu.VMEM)
ANY = pl.BlockSpec(memory_space=pl.ANY)
PARAMS = pltpu.CompilerParams(vmem_limit_bytes=16 * 1024 * 1024)


def call(kernel, out_shape, *args, scratch=(), flops=None):
    cost = None
    if flops is not None:
        cost = pl.CostEstimate(flops=flops, bytes_accessed=1 << 20, transcendentals=0)
    return pl.pallas_call(
        kernel,
        out_shape=out_shape,
        in_specs=[VMEM] * len(args),
        out_specs=jax.tree.map(lambda _: VMEM, out_shape),
        scratch_shapes=list(scratch),
        compiler_params=PARAMS,
        cost_estimate=cost,
    )(*args)


def f32(*shape):
    return jax.ShapeDtypeStruct(shape, jnp.float32)


def partner(k):
    return (GROUP - k) % GROUP


def spot():
    return lax.rem(lax.axis_index("tm"), GROUP)


def chunk_of(k):
    return lax.bitwise_xor(spot(), partner(k))


def share_of(ref, k, count):
    chunk = chunk_of(k)
    return ref[chunk // 2, pl.ds(lax.rem(chunk, 2) * count, count)]


def near_side():
    return 1 - lax.rem(lax.axis_index("gz"), 2)


def split_rows(ref, *lead):
    half = ref.shape[-2] // 2
    return [ref[(*lead, pl.ds(odd, half, stride=2), slice(None))] for odd in (0, 1)]


def join_rows(ref, lead, pair):
    half = ref.shape[-2] // 2
    for odd in (0, 1):
        ref[(*lead, pl.ds(odd, half, stride=2), slice(None))] = pair[odd]


def load(ref, *lead):
    return [[ref[(*lead, c, odd)] for odd in (0, 1)] for c in range(3)]


def store(ref, lead, value):
    for c in range(3):
        for odd in (0, 1):
            ref[(*lead, c, odd)] = value[c][odd]


def advance(last, here, ahead, alpha, upward=1.0):
    diffuse = alpha * TIME_STEP * VISCOSITY
    carry = alpha * TIME_STEP * 0.5
    result = [[None, None] for _ in range(3)]
    for odd in (0, 1):
        speed = [here[0][odd] * carry, here[1][odd] * carry, here[2][odd] * (carry * upward)]
        to_next = [diffuse - s for s in speed]
        to_last = [diffuse + s for s in speed]
        for c in range(3):
            w = here[c][odd]
            rows, width = w.shape
            other = here[c][1 - odd]
            if odd:
                y_next, y_last = pltpu.roll(other, rows - 1, 0), other
            else:
                y_next, y_last = other, pltpu.roll(other, 1, 0)
            total = (alpha - 6.0 * diffuse) * w
            total = total + (
                to_next[0] * pltpu.roll(w, width - 1, 1) + to_last[0] * pltpu.roll(w, 1, 1)
            )
            total = total + (to_next[1] * y_next + to_last[1] * y_last)
            total = total + (to_next[2] * ahead[c][odd] + to_last[2] * last[c][odd])
            result[c][odd] = total
    return result


def blend(new, beta, base):
    return [[new[c][odd] + beta * base[c][odd] for odd in (0, 1)] for c in range(3)]


def faces_kernel(own_ref, far_ref, near_ref):
    layers, width = own_ref.shape[1], near_ref.shape[1]
    near = near_side()
    top = layers - width
    far_ref[...] = own_ref[:, pl.ds((1 - near) * top, width)]
    near_ref[...] = own_ref[:, pl.ds(near * top, width)]


def inside_kernel(own_ref, rate_ref, edges, middle, faded, early_damp, late_damp, kept, damps, inner, *fields):
    layers = own_ref.shape[1]
    near = near_side()
    slices = lax.axis_size("tm")
    keep = (lax.axis_index("tm") != 0).astype(jnp.float32)

    def side_of(z):
        return (0, z) if z < layers - 1 - z else (1, layers - 1 - z)

    def from_near(z):
        return z - STAGES + near * (layers - 1 - 2 * z)

    def save(stage, z, value):
        low, high = z - stage, layers - 1 - stage - z
        if low < 3:
            store(edges, (stage, 0, low), value)
        if high < 3:
            store(edges, (stage, 1, high), value)

    for z in range(layers):
        side, slot = side_of(z)
        damp = [jnp.exp(r * (-1.0 / slices)) for r in split_rows(rate_ref, z)]
        start = [split_rows(own_ref, c, z) for c in range(3)]
        store(fields[0], (z,), start)
        store(kept, (z,), start)
        save(0, z, start)
        lost = [[damp[odd] * keep * start[c][odd] for odd in (0, 1)] for c in range(3)]
        if slot < STAGES:
            store(faded, (side, slot), lost)
            for odd in (0, 1):
                damps[side, odd, slot] = damp[odd]
        else:
            store(middle, (from_near(z),), lost)
            for odd in (0, 1):
                inner[odd, STAGES + from_near(z)] = damp[odd]

    for stage in range(1, STAGES + 1):
        kind = (stage - 1) % 3
        alpha, beta = MIX[kind]
        source, target = fields[kind], fields[(kind + 1) % 3]
        below, here = load(source, stage - 1), load(source, stage)
        for z in range(stage, layers - stage):
            above = load(source, z + 1)
            new = advance(below, here, above, alpha)
            if beta is not None:
                new = blend(new, beta, load(fields[0], z))
            if stage < STAGES:
                store(target, (z,), new)
                save(stage, z, new)
            else:
                lost = load(middle, from_near(z))
                store(
                    middle,
                    (from_near(z),),
                    [[new[c][odd] - lost[c][odd] for odd in (0, 1)] for c in range(3)],
                )
            below, here = here, above

    for odd in (0, 1):
        inner[odd, :STAGES] = damps[near, odd]
    early_damp[...] = share_of(inner, 0, early_damp.shape[0])
    late_damp[...] = share_of(damps.at[1 - near], 0, late_damp.shape[0])


def border(side, face_ref, edges, middle, faded, jumps, strip):
    width = STAGES
    upward = 1.0 - 2.0 * side.astype(jnp.float32)
    for slot in range(width):
        layer = slot + side * (width - 1 - 2 * slot)
        store(strip, (0, slot), [split_rows(face_ref, c, layer) for c in range(3)])

    def at(stage, slot):
        if slot < width:
            return load(strip, stage, slot)
        return load(edges, stage, side, slot - width)

    def step(turn, _):
        for kind, (alpha, beta) in enumerate(MIX):
            stage = 3 * turn + kind
            last, here = at(stage, 0), at(stage, 1)
            for slot in range(width):
                ahead = at(stage, slot + 2)
                new = advance(last, here, ahead, alpha, upward)
                if beta is not None:
                    new = blend(new, beta, at(3 * turn, slot + 1 + kind))
                store(strip, (stage + 1, slot), new)
                last, here = here, ahead
        return 0

    lax.fori_loop(0, STEPS, step, 0)
    for slot in range(jumps.shape[1]):
        if slot < width:
            end, lost = load(strip, STAGES, slot), load(faded, side, slot)
            jump = [[end[c][odd] - lost[c][odd] for odd in (0, 1)] for c in range(3)]
        else:
            jump = load(middle, slot - width)
        for odd in (0, 1):
            for c in range(3):
                jumps[odd, slot, c] = jump[c][odd]


def jumps_kernel(far, face_ref, edges, middle, faded, *refs):
    outs, strip, jumps = refs[:GROUP], refs[-2], refs[-1]
    side = far + (1 - 2 * far) * near_side()
    border(side, face_ref, edges, middle, faded, jumps, strip)
    for k, out in enumerate(outs):
        out[...] = share_of(jumps, k, out.shape[0])


def sort_in(jumps, order):
    for k in range(GROUP):
        order[lax.bitwise_xor(spot(), partner(k))] = jumps[k][...]


def sort_out(order, outs):
    for k in range(GROUP):
        outs[k][...] = order[lax.bitwise_xor(spot(), partner(k))]


def run(order, damp, total):
    for j in range(GROUP):
        jump = order[j]
        order[j] = total
        total = damp * total + jump
    return total


def total_kernel(*refs):
    jumps, damp_ref, out, order = refs[:GROUP], refs[GROUP], refs[GROUP + 1], refs[GROUP + 2]
    sort_in(jumps, order)
    out[...] = run(order, damp_ref[...][:, None], jnp.zeros(out.shape, jnp.float32))


def spread_kernel(*refs):
    carry_ref, jumps, damp_ref = refs[0], refs[1 : 1 + GROUP], refs[1 + GROUP]
    outs, order = refs[GROUP + 2 : -1], refs[-1]
    sort_in(jumps, order)
    run(order, damp_ref[...][:, None], jnp.where(lax.axis_index("tm") < GROUP, 0.0, carry_ref[...]))
    sort_out(order, outs)


def finish_kernel(far, kept, *refs):
    pieces, (out, part, sem) = refs[:GROUP], refs[-3:]
    layers, rows = out.shape[1], out.shape[2] // 2
    share = pieces[0].shape[0]
    count = 2 * share
    down = far + (1 - 2 * far) * near_side()
    first_slice = lax.axis_index("tm") == 0

    def write(base, count):
        copy = pltpu.make_async_copy(part.at[:, pl.ds(0, count)], out.at[:, pl.ds(base, count)], sem)
        copy.start()
        copy.wait()

    if not far:

        @pl.when(first_slice)
        def _():
            for layer in range(layers):
                pair = load(kept, layer)
                for c in range(3):
                    join_rows(part, (c, layer), pair[c])
            write(0, layers)

    @pl.when(jnp.logical_not(first_slice))
    def _():
        for k, piece in enumerate(pieces):
            chunk = chunk_of(k)
            for odd in (0, 1):

                @pl.when(chunk // 2 == odd)
                def _():
                    for j in range(share):
                        slot = lax.rem(chunk, 2) * share + j
                        layer = slot + down * (count - 1 - 2 * slot)
                        for c in range(3):
                            part[c, layer, pl.ds(odd, rows, stride=2), :] = piece[j, c]
        write(down * (layers - count), count)


def shards(states, rate):
    slices = lax.axis_size("tm")
    slabs = lax.axis_size("gz")
    groups = slices // GROUP
    own = states[0]
    layers, rows, width = own.shape[1:]
    middle_layers = layers - 2 * STAGES
    tile = (3, 2, rows // 2, width)
    face = f32(3, STAGES, rows, width)
    sizes = ((layers - STAGES) // 2, STAGES // 2)
    team = lax.axis_index("tm") // GROUP

    def halo(value, pairs):
        return lax.ppermute(value, "gz", [(i, j % slabs) for i, j in pairs])

    def swap(parts):
        return [parts[0]] + [
            lax.ppermute(parts[k], "tm", [(i, i ^ partner(k)) for i in range(slices)])
            for k in range(1, GROUP)
        ]

    def onward(value, distance):
        step = distance * GROUP
        return lax.ppermute(value, "tm", [(i, (i + step) % slices) for i in range(slices)])

    far_face, near_face = call(faces_kernel, [face, face], own)
    near_face = halo(near_face, [(i, i ^ 1) for i in range(slabs)])
    far_face = halo(far_face, [(i, i + 1 if i % 2 else i - 1 + slabs) for i in range(slabs)])
    row = (rows // 2, width)
    edges, middle, faded, *damps, kept = call(
        inside_kernel,
        [
            f32(STAGES, 2, 3, *tile),
            f32(middle_layers, *tile),
            f32(2, STAGES, *tile),
            *[f32(size, *row) for size in sizes],
            f32(layers, *tile),
        ],
        own, rate,
        scratch=[
            pltpu.VMEM((2, 2, STAGES, *row), jnp.float32),
            pltpu.VMEM((2, layers - STAGES, *row), jnp.float32),
        ]
        + [pltpu.VMEM((layers, *tile), jnp.float32)] * 3,
        flops=1 << 26,
    )
    strip = pltpu.VMEM((STAGES + 1, STAGES, *tile), jnp.float32)
    shares = [f32(size, 3, *row) for size in sizes]
    orders = [pltpu.VMEM((GROUP, *share.shape), jnp.float32) for share in shares]

    def after(value, earlier):
        return lax.optimization_barrier((value, earlier))[0]

    halves = []
    for far, face_ref in enumerate((near_face, far_face)):
        jumps = call(
            functools.partial(jumps_kernel, far), [shares[far]] * GROUP,
            face_ref, edges, middle, faded,
            scratch=[strip, pltpu.VMEM((2, 2 * sizes[far], 3, *row), jnp.float32)],
            flops=BUSY,
        )
        halves.append(swap(jumps))

    carries, total = [], halves[1][0]
    for far, jumps in enumerate(halves):
        jumps[0] = after(jumps[0], total)
        total = call(
            total_kernel, shares[far], *jumps, damps[far], scratch=[orders[far]], flops=BUSY
        )
        carry = onward(total, 1)
        if groups > 2:
            carry = jnp.where(team < 1, 0.0, carry)
            fade, distance = damps[far][:, None] ** GROUP, 1
            while distance < groups - 1:
                carry = carry + jnp.where(team < distance, 0.0, fade * onward(carry, distance))
                distance, fade = 2 * distance, fade * fade
        carries.append(carry)

    updated, news = None, None
    for far, (jumps, carry) in enumerate(zip(halves, carries)):
        if far:
            jumps[0] = after(jumps[0], news[0])
        news = call(
            spread_kernel, [shares[far]] * GROUP, carry, *jumps, damps[far],
            scratch=[orders[far]],
            flops=BUSY,
        )
        halves[far] = swap(news)
    for far, pieces in enumerate(halves):
        args = [kept, *pieces] + ([updated] if far else [])
        updated = pl.pallas_call(
            functools.partial(finish_kernel, far),
            out_shape=f32(*own.shape),
            in_specs=[VMEM] * (1 + GROUP) + [ANY] * far,
            out_specs=ANY,
            scratch_shapes=[
                pltpu.VMEM((3, 2 * sizes[far] if far else layers, rows, width), jnp.float32),
                pltpu.SemaphoreType.DMA,
            ],
            input_output_aliases={1 + GROUP: 0} if far else {},
            compiler_params=PARAMS,
            cost_estimate=pl.CostEstimate(flops=BUSY, bytes_accessed=1 << 20, transcendentals=0),
        )(*args)
    return updated[None]


def solution(mesh):
    return jax.shard_map(
        shards,
        mesh=mesh,
        in_specs=(P("tm", None, "gz", None, None), P("gz", None, None)),
        out_specs=P("tm", None, "gz", None, None),
        check_vma=False,
    )
```

```python
import functools

import jax
import jax.numpy as jnp
from jax import lax
from jax.experimental import pallas as pl
from jax.experimental.pallas import tpu as pltpu
from jax.sharding import PartitionSpec as P

STEPS = 2
STAGES = 3 * STEPS
BUSY = 1 << 32
GROUP = 4
VISCOSITY = 0.05
TIME_STEP = 0.2
MIX = ((1.0, None), (0.25, 0.75), (2.0 / 3.0, 1.0 / 3.0))
VMEM = pl.BlockSpec(memory_space=pltpu.VMEM)
ANY = pl.BlockSpec(memory_space=pl.ANY)
PARAMS = pltpu.CompilerParams(vmem_limit_bytes=16 * 1024 * 1024)


def call(kernel, out_shape, *args, scratch=(), flops=None):
    cost = None
    if flops is not None:
        cost = pl.CostEstimate(flops=flops, bytes_accessed=1 << 20, transcendentals=0)
    return pl.pallas_call(
        kernel,
        out_shape=out_shape,
        in_specs=[VMEM] * len(args),
        out_specs=jax.tree.map(lambda _: VMEM, out_shape),
        scratch_shapes=list(scratch),
        compiler_params=PARAMS,
        cost_estimate=cost,
    )(*args)


def f32(*shape):
    return jax.ShapeDtypeStruct(shape, jnp.float32)


def partner(k):
    return (GROUP - k) % GROUP


def spot():
    return lax.rem(lax.axis_index("tm"), GROUP)


def chunk_of(k):
    return lax.bitwise_xor(spot(), partner(k))


def share_of(ref, k, count):
    chunk = chunk_of(k)
    return ref[chunk // 2, pl.ds(lax.rem(chunk, 2) * count, count)]


def near_side():
    return 1 - lax.rem(lax.axis_index("gz"), 2)


def split_rows(ref, *lead):
    half = ref.shape[-2] // 2
    return [ref[(*lead, pl.ds(odd, half, stride=2), slice(None))] for odd in (0, 1)]


def join_rows(ref, lead, pair):
    half = ref.shape[-2] // 2
    for odd in (0, 1):
        ref[(*lead, pl.ds(odd, half, stride=2), slice(None))] = pair[odd]


def load(ref, *lead):
    return [[ref[(*lead, c, odd)] for odd in (0, 1)] for c in range(3)]


def store(ref, lead, value):
    for c in range(3):
        for odd in (0, 1):
            ref[(*lead, c, odd)] = value[c][odd]


def advance(last, here, ahead, alpha, upward=1.0):
    diffuse = alpha * TIME_STEP * VISCOSITY
    carry = alpha * TIME_STEP * 0.5
    result = [[None, None] for _ in range(3)]
    for odd in (0, 1):
        speed = [here[0][odd] * carry, here[1][odd] * carry, here[2][odd] * (carry * upward)]
        to_next = [diffuse - s for s in speed]
        to_last = [diffuse + s for s in speed]
        for c in range(3):
            w = here[c][odd]
            rows, width = w.shape
            other = here[c][1 - odd]
            if odd:
                y_next, y_last = pltpu.roll(other, rows - 1, 0), other
            else:
                y_next, y_last = other, pltpu.roll(other, 1, 0)
            total = (alpha - 6.0 * diffuse) * w
            total = total + (
                to_next[0] * pltpu.roll(w, width - 1, 1) + to_last[0] * pltpu.roll(w, 1, 1)
            )
            total = total + (to_next[1] * y_next + to_last[1] * y_last)
            total = total + (to_next[2] * ahead[c][odd] + to_last[2] * last[c][odd])
            result[c][odd] = total
    return result


def blend(new, beta, base):
    return [[new[c][odd] + beta * base[c][odd] for odd in (0, 1)] for c in range(3)]


def faces_kernel(own_ref, far_ref, near_ref):
    layers, width = own_ref.shape[1], near_ref.shape[1]
    near = near_side()
    top = layers - width
    far_ref[...] = own_ref[:, pl.ds((1 - near) * top, width)]
    near_ref[...] = own_ref[:, pl.ds(near * top, width)]


def inside_kernel(own_ref, rate_ref, edges, middle, faded, damp_ref, kept, damps, inner, *fields):
    layers = own_ref.shape[1]
    near = near_side()
    slices = lax.axis_size("tm")
    keep = (lax.axis_index("tm") != 0).astype(jnp.float32)

    def side_of(z):
        return (0, z) if z < layers - 1 - z else (1, layers - 1 - z)

    def from_near(z):
        return z - STAGES + near * (layers - 1 - 2 * z)

    def save(stage, z, value):
        low, high = z - stage, layers - 1 - stage - z
        if low < 3:
            store(edges, (stage, 0, low), value)
        if high < 3:
            store(edges, (stage, 1, high), value)

    for z in range(layers):
        side, slot = side_of(z)
        damp = [jnp.exp(r * (-1.0 / slices)) for r in split_rows(rate_ref, z)]
        start = [split_rows(own_ref, c, z) for c in range(3)]
        store(fields[0], (z,), start)
        store(kept, (z,), start)
        save(0, z, start)
        lost = [[damp[odd] * keep * start[c][odd] for odd in (0, 1)] for c in range(3)]
        if slot < STAGES:
            store(faded, (side, slot), lost)
            for odd in (0, 1):
                damps[side, odd, slot] = damp[odd]
        else:
            store(middle, (from_near(z),), lost)
            for odd in (0, 1):
                inner[odd, STAGES + from_near(z)] = damp[odd]

    for stage in range(1, STAGES + 1):
        kind = (stage - 1) % 3
        alpha, beta = MIX[kind]
        source, target = fields[kind], fields[(kind + 1) % 3]
        below, here = load(source, stage - 1), load(source, stage)
        for z in range(stage, layers - stage):
            above = load(source, z + 1)
            new = advance(below, here, above, alpha)
            if beta is not None:
                new = blend(new, beta, load(fields[0], z))
            if stage < STAGES:
                store(target, (z,), new)
                save(stage, z, new)
            else:
                lost = load(middle, from_near(z))
                store(
                    middle,
                    (from_near(z),),
                    [[new[c][odd] - lost[c][odd] for odd in (0, 1)] for c in range(3)],
                )
            below, here = here, above

    for odd in (0, 1):
        inner[odd, :STAGES] = damps[near, odd]
    early, late = inner.shape[1] // 2, STAGES // 2
    damp_ref[:early] = share_of(inner, 0, early)
    damp_ref[early:] = share_of(damps.at[1 - near], 0, late)


def border(side, face_ref, edges, middle, faded, jumps, strip):
    width = STAGES
    upward = 1.0 - 2.0 * side.astype(jnp.float32)
    for slot in range(width):
        layer = slot + side * (width - 1 - 2 * slot)
        store(strip, (0, slot), [split_rows(face_ref, c, layer) for c in range(3)])

    def at(stage, slot):
        if slot < width:
            return load(strip, stage, slot)
        return load(edges, stage, side, slot - width)

    def step(turn, _):
        for kind, (alpha, beta) in enumerate(MIX):
            stage = 3 * turn + kind
            last, here = at(stage, 0), at(stage, 1)
            for slot in range(width):
                ahead = at(stage, slot + 2)
                new = advance(last, here, ahead, alpha, upward)
                if beta is not None:
                    new = blend(new, beta, at(3 * turn, slot + 1 + kind))
                store(strip, (stage + 1, slot), new)
                last, here = here, ahead
        return 0

    lax.fori_loop(0, STEPS, step, 0)
    for slot in range(jumps.shape[1]):
        if slot < width:
            end, lost = load(strip, STAGES, slot), load(faded, side, slot)
            jump = [[end[c][odd] - lost[c][odd] for odd in (0, 1)] for c in range(3)]
        else:
            jump = load(middle, slot - width)
        for odd in (0, 1):
            for c in range(3):
                jumps[odd, slot, c] = jump[c][odd]


def jumps_kernel(far, face_ref, edges, middle, faded, *refs):
    outs, strip, jumps = refs[:GROUP], refs[-2], refs[-1]
    side = far + (1 - 2 * far) * near_side()
    border(side, face_ref, edges, middle, faded, jumps, strip)
    for k, out in enumerate(outs):
        out[...] = share_of(jumps, k, out.shape[0])


def sort_in(early, late, order):
    split = early[0].shape[0]
    for k in range(GROUP):
        place = lax.bitwise_xor(spot(), partner(k))
        order[place, :split] = early[k][...]
        order[place, split:] = late[k][...]


def sort_out(order, outs):
    for k in range(GROUP):
        outs[k][...] = order[lax.bitwise_xor(spot(), partner(k))]


def run(order, damp, total):
    for j in range(GROUP):
        jump = order[j]
        order[j] = total
        total = damp * total + jump
    return total


def total_of(jumps, damp):
    total = None
    for slice_ in range(GROUP):
        jump = jumps[slice_]
        total = jump if total is None else damp[:, None] * total + jump
    return total


def early_kernel(*refs):
    jumps, (damp_ref, out, order) = refs[:GROUP], refs[GROUP:]
    for k in range(GROUP):
        order[lax.bitwise_xor(spot(), partner(k))] = jumps[k][...]
    out[...] = total_of(order, damp_ref[: out.shape[0]])


def total_kernel(early_ref, *refs):
    jumps, (damp_ref, out, order) = refs[:GROUP], refs[GROUP:]
    split = early_ref.shape[0]
    for k in range(GROUP):
        order[lax.bitwise_xor(spot(), partner(k))] = jumps[k][...]
    out[:split] = early_ref[...]
    out[split:] = total_of(order, damp_ref[split:])


def spread_kernel(*refs):
    carry_ref, early, late = refs[0], refs[1 : 1 + GROUP], refs[1 + GROUP : 1 + 2 * GROUP]
    damp_ref, outs, order = refs[1 + 2 * GROUP], refs[2 + 2 * GROUP : -1], refs[-1]
    sort_in(early, late, order)
    run(order, damp_ref[...][:, None], jnp.where(lax.axis_index("tm") < GROUP, 0.0, carry_ref[...]))
    sort_out(order, outs)


def write(whole, out, sem):
    copy = pltpu.make_async_copy(whole, out, sem)
    copy.start()
    copy.wait()


def first_kernel(kept, out, whole, sem):
    @pl.when(lax.axis_index("tm") == 0)
    def _():
        for layer in range(out.shape[1]):
            pair = load(kept, layer)
            for c in range(3):
                join_rows(whole, (c, layer), pair[c])
        write(whole, out, sem)


def finish_kernel(*refs):
    pieces, (_, out, whole, sem) = refs[:GROUP], refs[GROUP:]
    layers, rows = out.shape[1], out.shape[2] // 2
    split = (layers - STAGES) // 2
    near = near_side()

    @pl.when(lax.axis_index("tm") != 0)
    def _():
        for k, piece in enumerate(pieces):
            chunk = chunk_of(k)
            for odd in (0, 1):

                @pl.when(chunk // 2 == odd)
                def _():
                    for j in range(piece.shape[0]):
                        if j < split:
                            slot = lax.rem(chunk, 2) * split + j
                        else:
                            slot = layers - 1 - (lax.rem(chunk, 2) * (STAGES // 2) + j - split)
                        layer = slot + near * (layers - 1 - 2 * slot)
                        for c in range(3):
                            whole[c, layer, pl.ds(odd, rows, stride=2), :] = piece[j, c]
        write(whole, out, sem)


def shards(states, rate):
    slices = lax.axis_size("tm")
    slabs = lax.axis_size("gz")
    groups = slices // GROUP
    own = states[0]
    layers, rows, width = own.shape[1:]
    middle_layers = layers - 2 * STAGES
    tile = (3, 2, rows // 2, width)
    face = f32(3, STAGES, rows, width)
    sizes = ((layers - STAGES) // 2, STAGES // 2)
    team = lax.axis_index("tm") // GROUP

    def halo(value, pairs):
        return lax.ppermute(value, "gz", [(i, j % slabs) for i, j in pairs])

    def swap(parts):
        return [parts[0]] + [
            lax.ppermute(parts[k], "tm", [(i, i ^ partner(k)) for i in range(slices)])
            for k in range(1, GROUP)
        ]

    def onward(value, distance):
        step = distance * GROUP
        return lax.ppermute(value, "tm", [(i, (i + step) % slices) for i in range(slices)])

    far_face, near_face = call(faces_kernel, [face, face], own)
    near_face = halo(near_face, [(i, i ^ 1) for i in range(slabs)])
    far_face = halo(far_face, [(i, i + 1 if i % 2 else i - 1 + slabs) for i in range(slabs)])
    row = (rows // 2, width)
    edges, middle, faded, damp, kept = call(
        inside_kernel,
        [
            f32(STAGES, 2, 3, *tile),
            f32(middle_layers, *tile),
            f32(2, STAGES, *tile),
            f32(sum(sizes), *row),
            f32(layers, *tile),
        ],
        own, rate,
        scratch=[
            pltpu.VMEM((2, 2, STAGES, *row), jnp.float32),
            pltpu.VMEM((2, layers - STAGES, *row), jnp.float32),
        ]
        + [pltpu.VMEM((layers, *tile), jnp.float32)] * 3,
        flops=1 << 26,
    )
    strip = pltpu.VMEM((STAGES + 1, STAGES, *tile), jnp.float32)
    shares = [f32(size, 3, *row) for size in sizes]
    whole_share = f32(sum(sizes), 3, *row)
    order = pltpu.VMEM((GROUP, *whole_share.shape), jnp.float32)

    def after(value, earlier):
        return lax.optimization_barrier((value, earlier))[0]

    halves = []
    for far, face_ref in enumerate((near_face, far_face)):
        jumps = call(
            functools.partial(jumps_kernel, far), [shares[far]] * GROUP,
            face_ref, edges, middle, faded,
            scratch=[strip, pltpu.VMEM((2, 2 * sizes[far], 3, *row), jnp.float32)],
            flops=BUSY,
        )
        halves.append(swap(jumps))

    orders = [pltpu.VMEM((GROUP, *share.shape), jnp.float32) for share in shares]
    halves[0][0] = after(halves[0][0], halves[1][0])
    total = call(early_kernel, shares[0], *halves[0], damp, scratch=[orders[0]], flops=BUSY)
    total = call(
        total_kernel, whole_share, total, *halves[1], damp, scratch=[orders[1]], flops=BUSY
    )
    carry = onward(total, 1)
    if groups > 2:
        carry = jnp.where(team < 1, 0.0, carry)
        fade, distance = damp[:, None] ** GROUP, 1
        while distance < groups - 1:
            carry = carry + jnp.where(team < distance, 0.0, fade * onward(carry, distance))
            distance, fade = 2 * distance, fade * fade
    news = call(
        spread_kernel, [whole_share] * GROUP, carry, *halves[0], *halves[1], damp, scratch=[order]
    )
    pieces = swap(news)
    whole = [pltpu.VMEM(own.shape, jnp.float32), pltpu.SemaphoreType.DMA]
    updated = pl.pallas_call(
        first_kernel,
        out_shape=f32(*own.shape),
        in_specs=[VMEM],
        out_specs=ANY,
        scratch_shapes=whole,
        compiler_params=PARAMS,
        cost_estimate=pl.CostEstimate(flops=BUSY, bytes_accessed=1 << 20, transcendentals=0),
    )(after(kept, pieces[1]))
    updated = pl.pallas_call(
        finish_kernel,
        out_shape=f32(*own.shape),
        in_specs=[VMEM] * GROUP + [ANY],
        out_specs=ANY,
        scratch_shapes=whole,
        input_output_aliases={GROUP: 0},
        compiler_params=PARAMS,
    )(*pieces, updated)
    return updated[None]


def solution(mesh):
    return jax.shard_map(
        shards,
        mesh=mesh,
        in_specs=(P("tm", None, "gz", None, None), P("gz", None, None)),
        out_specs=P("tm", None, "gz", None, None),
        check_vma=False,
    )
```

```python
import functools

import jax
import jax.numpy as jnp
from jax import lax
from jax.experimental import pallas as pl
from jax.experimental.pallas import tpu as pltpu
from jax.sharding import PartitionSpec as P

STEPS = 2
STAGES = 3 * STEPS
BUSY = 1 << 32
GROUP = 4
VISCOSITY = 0.05
TIME_STEP = 0.2
MIX = ((1.0, None), (0.25, 0.75), (2.0 / 3.0, 1.0 / 3.0))
VMEM = pl.BlockSpec(memory_space=pltpu.VMEM)
ANY = pl.BlockSpec(memory_space=pl.ANY)
PARAMS = pltpu.CompilerParams(vmem_limit_bytes=16 * 1024 * 1024)


def call(kernel, out_shape, *args, scratch=(), flops=None):
    cost = None
    if flops is not None:
        cost = pl.CostEstimate(flops=flops, bytes_accessed=1 << 20, transcendentals=0)
    return pl.pallas_call(
        kernel,
        out_shape=out_shape,
        in_specs=[VMEM] * len(args),
        out_specs=jax.tree.map(lambda _: VMEM, out_shape),
        scratch_shapes=list(scratch),
        compiler_params=PARAMS,
        cost_estimate=cost,
    )(*args)


def f32(*shape):
    return jax.ShapeDtypeStruct(shape, jnp.float32)


def partner(k):
    return (GROUP - k) % GROUP


def spot():
    return lax.rem(lax.axis_index("tm"), GROUP)


def chunk_of(k):
    return lax.bitwise_xor(spot(), partner(k))


def share_of(ref, k, count):
    chunk = chunk_of(k)
    return ref[chunk // 2, pl.ds(lax.rem(chunk, 2) * count, count)]


def near_side():
    return 1 - lax.rem(lax.axis_index("gz"), 2)


def split_rows(ref, *lead):
    half = ref.shape[-2] // 2
    return [ref[(*lead, pl.ds(odd, half, stride=2), slice(None))] for odd in (0, 1)]


def join_rows(ref, lead, pair):
    half = ref.shape[-2] // 2
    for odd in (0, 1):
        ref[(*lead, pl.ds(odd, half, stride=2), slice(None))] = pair[odd]


def load(ref, *lead):
    return [[ref[(*lead, c, odd)] for odd in (0, 1)] for c in range(3)]


def store(ref, lead, value):
    for c in range(3):
        for odd in (0, 1):
            ref[(*lead, c, odd)] = value[c][odd]


def advance(last, here, ahead, alpha, upward=1.0):
    diffuse = alpha * TIME_STEP * VISCOSITY
    carry = alpha * TIME_STEP * 0.5
    result = [[None, None] for _ in range(3)]
    for odd in (0, 1):
        speed = [here[0][odd] * carry, here[1][odd] * carry, here[2][odd] * (carry * upward)]
        to_next = [diffuse - s for s in speed]
        to_last = [diffuse + s for s in speed]
        for c in range(3):
            w = here[c][odd]
            rows, width = w.shape
            other = here[c][1 - odd]
            if odd:
                y_next, y_last = pltpu.roll(other, rows - 1, 0), other
            else:
                y_next, y_last = other, pltpu.roll(other, 1, 0)
            total = (alpha - 6.0 * diffuse) * w
            total = total + (
                to_next[0] * pltpu.roll(w, width - 1, 1) + to_last[0] * pltpu.roll(w, 1, 1)
            )
            total = total + (to_next[1] * y_next + to_last[1] * y_last)
            total = total + (to_next[2] * ahead[c][odd] + to_last[2] * last[c][odd])
            result[c][odd] = total
    return result


def blend(new, beta, base):
    return [[new[c][odd] + beta * base[c][odd] for odd in (0, 1)] for c in range(3)]


def faces_kernel(own_ref, far_ref, near_ref, sems):
    layers, width = own_ref.shape[1], near_ref.shape[1]
    near = near_side()
    top = layers - width
    copies = [
        pltpu.make_async_copy(own_ref.at[c, pl.ds(start, width)], ref.at[c], sems.at[c, j])
        for j, (ref, start) in enumerate(((near_ref, near * top), (far_ref, (1 - near) * top)))
        for c in range(3)
    ]
    for copy in copies:
        copy.start()
    for copy in copies:
        copy.wait()


def inside_kernel(own_ref, rate_ref, edges, middle, faded, early_damp, late_damp, kept, damps, inner, *fields):
    layers = own_ref.shape[1]
    near = near_side()
    slices = lax.axis_size("tm")
    keep = (lax.axis_index("tm") != 0).astype(jnp.float32)

    def side_of(z):
        return (0, z) if z < layers - 1 - z else (1, layers - 1 - z)

    def from_near(z):
        return z - STAGES + near * (layers - 1 - 2 * z)

    def save(stage, z, value):
        low, high = z - stage, layers - 1 - stage - z
        if low < 3:
            store(edges, (stage, 0, low), value)
        if high < 3:
            store(edges, (stage, 1, high), value)

    for z in range(layers):
        side, slot = side_of(z)
        damp = [jnp.exp(r * (-1.0 / slices)) for r in split_rows(rate_ref, z)]
        start = [split_rows(own_ref, c, z) for c in range(3)]
        store(fields[0], (z,), start)
        store(kept, (z,), start)
        save(0, z, start)
        lost = [[damp[odd] * keep * start[c][odd] for odd in (0, 1)] for c in range(3)]
        if slot < STAGES:
            store(faded, (side, slot), lost)
            for odd in (0, 1):
                damps[side, odd, slot] = damp[odd]
        else:
            store(middle, (from_near(z),), lost)
            for odd in (0, 1):
                inner[odd, STAGES + from_near(z)] = damp[odd]

    for stage in range(1, STAGES + 1):
        kind = (stage - 1) % 3
        alpha, beta = MIX[kind]
        source, target = fields[kind], fields[(kind + 1) % 3]
        below, here = load(source, stage - 1), load(source, stage)
        for z in range(stage, layers - stage):
            above = load(source, z + 1)
            new = advance(below, here, above, alpha)
            if beta is not None:
                new = blend(new, beta, load(fields[0], z))
            if stage < STAGES:
                store(target, (z,), new)
                save(stage, z, new)
            else:
                lost = load(middle, from_near(z))
                store(
                    middle,
                    (from_near(z),),
                    [[new[c][odd] - lost[c][odd] for odd in (0, 1)] for c in range(3)],
                )
            below, here = here, above

    for odd in (0, 1):
        inner[odd, :STAGES] = damps[near, odd]
    early_damp[...] = share_of(inner, 0, early_damp.shape[0])
    late_damp[...] = share_of(damps.at[1 - near], 0, late_damp.shape[0])


def border(side, face_ref, edges, middle, faded, jumps, strip):
    width = STAGES
    upward = 1.0 - 2.0 * side.astype(jnp.float32)
    for slot in range(width):
        layer = slot + side * (width - 1 - 2 * slot)
        store(strip, (0, slot), [split_rows(face_ref, c, layer) for c in range(3)])

    def at(stage, slot):
        if slot < width:
            return load(strip, stage, slot)
        return load(edges, stage, side, slot - width)

    def step(turn, _):
        for kind, (alpha, beta) in enumerate(MIX):
            stage = 3 * turn + kind
            last, here = at(stage, 0), at(stage, 1)
            for slot in range(width):
                ahead = at(stage, slot + 2)
                new = advance(last, here, ahead, alpha, upward)
                if beta is not None:
                    new = blend(new, beta, at(3 * turn, slot + 1 + kind))
                store(strip, (stage + 1, slot), new)
                last, here = here, ahead
        return 0

    lax.fori_loop(0, STEPS, step, 0)
    for slot in range(jumps.shape[1]):
        if slot < width:
            end, lost = load(strip, STAGES, slot), load(faded, side, slot)
            jump = [[end[c][odd] - lost[c][odd] for odd in (0, 1)] for c in range(3)]
        else:
            jump = load(middle, slot - width)
        for odd in (0, 1):
            for c in range(3):
                jumps[odd, slot, c] = jump[c][odd]


def jumps_kernel(far, face_ref, edges, middle, faded, *refs):
    outs, strip, jumps = refs[:GROUP], refs[-2], refs[-1]
    side = far + (1 - 2 * far) * near_side()
    border(side, face_ref, edges, middle, faded, jumps, strip)
    for k, out in enumerate(outs):
        out[...] = share_of(jumps, k, out.shape[0])


def sort_in(jumps, order):
    for k in range(GROUP):
        order[lax.bitwise_xor(spot(), partner(k))] = jumps[k][...]


def sort_out(order, outs):
    for k in range(GROUP):
        outs[k][...] = order[lax.bitwise_xor(spot(), partner(k))]


def run(order, damp, total):
    for j in range(GROUP):
        jump = order[j]
        order[j] = total
        total = damp * total + jump
    return total


def total_kernel(*refs):
    jumps, damp_ref, out, order = refs[:GROUP], refs[GROUP], refs[GROUP + 1], refs[GROUP + 2]
    sort_in(jumps, order)
    out[...] = run(order, damp_ref[...][:, None], jnp.zeros(out.shape, jnp.float32))


def spread_kernel(*refs):
    carry_ref, jumps, damp_ref = refs[0], refs[1 : 1 + GROUP], refs[1 + GROUP]
    outs, order = refs[GROUP + 2 : -1], refs[-1]
    sort_in(jumps, order)
    run(order, damp_ref[...][:, None], jnp.where(lax.axis_index("tm") < GROUP, 0.0, carry_ref[...]))
    sort_out(order, outs)


def finish_kernel(far, kept, *refs):
    pieces, (out, part, sem) = refs[:GROUP], refs[-3:]
    layers, rows = out.shape[1], out.shape[2] // 2
    share = pieces[0].shape[0]
    count = 2 * share
    down = far + (1 - 2 * far) * near_side()
    first_slice = lax.axis_index("tm") == 0

    def write(base, count):
        copy = pltpu.make_async_copy(part.at[:, pl.ds(0, count)], out.at[:, pl.ds(base, count)], sem)
        copy.start()
        copy.wait()

    if not far:

        @pl.when(first_slice)
        def _():
            for layer in range(layers):
                pair = load(kept, layer)
                for c in range(3):
                    join_rows(part, (c, layer), pair[c])
            write(0, layers)

    @pl.when(jnp.logical_not(first_slice))
    def _():
        for k, piece in enumerate(pieces):
            chunk = chunk_of(k)
            for odd in (0, 1):

                @pl.when(chunk // 2 == odd)
                def _():
                    for j in range(share):
                        slot = lax.rem(chunk, 2) * share + j
                        layer = slot + down * (count - 1 - 2 * slot)
                        for c in range(3):
                            part[c, layer, pl.ds(odd, rows, stride=2), :] = piece[j, c]
        write(down * (layers - count), count)


def shards(states, rate):
    slices = lax.axis_size("tm")
    slabs = lax.axis_size("gz")
    groups = slices // GROUP
    own = states[0]
    layers, rows, width = own.shape[1:]
    middle_layers = layers - 2 * STAGES
    tile = (3, 2, rows // 2, width)
    face = f32(3, STAGES, rows, width)
    sizes = ((layers - STAGES) // 2, STAGES // 2)
    team = lax.axis_index("tm") // GROUP

    def halo(value, pairs):
        return lax.ppermute(value, "gz", [(i, j % slabs) for i, j in pairs])

    def swap(parts):
        return [parts[0]] + [
            lax.ppermute(parts[k], "tm", [(i, i ^ partner(k)) for i in range(slices)])
            for k in range(1, GROUP)
        ]

    def onward(value, distance):
        step = distance * GROUP
        return lax.ppermute(value, "tm", [(i, (i + step) % slices) for i in range(slices)])

    far_face, near_face = pl.pallas_call(
        faces_kernel,
        out_shape=[face, face],
        in_specs=[ANY],
        out_specs=[ANY, ANY],
        scratch_shapes=[pltpu.SemaphoreType.DMA((3, 2))],
        compiler_params=pltpu.CompilerParams(vmem_limit_bytes=60 << 20),
    )(own)
    near_face = halo(near_face, [(i, i ^ 1) for i in range(slabs)])
    far_face = halo(far_face, [(i, i + 1 if i % 2 else i - 1 + slabs) for i in range(slabs)])
    row = (rows // 2, width)
    edges, middle, faded, *damps, kept = call(
        inside_kernel,
        [
            f32(STAGES, 2, 3, *tile),
            f32(middle_layers, *tile),
            f32(2, STAGES, *tile),
            *[f32(size, *row) for size in sizes],
            f32(layers, *tile),
        ],
        own, rate,
        scratch=[
            pltpu.VMEM((2, 2, STAGES, *row), jnp.float32),
            pltpu.VMEM((2, layers - STAGES, *row), jnp.float32),
        ]
        + [pltpu.VMEM((layers, *tile), jnp.float32)] * 3,
        flops=1 << 26,
    )
    strip = pltpu.VMEM((STAGES + 1, STAGES, *tile), jnp.float32)
    shares = [f32(size, 3, *row) for size in sizes]
    orders = [pltpu.VMEM((GROUP, *share.shape), jnp.float32) for share in shares]

    def after(value, earlier):
        return lax.optimization_barrier((value, earlier))[0]

    halves = []
    for far, face_ref in enumerate((near_face, far_face)):
        jumps = call(
            functools.partial(jumps_kernel, far), [shares[far]] * GROUP,
            face_ref, edges, middle, faded,
            scratch=[strip, pltpu.VMEM((2, 2 * sizes[far], 3, *row), jnp.float32)],
            flops=BUSY,
        )
        halves.append(swap(jumps))

    carries, total = [], halves[1][0]
    for far, jumps in enumerate(halves):
        jumps[0] = after(jumps[0], total)
        total = call(
            total_kernel, shares[far], *jumps, damps[far], scratch=[orders[far]], flops=BUSY
        )
        carry = onward(total, 1)
        if groups > 2:
            carry = jnp.where(team < 1, 0.0, carry)
            fade, distance = damps[far][:, None] ** GROUP, 1
            while distance < groups - 1:
                carry = carry + jnp.where(team < distance, 0.0, fade * onward(carry, distance))
                distance, fade = 2 * distance, fade * fade
        carries.append(carry)

    updated, news = None, None
    for far, (jumps, carry) in enumerate(zip(halves, carries)):
        if far:
            jumps[0] = after(jumps[0], news[0])
        news = call(
            spread_kernel, [shares[far]] * GROUP, carry, *jumps, damps[far],
            scratch=[orders[far]],
            flops=BUSY,
        )
        halves[far] = swap(news)
    for far, pieces in enumerate(halves):
        args = [kept, *pieces] + ([updated] if far else [])
        updated = pl.pallas_call(
            functools.partial(finish_kernel, far),
            out_shape=f32(*own.shape),
            in_specs=[VMEM] * (1 + GROUP) + [ANY] * far,
            out_specs=ANY,
            scratch_shapes=[
                pltpu.VMEM((3, 2 * sizes[far] if far else layers, rows, width), jnp.float32),
                pltpu.SemaphoreType.DMA,
            ],
            input_output_aliases={1 + GROUP: 0} if far else {},
            compiler_params=PARAMS,
            cost_estimate=pl.CostEstimate(flops=BUSY, bytes_accessed=1 << 20, transcendentals=0),
        )(*args)
    return updated[None]


def solution(mesh):
    return jax.shard_map(
        shards,
        mesh=mesh,
        in_specs=(P("tm", None, "gz", None, None), P("gz", None, None)),
        out_specs=P("tm", None, "gz", None, None),
        check_vma=False,
    )
```

```python
import functools

import jax
import jax.numpy as jnp
from jax import lax
from jax.experimental import pallas as pl
from jax.experimental.pallas import tpu as pltpu
from jax.sharding import PartitionSpec as P

STEPS = 2
STAGES = 3 * STEPS
BUSY = 1 << 32
GROUP = 4
VISCOSITY = 0.05
TIME_STEP = 0.2
MIX = ((1.0, None), (0.25, 0.75), (2.0 / 3.0, 1.0 / 3.0))
VMEM = pl.BlockSpec(memory_space=pltpu.VMEM)
ANY = pl.BlockSpec(memory_space=pl.ANY)
PARAMS = pltpu.CompilerParams(vmem_limit_bytes=16 * 1024 * 1024)


def call(kernel, out_shape, *args, scratch=(), flops=None):
    cost = None
    if flops is not None:
        cost = pl.CostEstimate(flops=flops, bytes_accessed=1 << 20, transcendentals=0)
    return pl.pallas_call(
        kernel,
        out_shape=out_shape,
        in_specs=[VMEM] * len(args),
        out_specs=jax.tree.map(lambda _: VMEM, out_shape),
        scratch_shapes=list(scratch),
        compiler_params=PARAMS,
        cost_estimate=cost,
    )(*args)


def f32(*shape):
    return jax.ShapeDtypeStruct(shape, jnp.float32)


def partner(k):
    return (GROUP - k) % GROUP


def spot():
    return lax.rem(lax.axis_index("tm"), GROUP)


def chunk_of(k):
    return lax.bitwise_xor(spot(), partner(k))


def share_of(ref, k, count):
    chunk = chunk_of(k)
    return ref[chunk // 2, pl.ds(lax.rem(chunk, 2) * count, count)]


def near_side():
    return 1 - lax.rem(lax.axis_index("gz"), 2)


def split_rows(ref, *lead):
    half = ref.shape[-2] // 2
    return [ref[(*lead, pl.ds(odd, half, stride=2), slice(None))] for odd in (0, 1)]


def join_rows(ref, lead, pair):
    half = ref.shape[-2] // 2
    for odd in (0, 1):
        ref[(*lead, pl.ds(odd, half, stride=2), slice(None))] = pair[odd]


def load(ref, *lead):
    return [[ref[(*lead, c, odd)] for odd in (0, 1)] for c in range(3)]


def store(ref, lead, value):
    for c in range(3):
        for odd in (0, 1):
            ref[(*lead, c, odd)] = value[c][odd]


def advance(last, here, ahead, alpha, upward=1.0):
    diffuse = alpha * TIME_STEP * VISCOSITY
    carry = alpha * TIME_STEP * 0.5
    result = [[None, None] for _ in range(3)]
    for odd in (0, 1):
        speed = [here[0][odd] * carry, here[1][odd] * carry, here[2][odd] * (carry * upward)]
        to_next = [diffuse - s for s in speed]
        to_last = [diffuse + s for s in speed]
        for c in range(3):
            w = here[c][odd]
            rows, width = w.shape
            other = here[c][1 - odd]
            if odd:
                y_next, y_last = pltpu.roll(other, rows - 1, 0), other
            else:
                y_next, y_last = other, pltpu.roll(other, 1, 0)
            total = (alpha - 6.0 * diffuse) * w
            total = total + (
                to_next[0] * pltpu.roll(w, width - 1, 1) + to_last[0] * pltpu.roll(w, 1, 1)
            )
            total = total + (to_next[1] * y_next + to_last[1] * y_last)
            total = total + (to_next[2] * ahead[c][odd] + to_last[2] * last[c][odd])
            result[c][odd] = total
    return result


def blend(new, beta, base):
    return [[new[c][odd] + beta * base[c][odd] for odd in (0, 1)] for c in range(3)]


def faces_kernel(own_ref, far_ref, near_ref):
    layers, width = own_ref.shape[1], near_ref.shape[1]
    near = near_side()
    top = layers - width
    far_ref[...] = own_ref[:, pl.ds((1 - near) * top, width)]
    near_ref[...] = own_ref[:, pl.ds(near * top, width)]


def inside_kernel(own_ref, rate_ref, edges, middle, faded, damp_ref, kept, damps, inner, *fields):
    layers = own_ref.shape[1]
    near = near_side()
    slices = lax.axis_size("tm")
    keep = (lax.axis_index("tm") != 0).astype(jnp.float32)

    def side_of(z):
        return (0, z) if z < layers - 1 - z else (1, layers - 1 - z)

    def from_near(z):
        return z - STAGES + near * (layers - 1 - 2 * z)

    def save(stage, z, value):
        low, high = z - stage, layers - 1 - stage - z
        if low < 3:
            store(edges, (stage, 0, low), value)
        if high < 3:
            store(edges, (stage, 1, high), value)

    for z in range(layers):
        side, slot = side_of(z)
        damp = [jnp.exp(r * (-1.0 / slices)) for r in split_rows(rate_ref, z)]
        start = [split_rows(own_ref, c, z) for c in range(3)]
        store(fields[0], (z,), start)
        store(kept, (z,), start)
        save(0, z, start)
        lost = [[damp[odd] * keep * start[c][odd] for odd in (0, 1)] for c in range(3)]
        if slot < STAGES:
            store(faded, (side, slot), lost)
            for odd in (0, 1):
                damps[side, odd, slot] = damp[odd]
        else:
            store(middle, (from_near(z),), lost)
            for odd in (0, 1):
                inner[odd, STAGES + from_near(z)] = damp[odd]

    for stage in range(1, STAGES + 1):
        kind = (stage - 1) % 3
        alpha, beta = MIX[kind]
        source, target = fields[kind], fields[(kind + 1) % 3]
        below, here = load(source, stage - 1), load(source, stage)
        for z in range(stage, layers - stage):
            above = load(source, z + 1)
            new = advance(below, here, above, alpha)
            if beta is not None:
                new = blend(new, beta, load(fields[0], z))
            if stage < STAGES:
                store(target, (z,), new)
                save(stage, z, new)
            else:
                lost = load(middle, from_near(z))
                store(
                    middle,
                    (from_near(z),),
                    [[new[c][odd] - lost[c][odd] for odd in (0, 1)] for c in range(3)],
                )
            below, here = here, above

    for odd in (0, 1):
        inner[odd, :STAGES] = damps[near, odd]
    early, late = inner.shape[1] // 2, STAGES // 2
    damp_ref[:early] = share_of(inner, 0, early)
    damp_ref[early:] = share_of(damps.at[1 - near], 0, late)


def border(side, face_ref, edges, middle, faded, jumps, strip):
    width = STAGES
    upward = 1.0 - 2.0 * side.astype(jnp.float32)
    for slot in range(width):
        layer = slot + side * (width - 1 - 2 * slot)
        store(strip, (0, slot), [split_rows(face_ref, c, layer) for c in range(3)])

    def at(stage, slot):
        if slot < width:
            return load(strip, stage, slot)
        return load(edges, stage, side, slot - width)

    def step(turn, _):
        for kind, (alpha, beta) in enumerate(MIX):
            stage = 3 * turn + kind
            last, here = at(stage, 0), at(stage, 1)
            for slot in range(width):
                ahead = at(stage, slot + 2)
                new = advance(last, here, ahead, alpha, upward)
                if beta is not None:
                    new = blend(new, beta, at(3 * turn, slot + 1 + kind))
                store(strip, (stage + 1, slot), new)
                last, here = here, ahead
        return 0

    lax.fori_loop(0, STEPS, step, 0)
    for slot in range(jumps.shape[1]):
        if slot < width:
            end, lost = load(strip, STAGES, slot), load(faded, side, slot)
            jump = [[end[c][odd] - lost[c][odd] for odd in (0, 1)] for c in range(3)]
        else:
            jump = load(middle, slot - width)
        for odd in (0, 1):
            for c in range(3):
                jumps[odd, slot, c] = jump[c][odd]


def jumps_kernel(far, face_ref, edges, middle, faded, *refs):
    outs, strip, jumps = refs[:GROUP], refs[-2], refs[-1]
    side = far + (1 - 2 * far) * near_side()
    border(side, face_ref, edges, middle, faded, jumps, strip)
    for k, out in enumerate(outs):
        out[...] = share_of(jumps, k, out.shape[0])


def sort_in(early, late, order):
    split = early[0].shape[0]
    for k in range(GROUP):
        place = lax.bitwise_xor(spot(), partner(k))
        order[place, :split] = early[k][...]
        order[place, split:] = late[k][...]


def sort_out(order, outs):
    for k in range(GROUP):
        outs[k][...] = order[lax.bitwise_xor(spot(), partner(k))]


def run(order, damp, total):
    for j in range(GROUP):
        jump = order[j]
        order[j] = total
        total = damp * total + jump
    return total


def total_of(jumps, damp):
    total = None
    for slice_ in range(GROUP):
        jump = jumps[slice_]
        total = jump if total is None else damp[:, None] * total + jump
    return total


def total_kernel(first, *refs):
    jumps, (damp_ref, out, order) = refs[:GROUP], refs[GROUP:]
    for k in range(GROUP):
        order[lax.bitwise_xor(spot(), partner(k))] = jumps[k][...]
    out[...] = total_of(order, damp_ref[first : first + out.shape[0]])


def spread_kernel(early_carry, late_carry, *refs):
    early, late = refs[:GROUP], refs[GROUP : 2 * GROUP]
    damp_ref, outs, order, carry = refs[2 * GROUP], refs[1 + 2 * GROUP : -2], refs[-2], refs[-1]
    split = early_carry.shape[0]
    sort_in(early, late, order)
    carry[:split] = early_carry[...]
    carry[split:] = late_carry[...]
    run(order, damp_ref[...][:, None], jnp.where(lax.axis_index("tm") < GROUP, 0.0, carry[...]))
    sort_out(order, outs)


def write(whole, out, sem):
    copy = pltpu.make_async_copy(whole, out, sem)
    copy.start()
    copy.wait()


def first_kernel(kept, out, whole, sem):
    @pl.when(lax.axis_index("tm") == 0)
    def _():
        for layer in range(out.shape[1]):
            pair = load(kept, layer)
            for c in range(3):
                join_rows(whole, (c, layer), pair[c])
        write(whole, out, sem)


def finish_kernel(*refs):
    pieces, (_, out, whole, sem) = refs[:GROUP], refs[GROUP:]
    layers, rows = out.shape[1], out.shape[2] // 2
    split = (layers - STAGES) // 2
    near = near_side()

    @pl.when(lax.axis_index("tm") != 0)
    def _():
        for k, piece in enumerate(pieces):
            chunk = chunk_of(k)
            for odd in (0, 1):

                @pl.when(chunk // 2 == odd)
                def _():
                    for j in range(piece.shape[0]):
                        if j < split:
                            slot = lax.rem(chunk, 2) * split + j
                        else:
                            slot = layers - 1 - (lax.rem(chunk, 2) * (STAGES // 2) + j - split)
                        layer = slot + near * (layers - 1 - 2 * slot)
                        for c in range(3):
                            whole[c, layer, pl.ds(odd, rows, stride=2), :] = piece[j, c]
        write(whole, out, sem)


def shards(states, rate):
    slices = lax.axis_size("tm")
    slabs = lax.axis_size("gz")
    groups = slices // GROUP
    own = states[0]
    layers, rows, width = own.shape[1:]
    middle_layers = layers - 2 * STAGES
    tile = (3, 2, rows // 2, width)
    face = f32(3, STAGES, rows, width)
    sizes = ((layers - STAGES) // 2, STAGES // 2)
    team = lax.axis_index("tm") // GROUP

    def halo(value, pairs):
        return lax.ppermute(value, "gz", [(i, j % slabs) for i, j in pairs])

    def swap(parts):
        return [parts[0]] + [
            lax.ppermute(parts[k], "tm", [(i, i ^ partner(k)) for i in range(slices)])
            for k in range(1, GROUP)
        ]

    def onward(value, distance):
        step = distance * GROUP
        return lax.ppermute(value, "tm", [(i, (i + step) % slices) for i in range(slices)])

    far_face, near_face = call(faces_kernel, [face, face], own)
    near_face = halo(near_face, [(i, i ^ 1) for i in range(slabs)])
    far_face = halo(far_face, [(i, i + 1 if i % 2 else i - 1 + slabs) for i in range(slabs)])
    row = (rows // 2, width)
    edges, middle, faded, damp, kept = call(
        inside_kernel,
        [
            f32(STAGES, 2, 3, *tile),
            f32(middle_layers, *tile),
            f32(2, STAGES, *tile),
            f32(sum(sizes), *row),
            f32(layers, *tile),
        ],
        own, rate,
        scratch=[
            pltpu.VMEM((2, 2, STAGES, *row), jnp.float32),
            pltpu.VMEM((2, layers - STAGES, *row), jnp.float32),
        ]
        + [pltpu.VMEM((layers, *tile), jnp.float32)] * 3,
        flops=1 << 26,
    )
    strip = pltpu.VMEM((STAGES + 1, STAGES, *tile), jnp.float32)
    shares = [f32(size, 3, *row) for size in sizes]
    whole_share = f32(sum(sizes), 3, *row)
    order = pltpu.VMEM((GROUP, *whole_share.shape), jnp.float32)

    def after(value, earlier):
        return lax.optimization_barrier((value, earlier))[0]

    halves = []
    for far, face_ref in enumerate((near_face, far_face)):
        jumps = call(
            functools.partial(jumps_kernel, far), [shares[far]] * GROUP,
            face_ref, edges, middle, faded,
            scratch=[strip, pltpu.VMEM((2, 2 * sizes[far], 3, *row), jnp.float32)],
            flops=BUSY,
        )
        halves.append(swap(jumps))

    orders = [pltpu.VMEM((GROUP, *share.shape), jnp.float32) for share in shares]
    carries, total = [], halves[1][0]
    for far, jumps in enumerate(halves):
        jumps[0] = after(jumps[0], total)
        first = far * sizes[0]
        total = call(
            functools.partial(total_kernel, first), shares[far], *jumps, damp,
            scratch=[orders[far]],
            flops=BUSY,
        )
        carry = onward(total, 1)
        if groups > 2:
            carry = jnp.where(team < 1, 0.0, carry)
            fade, distance = damp[first : first + sizes[far], None] ** GROUP, 1
            while distance < groups - 1:
                carry = carry + jnp.where(team < distance, 0.0, fade * onward(carry, distance))
                distance, fade = 2 * distance, fade * fade
        carries.append(carry)
    news = call(
        spread_kernel, [whole_share] * GROUP, *carries, *halves[0], *halves[1], damp,
        scratch=[order, pltpu.VMEM(whole_share.shape, jnp.float32)],
    )
    pieces = swap(news)
    whole = [pltpu.VMEM(own.shape, jnp.float32), pltpu.SemaphoreType.DMA]
    updated = pl.pallas_call(
        first_kernel,
        out_shape=f32(*own.shape),
        in_specs=[VMEM],
        out_specs=ANY,
        scratch_shapes=whole,
        compiler_params=PARAMS,
        cost_estimate=pl.CostEstimate(flops=BUSY, bytes_accessed=1 << 20, transcendentals=0),
    )(after(kept, pieces[1]))
    updated = pl.pallas_call(
        finish_kernel,
        out_shape=f32(*own.shape),
        in_specs=[VMEM] * GROUP + [ANY],
        out_specs=ANY,
        scratch_shapes=whole,
        input_output_aliases={GROUP: 0},
        compiler_params=PARAMS,
    )(*pieces, updated)
    return updated[None]


def solution(mesh):
    return jax.shard_map(
        shards,
        mesh=mesh,
        in_specs=(P("tm", None, "gz", None, None), P("gz", None, None)),
        out_specs=P("tm", None, "gz", None, None),
        check_vma=False,
    )
```

```python
import functools

import jax
import jax.numpy as jnp
from jax import lax
from jax.experimental import pallas as pl
from jax.experimental.pallas import tpu as pltpu
from jax.sharding import PartitionSpec as P

STEPS = 2
STAGES = 3 * STEPS
BUSY = 1 << 32
GROUP = 4
VISCOSITY = 0.05
TIME_STEP = 0.2
MIX = ((1.0, None), (0.25, 0.75), (2.0 / 3.0, 1.0 / 3.0))
VMEM = pl.BlockSpec(memory_space=pltpu.VMEM)
ANY = pl.BlockSpec(memory_space=pl.ANY)
PARAMS = pltpu.CompilerParams(vmem_limit_bytes=16 * 1024 * 1024)


def call(kernel, out_shape, *args, scratch=(), flops=None):
    cost = None
    if flops is not None:
        cost = pl.CostEstimate(flops=flops, bytes_accessed=1 << 20, transcendentals=0)
    return pl.pallas_call(
        kernel,
        out_shape=out_shape,
        in_specs=[VMEM] * len(args),
        out_specs=jax.tree.map(lambda _: VMEM, out_shape),
        scratch_shapes=list(scratch),
        compiler_params=PARAMS,
        cost_estimate=cost,
    )(*args)


def f32(*shape):
    return jax.ShapeDtypeStruct(shape, jnp.float32)


def partner(k):
    return (GROUP - k) % GROUP


def spot():
    return lax.rem(lax.axis_index("tm"), GROUP)


def chunk_of(k):
    return lax.bitwise_xor(spot(), partner(k))


def share_of(ref, k, count):
    chunk = chunk_of(k)
    return ref[chunk // 2, pl.ds(lax.rem(chunk, 2) * count, count)]


def near_side():
    return 1 - lax.rem(lax.axis_index("gz"), 2)


def split_rows(ref, *lead):
    half = ref.shape[-2] // 2
    return [ref[(*lead, pl.ds(odd, half, stride=2), slice(None))] for odd in (0, 1)]


def join_rows(ref, lead, pair):
    half = ref.shape[-2] // 2
    for odd in (0, 1):
        ref[(*lead, pl.ds(odd, half, stride=2), slice(None))] = pair[odd]


def load(ref, *lead):
    return [[ref[(*lead, c, odd)] for odd in (0, 1)] for c in range(3)]


def store(ref, lead, value):
    for c in range(3):
        for odd in (0, 1):
            ref[(*lead, c, odd)] = value[c][odd]


def advance(last, here, ahead, alpha, upward=1.0):
    diffuse = alpha * TIME_STEP * VISCOSITY
    carry = alpha * TIME_STEP * 0.5
    result = [[None, None] for _ in range(3)]
    for odd in (0, 1):
        speed = [here[0][odd] * carry, here[1][odd] * carry, here[2][odd] * (carry * upward)]
        to_next = [diffuse - s for s in speed]
        to_last = [diffuse + s for s in speed]
        for c in range(3):
            w = here[c][odd]
            rows, width = w.shape
            other = here[c][1 - odd]
            if odd:
                y_next, y_last = pltpu.roll(other, rows - 1, 0), other
            else:
                y_next, y_last = other, pltpu.roll(other, 1, 0)
            total = (alpha - 6.0 * diffuse) * w
            total = total + (
                to_next[0] * pltpu.roll(w, width - 1, 1) + to_last[0] * pltpu.roll(w, 1, 1)
            )
            total = total + (to_next[1] * y_next + to_last[1] * y_last)
            total = total + (to_next[2] * ahead[c][odd] + to_last[2] * last[c][odd])
            result[c][odd] = total
    return result


def blend(new, beta, base):
    return [[new[c][odd] + beta * base[c][odd] for odd in (0, 1)] for c in range(3)]


def faces_kernel(own_ref, far_ref, near_ref):
    layers, width = own_ref.shape[1], near_ref.shape[1]
    near = near_side()
    top = layers - width
    far_ref[...] = own_ref[:, pl.ds((1 - near) * top, width)]
    near_ref[...] = own_ref[:, pl.ds(near * top, width)]


def inside_kernel(own_ref, rate_ref, edges, middle, faded, damp_ref, kept, damps, inner, *fields):
    layers = own_ref.shape[1]
    near = near_side()
    slices = lax.axis_size("tm")
    keep = (lax.axis_index("tm") != 0).astype(jnp.float32)

    def side_of(z):
        return (0, z) if z < layers - 1 - z else (1, layers - 1 - z)

    def from_near(z):
        return z - STAGES + near * (layers - 1 - 2 * z)

    def save(stage, z, value):
        low, high = z - stage, layers - 1 - stage - z
        if low < 3:
            store(edges, (stage, 0, low), value)
        if high < 3:
            store(edges, (stage, 1, high), value)

    for z in range(layers):
        side, slot = side_of(z)
        damp = [jnp.exp(r * (-1.0 / slices)) for r in split_rows(rate_ref, z)]
        start = [split_rows(own_ref, c, z) for c in range(3)]
        store(fields[0], (z,), start)
        store(kept, (z,), start)
        save(0, z, start)
        lost = [[damp[odd] * keep * start[c][odd] for odd in (0, 1)] for c in range(3)]
        if slot < STAGES:
            store(faded, (side, slot), lost)
            for odd in (0, 1):
                damps[side, odd, slot] = damp[odd]
        else:
            store(middle, (from_near(z),), lost)
            for odd in (0, 1):
                inner[odd, STAGES + from_near(z)] = damp[odd]

    for stage in range(1, STAGES + 1):
        kind = (stage - 1) % 3
        alpha, beta = MIX[kind]
        source, target = fields[kind], fields[(kind + 1) % 3]
        below, here = load(source, stage - 1), load(source, stage)
        for z in range(stage, layers - stage):
            above = load(source, z + 1)
            new = advance(below, here, above, alpha)
            if beta is not None:
                new = blend(new, beta, load(fields[0], z))
            if stage < STAGES:
                store(target, (z,), new)
                save(stage, z, new)
            else:
                lost = load(middle, from_near(z))
                store(
                    middle,
                    (from_near(z),),
                    [[new[c][odd] - lost[c][odd] for odd in (0, 1)] for c in range(3)],
                )
            below, here = here, above

    for odd in (0, 1):
        inner[odd, :STAGES] = damps[near, odd]
    early, late = inner.shape[1] // 2, STAGES // 2
    damp_ref[:early] = share_of(inner, 0, early)
    damp_ref[early:] = share_of(damps.at[1 - near], 0, late)


def border(side, face_ref, edges, middle, faded, jumps, strip):
    width = STAGES
    upward = 1.0 - 2.0 * side.astype(jnp.float32)
    for slot in range(width):
        layer = slot + side * (width - 1 - 2 * slot)
        store(strip, (0, slot), [split_rows(face_ref, c, layer) for c in range(3)])

    def at(stage, slot):
        if slot < width:
            return load(strip, stage, slot)
        return load(edges, stage, side, slot - width)

    def step(turn, _):
        for kind, (alpha, beta) in enumerate(MIX):
            stage = 3 * turn + kind
            last, here = at(stage, 0), at(stage, 1)
            for slot in range(width):
                ahead = at(stage, slot + 2)
                new = advance(last, here, ahead, alpha, upward)
                if beta is not None:
                    new = blend(new, beta, at(3 * turn, slot + 1 + kind))
                store(strip, (stage + 1, slot), new)
                last, here = here, ahead
        return 0

    lax.fori_loop(0, STEPS, step, 0)
    for slot in range(jumps.shape[1]):
        if slot < width:
            end, lost = load(strip, STAGES, slot), load(faded, side, slot)
            jump = [[end[c][odd] - lost[c][odd] for odd in (0, 1)] for c in range(3)]
        else:
            jump = load(middle, slot - width)
        for odd in (0, 1):
            for c in range(3):
                jumps[odd, slot, c] = jump[c][odd]


def jumps_kernel(far, face_ref, edges, middle, faded, *refs):
    outs, strip, jumps = refs[:GROUP], refs[-2], refs[-1]
    side = far + (1 - 2 * far) * near_side()
    border(side, face_ref, edges, middle, faded, jumps, strip)
    for k, out in enumerate(outs):
        out[...] = share_of(jumps, k, out.shape[0])


def run(order, damp, total):
    for j in range(GROUP):
        jump = order[j]
        order[j] = total
        total = damp * total + jump
    return total


def total_of(jumps, damp):
    total = None
    for slice_ in range(GROUP):
        jump = jumps[slice_]
        total = jump if total is None else damp[:, None] * total + jump
    return total


def total_kernel(first, *refs):
    jumps, (damp_ref, out, order) = refs[:GROUP], refs[GROUP:]
    for k in range(GROUP):
        order[lax.bitwise_xor(spot(), partner(k))] = jumps[k][...]
    out[...] = total_of(order, damp_ref[first : first + out.shape[0]])


def news_of(first, carry_ref, jumps, damp_ref, order):
    for k in range(GROUP):
        order[lax.bitwise_xor(spot(), partner(k))] = jumps[k][...]
    damp = damp_ref[first : first + carry_ref.shape[0]][:, None]
    run(order, damp, jnp.where(lax.axis_index("tm") < GROUP, 0.0, carry_ref[...]))


def early_kernel(carry_ref, *refs):
    jumps, damp_ref, outs, order = refs[:GROUP], refs[GROUP], refs[GROUP + 1 : -1], refs[-1]
    news_of(0, carry_ref, jumps, damp_ref, order)
    for k, out in enumerate(outs):
        out[...] = order[lax.bitwise_xor(spot(), partner(k))]


def late_kernel(across_ref, carry_ref, *refs):
    jumps, damp_ref, outs, order = refs[:GROUP], refs[GROUP], refs[GROUP + 1 : -1], refs[-1]
    split = across_ref.shape[0]
    news_of(split, carry_ref, jumps, damp_ref, order)
    for k, out in enumerate(outs):
        value = order[lax.bitwise_xor(spot(), partner(k))]
        if k == 1:
            out[:split] = across_ref[...]
            out[split:] = value
        else:
            out[...] = value


def write(whole, out, sem):
    copy = pltpu.make_async_copy(whole, out, sem)
    copy.start()
    copy.wait()


def first_kernel(kept, out, whole, sem):
    @pl.when(lax.axis_index("tm") == 0)
    def _():
        for layer in range(out.shape[1]):
            pair = load(kept, layer)
            for c in range(3):
                join_rows(whole, (c, layer), pair[c])
        write(whole, out, sem)


def pass_kernel(back_ref, side_ref, back, side):
    back[...] = back_ref[...]
    side[...] = side_ref[...]


def put(whole, held):
    layers, rows = whole.shape[1], whole.shape[2] // 2
    split = (layers - STAGES) // 2
    near = near_side()
    for k, first, piece in held:
        chunk = chunk_of(k)
        for odd in (0, 1):

            @pl.when(chunk // 2 == odd)
            def _():
                for j in range(first, first + piece.shape[0]):
                    if j < split:
                        slot = lax.rem(chunk, 2) * split + j
                    else:
                        slot = layers - 1 - (lax.rem(chunk, 2) * (STAGES // 2) + j - split)
                    layer = slot + near * (layers - 1 - 2 * slot)
                    for c in range(3):
                        whole[c, layer, pl.ds(odd, rows, stride=2), :] = piece[j - first, c]


def gather_kernel(early_own, late_own, across, early_back, early_side, whole):
    split = early_own.shape[0]
    held = ((0, 0, early_own), (0, split, late_own), (1, 0, across))
    put(whole, held + ((2, 0, early_back), (3, 0, early_side)))


def finish_kernel(gathered, late_back, late_side, _, out, whole, sem):
    split = (whole.shape[1] - STAGES) // 2

    @pl.when(lax.axis_index("tm") != 0)
    def _():
        whole[...] = gathered[...]
        put(whole, ((2, split, late_back), (3, split, late_side)))
        write(whole, out, sem)


def shards(states, rate):
    slices = lax.axis_size("tm")
    slabs = lax.axis_size("gz")
    groups = slices // GROUP
    own = states[0]
    layers, rows, width = own.shape[1:]
    middle_layers = layers - 2 * STAGES
    tile = (3, 2, rows // 2, width)
    face = f32(3, STAGES, rows, width)
    sizes = ((layers - STAGES) // 2, STAGES // 2)
    team = lax.axis_index("tm") // GROUP

    def halo(value, pairs):
        return lax.ppermute(value, "gz", [(i, j % slabs) for i, j in pairs])

    def exchange(value, k):
        return lax.ppermute(value, "tm", [(i, i ^ partner(k)) for i in range(slices)])

    def swap(parts):
        return [parts[0]] + [exchange(parts[k], k) for k in range(1, GROUP)]

    def onward(value, distance):
        step = distance * GROUP
        return lax.ppermute(value, "tm", [(i, (i + step) % slices) for i in range(slices)])

    far_face, near_face = call(faces_kernel, [face, face], own)
    near_face = halo(near_face, [(i, i ^ 1) for i in range(slabs)])
    far_face = halo(far_face, [(i, i + 1 if i % 2 else i - 1 + slabs) for i in range(slabs)])
    row = (rows // 2, width)
    edges, middle, faded, damp, kept = call(
        inside_kernel,
        [
            f32(STAGES, 2, 3, *tile),
            f32(middle_layers, *tile),
            f32(2, STAGES, *tile),
            f32(sum(sizes), *row),
            f32(layers, *tile),
        ],
        own, rate,
        scratch=[
            pltpu.VMEM((2, 2, STAGES, *row), jnp.float32),
            pltpu.VMEM((2, layers - STAGES, *row), jnp.float32),
        ]
        + [pltpu.VMEM((layers, *tile), jnp.float32)] * 3,
        flops=1 << 26,
    )
    strip = pltpu.VMEM((STAGES + 1, STAGES, *tile), jnp.float32)
    shares = [f32(size, 3, *row) for size in sizes]
    whole_share = f32(sum(sizes), 3, *row)

    def after(value, earlier):
        return lax.optimization_barrier((value, earlier))[0]

    halves = []
    for far, face_ref in enumerate((near_face, far_face)):
        jumps = call(
            functools.partial(jumps_kernel, far), [shares[far]] * GROUP,
            face_ref, edges, middle, faded,
            scratch=[strip, pltpu.VMEM((2, 2 * sizes[far], 3, *row), jnp.float32)],
            flops=BUSY,
        )
        halves.append(swap(jumps))

    orders = [pltpu.VMEM((GROUP, *share.shape), jnp.float32) for share in shares]
    carries, total = [], halves[1][0]
    for far, jumps in enumerate(halves):
        jumps[0] = after(jumps[0], total)
        first = far * sizes[0]
        total = call(
            functools.partial(total_kernel, first), shares[far], *jumps, damp,
            scratch=[orders[far]],
            flops=BUSY,
        )
        carry = onward(total, 1)
        if groups > 2:
            carry = jnp.where(team < 1, 0.0, carry)
            fade, distance = damp[first : first + sizes[far], None] ** GROUP, 1
            while distance < groups - 1:
                carry = carry + jnp.where(team < distance, 0.0, fade * onward(carry, distance))
                distance, fade = 2 * distance, fade * fade
        carries.append(carry)
    early = call(
        early_kernel, [shares[0]] * GROUP, carries[0], *halves[0], damp, scratch=[orders[0]],
        flops=BUSY,
    )
    back, side = exchange(early[2], 2), exchange(early[3], 3)
    late = call(
        late_kernel, [shares[1], whole_share, shares[1], shares[1]],
        early[1], carries[1], *halves[1], damp,
        scratch=[orders[1]],
        flops=BUSY,
    )
    late = [*late[:2], *call(pass_kernel, [shares[1]] * 2, *late[2:], flops=BUSY)]
    late_own, across, late_back, late_side = swap(late)
    gathered = call(
        gather_kernel, f32(*own.shape), early[0], late_own, across, back, side, flops=BUSY
    )
    pieces = [gathered, late_back, late_side]
    whole = [pltpu.VMEM(own.shape, jnp.float32), pltpu.SemaphoreType.DMA]
    updated = pl.pallas_call(
        first_kernel,
        out_shape=f32(*own.shape),
        in_specs=[VMEM],
        out_specs=ANY,
        scratch_shapes=whole,
        compiler_params=PARAMS,
        cost_estimate=pl.CostEstimate(flops=BUSY, bytes_accessed=1 << 20, transcendentals=0),
    )(after(kept, gathered))
    updated = pl.pallas_call(
        finish_kernel,
        out_shape=f32(*own.shape),
        in_specs=[VMEM] * len(pieces) + [ANY],
        out_specs=ANY,
        scratch_shapes=whole,
        input_output_aliases={len(pieces): 0},
        compiler_params=PARAMS,
    )(*pieces, updated)
    return updated[None]


def solution(mesh):
    return jax.shard_map(
        shards,
        mesh=mesh,
        in_specs=(P("tm", None, "gz", None, None), P("gz", None, None)),
        out_specs=P("tm", None, "gz", None, None),
        check_vma=False,
    )
```

```python
import functools

import jax
import jax.numpy as jnp
from jax import lax
from jax.experimental import pallas as pl
from jax.experimental.pallas import tpu as pltpu
from jax.sharding import PartitionSpec as P

STEPS = 2
STAGES = 3 * STEPS
BUSY = 1 << 32
GROUP = 4
VISCOSITY = 0.05
TIME_STEP = 0.2
MIX = ((1.0, None), (0.25, 0.75), (2.0 / 3.0, 1.0 / 3.0))
VMEM = pl.BlockSpec(memory_space=pltpu.VMEM)
ANY = pl.BlockSpec(memory_space=pl.ANY)
PARAMS = pltpu.CompilerParams(vmem_limit_bytes=16 * 1024 * 1024)


def call(kernel, out_shape, *args, scratch=(), flops=None):
    cost = None
    if flops is not None:
        cost = pl.CostEstimate(flops=flops, bytes_accessed=1 << 20, transcendentals=0)
    return pl.pallas_call(
        kernel,
        out_shape=out_shape,
        in_specs=[VMEM] * len(args),
        out_specs=jax.tree.map(lambda _: VMEM, out_shape),
        scratch_shapes=list(scratch),
        compiler_params=PARAMS,
        cost_estimate=cost,
    )(*args)


def f32(*shape):
    return jax.ShapeDtypeStruct(shape, jnp.float32)


def partner(k):
    return (GROUP - k) % GROUP


def spot():
    return lax.rem(lax.axis_index("tm"), GROUP)


def chunk_of(k):
    return lax.bitwise_xor(spot(), partner(k))


def share_of(ref, k, count):
    chunk = chunk_of(k)
    return ref[chunk // 2, pl.ds(lax.rem(chunk, 2) * count, count)]


def near_side():
    return 1 - lax.rem(lax.axis_index("gz"), 2)


def split_rows(ref, *lead):
    half = ref.shape[-2] // 2
    return [ref[(*lead, pl.ds(odd, half, stride=2), slice(None))] for odd in (0, 1)]


def join_rows(ref, lead, pair):
    half = ref.shape[-2] // 2
    for odd in (0, 1):
        ref[(*lead, pl.ds(odd, half, stride=2), slice(None))] = pair[odd]


def load(ref, *lead):
    return [[ref[(*lead, c, odd)] for odd in (0, 1)] for c in range(3)]


def store(ref, lead, value):
    for c in range(3):
        for odd in (0, 1):
            ref[(*lead, c, odd)] = value[c][odd]


def advance(last, here, ahead, alpha, upward=1.0):
    diffuse = alpha * TIME_STEP * VISCOSITY
    carry = alpha * TIME_STEP * 0.5
    result = [[None, None] for _ in range(3)]
    for odd in (0, 1):
        speed = [here[0][odd] * carry, here[1][odd] * carry, here[2][odd] * (carry * upward)]
        to_next = [diffuse - s for s in speed]
        to_last = [diffuse + s for s in speed]
        for c in range(3):
            w = here[c][odd]
            rows, width = w.shape
            other = here[c][1 - odd]
            if odd:
                y_next, y_last = pltpu.roll(other, rows - 1, 0), other
            else:
                y_next, y_last = other, pltpu.roll(other, 1, 0)
            total = (alpha - 6.0 * diffuse) * w
            total = total + (
                to_next[0] * pltpu.roll(w, width - 1, 1) + to_last[0] * pltpu.roll(w, 1, 1)
            )
            total = total + (to_next[1] * y_next + to_last[1] * y_last)
            total = total + (to_next[2] * ahead[c][odd] + to_last[2] * last[c][odd])
            result[c][odd] = total
    return result


def blend(new, beta, base):
    return [[new[c][odd] + beta * base[c][odd] for odd in (0, 1)] for c in range(3)]


def faces_kernel(own_ref, far_ref, near_ref):
    layers, width = own_ref.shape[1], near_ref.shape[1]
    near = near_side()
    top = layers - width
    far_ref[...] = own_ref[:, pl.ds((1 - near) * top, width)]
    near_ref[...] = own_ref[:, pl.ds(near * top, width)]


def inside_kernel(own_ref, rate_ref, edges, middle, faded, damp_ref, kept, damps, inner, *fields):
    layers = own_ref.shape[1]
    near = near_side()
    slices = lax.axis_size("tm")
    keep = (lax.axis_index("tm") != 0).astype(jnp.float32)

    def side_of(z):
        return (0, z) if z < layers - 1 - z else (1, layers - 1 - z)

    def from_near(z):
        return z - STAGES + near * (layers - 1 - 2 * z)

    def save(stage, z, value):
        low, high = z - stage, layers - 1 - stage - z
        if low < 3:
            store(edges, (stage, 0, low), value)
        if high < 3:
            store(edges, (stage, 1, high), value)

    for z in range(layers):
        side, slot = side_of(z)
        damp = [jnp.exp(r * (-1.0 / slices)) for r in split_rows(rate_ref, z)]
        start = [split_rows(own_ref, c, z) for c in range(3)]
        store(fields[0], (z,), start)
        store(kept, (z,), start)
        save(0, z, start)
        lost = [[damp[odd] * keep * start[c][odd] for odd in (0, 1)] for c in range(3)]
        if slot < STAGES:
            store(faded, (side, slot), lost)
            for odd in (0, 1):
                damps[side, odd, slot] = damp[odd]
        else:
            store(middle, (from_near(z),), lost)
            for odd in (0, 1):
                inner[odd, STAGES + from_near(z)] = damp[odd]

    for stage in range(1, STAGES + 1):
        kind = (stage - 1) % 3
        alpha, beta = MIX[kind]
        source, target = fields[kind], fields[(kind + 1) % 3]
        below, here = load(source, stage - 1), load(source, stage)
        for z in range(stage, layers - stage):
            above = load(source, z + 1)
            new = advance(below, here, above, alpha)
            if beta is not None:
                new = blend(new, beta, load(fields[0], z))
            if stage < STAGES:
                store(target, (z,), new)
                save(stage, z, new)
            else:
                lost = load(middle, from_near(z))
                store(
                    middle,
                    (from_near(z),),
                    [[new[c][odd] - lost[c][odd] for odd in (0, 1)] for c in range(3)],
                )
            below, here = here, above

    for odd in (0, 1):
        inner[odd, :STAGES] = damps[near, odd]
    early, late = inner.shape[1] // 2, STAGES // 2
    damp_ref[:early] = share_of(inner, 0, early)
    damp_ref[early:] = share_of(damps.at[1 - near], 0, late)


def border(side, face_ref, edges, middle, faded, jumps, strip):
    width = STAGES
    upward = 1.0 - 2.0 * side.astype(jnp.float32)
    for slot in range(width):
        layer = slot + side * (width - 1 - 2 * slot)
        store(strip, (0, slot), [split_rows(face_ref, c, layer) for c in range(3)])

    def at(stage, slot):
        if slot < width:
            return load(strip, stage, slot)
        return load(edges, stage, side, slot - width)

    def step(turn, _):
        for kind, (alpha, beta) in enumerate(MIX):
            stage = 3 * turn + kind
            last, here = at(stage, 0), at(stage, 1)
            for slot in range(width):
                ahead = at(stage, slot + 2)
                new = advance(last, here, ahead, alpha, upward)
                if beta is not None:
                    new = blend(new, beta, at(3 * turn, slot + 1 + kind))
                store(strip, (stage + 1, slot), new)
                last, here = here, ahead
        return 0

    lax.fori_loop(0, STEPS, step, 0)
    for slot in range(jumps.shape[1]):
        if slot < width:
            end, lost = load(strip, STAGES, slot), load(faded, side, slot)
            jump = [[end[c][odd] - lost[c][odd] for odd in (0, 1)] for c in range(3)]
        else:
            jump = load(middle, slot - width)
        for odd in (0, 1):
            for c in range(3):
                jumps[odd, slot, c] = jump[c][odd]


def jumps_kernel(far, face_ref, edges, middle, faded, *refs):
    outs, strip, jumps = refs[:GROUP], refs[-2], refs[-1]
    side = far + (1 - 2 * far) * near_side()
    border(side, face_ref, edges, middle, faded, jumps, strip)
    for k, out in enumerate(outs):
        out[...] = share_of(jumps, k, out.shape[0])


def run(order, damp, total):
    for j in range(GROUP):
        jump = order[j]
        order[j] = total
        total = damp * total + jump
    return total


def total_of(jumps, damp):
    total = None
    for slice_ in range(GROUP):
        jump = jumps[slice_]
        total = jump if total is None else damp[:, None] * total + jump
    return total


def total_kernel(first, *refs):
    jumps, (damp_ref, out, order) = refs[:GROUP], refs[GROUP:]
    for k in range(GROUP):
        order[lax.bitwise_xor(spot(), partner(k))] = jumps[k][...]
    out[...] = total_of(order, damp_ref[first : first + out.shape[0]])


def news_of(first, carry_ref, jumps, damp_ref, order):
    for k in range(GROUP):
        order[lax.bitwise_xor(spot(), partner(k))] = jumps[k][...]
    damp = damp_ref[first : first + carry_ref.shape[0]][:, None]
    run(order, damp, jnp.where(lax.axis_index("tm") < GROUP, 0.0, carry_ref[...]))


def early_kernel(carry_ref, *refs):
    jumps, damp_ref, outs, order = refs[:GROUP], refs[GROUP], refs[GROUP + 1 : -1], refs[-1]
    news_of(0, carry_ref, jumps, damp_ref, order)
    for k, out in enumerate(outs):
        out[...] = order[lax.bitwise_xor(spot(), partner(k))]


def late_kernel(across_ref, back_ref, carry_ref, *refs):
    jumps, damp_ref, outs, order = refs[:GROUP], refs[GROUP], refs[GROUP + 1 : -1], refs[-1]
    split = across_ref.shape[0]
    news_of(split, carry_ref, jumps, damp_ref, order)
    for k, out in enumerate(outs):
        value = order[lax.bitwise_xor(spot(), partner(k))]
        if k in (1, 2):
            out[:split] = (across_ref if k == 1 else back_ref)[...]
            out[split:] = value
        else:
            out[...] = value


def write(whole, out, sem):
    copy = pltpu.make_async_copy(whole, out, sem)
    copy.start()
    copy.wait()


def first_kernel(kept, out, whole, sem):
    @pl.when(lax.axis_index("tm") == 0)
    def _():
        for layer in range(out.shape[1]):
            pair = load(kept, layer)
            for c in range(3):
                join_rows(whole, (c, layer), pair[c])
        write(whole, out, sem)


def pass_kernel(side_ref, side):
    side[...] = side_ref[...]


def put(whole, held):
    layers, rows = whole.shape[1], whole.shape[2] // 2
    split = (layers - STAGES) // 2
    near = near_side()
    for k, first, piece in held:
        chunk = chunk_of(k)
        for odd in (0, 1):

            @pl.when(chunk // 2 == odd)
            def _():
                for j in range(first, first + piece.shape[0]):
                    if j < split:
                        slot = lax.rem(chunk, 2) * split + j
                    else:
                        slot = layers - 1 - (lax.rem(chunk, 2) * (STAGES // 2) + j - split)
                    layer = slot + near * (layers - 1 - 2 * slot)
                    for c in range(3):
                        whole[c, layer, pl.ds(odd, rows, stride=2), :] = piece[j - first, c]


def gather_kernel(early_own, late_own, across, back, early_side, whole):
    split = early_own.shape[0]
    held = ((0, 0, early_own), (0, split, late_own), (1, 0, across), (3, 0, early_side))
    put(whole, held + ((2, 0, back),))


def finish_kernel(gathered, late_side, _, out, whole, sem):
    split = (whole.shape[1] - STAGES) // 2

    @pl.when(lax.axis_index("tm") != 0)
    def _():
        whole[...] = gathered[...]
        put(whole, ((3, split, late_side),))
        write(whole, out, sem)


def shards(states, rate):
    slices = lax.axis_size("tm")
    slabs = lax.axis_size("gz")
    groups = slices // GROUP
    own = states[0]
    layers, rows, width = own.shape[1:]
    middle_layers = layers - 2 * STAGES
    tile = (3, 2, rows // 2, width)
    face = f32(3, STAGES, rows, width)
    sizes = ((layers - STAGES) // 2, STAGES // 2)
    team = lax.axis_index("tm") // GROUP

    def halo(value, pairs):
        return lax.ppermute(value, "gz", [(i, j % slabs) for i, j in pairs])

    def exchange(value, k):
        return lax.ppermute(value, "tm", [(i, i ^ partner(k)) for i in range(slices)])

    def swap(parts):
        return [parts[0]] + [exchange(parts[k], k) for k in range(1, GROUP)]

    def onward(value, distance):
        step = distance * GROUP
        return lax.ppermute(value, "tm", [(i, (i + step) % slices) for i in range(slices)])

    far_face, near_face = call(faces_kernel, [face, face], own)
    near_face = halo(near_face, [(i, i ^ 1) for i in range(slabs)])
    far_face = halo(far_face, [(i, i + 1 if i % 2 else i - 1 + slabs) for i in range(slabs)])
    row = (rows // 2, width)
    edges, middle, faded, damp, kept = call(
        inside_kernel,
        [
            f32(STAGES, 2, 3, *tile),
            f32(middle_layers, *tile),
            f32(2, STAGES, *tile),
            f32(sum(sizes), *row),
            f32(layers, *tile),
        ],
        own, rate,
        scratch=[
            pltpu.VMEM((2, 2, STAGES, *row), jnp.float32),
            pltpu.VMEM((2, layers - STAGES, *row), jnp.float32),
        ]
        + [pltpu.VMEM((layers, *tile), jnp.float32)] * 3,
        flops=1 << 26,
    )
    strip = pltpu.VMEM((STAGES + 1, STAGES, *tile), jnp.float32)
    shares = [f32(size, 3, *row) for size in sizes]
    whole_share = f32(sum(sizes), 3, *row)

    def after(value, earlier):
        return lax.optimization_barrier((value, earlier))[0]

    halves = []
    for far, face_ref in enumerate((near_face, far_face)):
        jumps = call(
            functools.partial(jumps_kernel, far), [shares[far]] * GROUP,
            face_ref, edges, middle, faded,
            scratch=[strip, pltpu.VMEM((2, 2 * sizes[far], 3, *row), jnp.float32)],
            flops=BUSY,
        )
        halves.append(swap(jumps))

    orders = [pltpu.VMEM((GROUP, *share.shape), jnp.float32) for share in shares]
    carries, total = [], halves[1][0]
    for far, jumps in enumerate(halves):
        jumps[0] = after(jumps[0], total)
        first = far * sizes[0]
        total = call(
            functools.partial(total_kernel, first), shares[far], *jumps, damp,
            scratch=[orders[far]],
            flops=BUSY,
        )
        carry = onward(total, 1)
        if groups > 2:
            carry = jnp.where(team < 1, 0.0, carry)
            fade, distance = damp[first : first + sizes[far], None] ** GROUP, 1
            while distance < groups - 1:
                carry = carry + jnp.where(team < distance, 0.0, fade * onward(carry, distance))
                distance, fade = 2 * distance, fade * fade
        carries.append(carry)
    early = call(
        early_kernel, [shares[0]] * GROUP, carries[0], *halves[0], damp, scratch=[orders[0]],
        flops=BUSY,
    )
    side = exchange(early[3], 3)
    late = call(
        late_kernel, [shares[1], whole_share, whole_share, shares[1]],
        early[1], early[2], carries[1], *halves[1], damp,
        scratch=[orders[1]],
        flops=BUSY,
    )
    late = [*late[:3], call(pass_kernel, shares[1], late[3], flops=BUSY)]
    late_own, across, back, late_side = swap(late)
    gathered = call(
        gather_kernel, f32(*own.shape), early[0], late_own, across, back, side, flops=BUSY
    )
    pieces = [gathered, late_side]
    whole = [pltpu.VMEM(own.shape, jnp.float32), pltpu.SemaphoreType.DMA]
    updated = pl.pallas_call(
        first_kernel,
        out_shape=f32(*own.shape),
        in_specs=[VMEM],
        out_specs=ANY,
        scratch_shapes=whole,
        compiler_params=PARAMS,
        cost_estimate=pl.CostEstimate(flops=BUSY, bytes_accessed=1 << 20, transcendentals=0),
    )(after(kept, early[0]))
    updated = pl.pallas_call(
        finish_kernel,
        out_shape=f32(*own.shape),
        in_specs=[VMEM] * len(pieces) + [ANY],
        out_specs=ANY,
        scratch_shapes=whole,
        input_output_aliases={len(pieces): 0},
        compiler_params=PARAMS,
    )(*pieces, updated)
    return updated[None]


def solution(mesh):
    return jax.shard_map(
        shards,
        mesh=mesh,
        in_specs=(P("tm", None, "gz", None, None), P("gz", None, None)),
        out_specs=P("tm", None, "gz", None, None),
        check_vma=False,
    )
```

```python
import functools

import jax
import jax.numpy as jnp
from jax import lax
from jax.experimental import pallas as pl
from jax.experimental.pallas import tpu as pltpu
from jax.sharding import PartitionSpec as P

STEPS = 2
STAGES = 3 * STEPS
BUSY = 1 << 32
GROUP = 4
VISCOSITY = 0.05
TIME_STEP = 0.2
MIX = ((1.0, None), (0.25, 0.75), (2.0 / 3.0, 1.0 / 3.0))
VMEM = pl.BlockSpec(memory_space=pltpu.VMEM)
ANY = pl.BlockSpec(memory_space=pl.ANY)
PARAMS = pltpu.CompilerParams(vmem_limit_bytes=16 * 1024 * 1024)


def call(kernel, out_shape, *args, scratch=(), flops=None):
    cost = None
    if flops is not None:
        cost = pl.CostEstimate(flops=flops, bytes_accessed=1 << 20, transcendentals=0)
    return pl.pallas_call(
        kernel,
        out_shape=out_shape,
        in_specs=[VMEM] * len(args),
        out_specs=jax.tree.map(lambda _: VMEM, out_shape),
        scratch_shapes=list(scratch),
        compiler_params=PARAMS,
        cost_estimate=cost,
    )(*args)


def f32(*shape):
    return jax.ShapeDtypeStruct(shape, jnp.float32)


def partner(k):
    return (0, 2, 3, 1)[k]


def spot():
    return lax.rem(lax.axis_index("tm"), GROUP)


def chunk_of(k):
    return lax.bitwise_xor(spot(), partner(k))


def share_of(ref, k, count):
    chunk = chunk_of(k)
    return ref[chunk // 2, pl.ds(lax.rem(chunk, 2) * count, count)]


def near_side():
    return 1 - lax.rem(lax.axis_index("gz"), 2)


def split_rows(ref, *lead):
    half = ref.shape[-2] // 2
    return [ref[(*lead, pl.ds(odd, half, stride=2), slice(None))] for odd in (0, 1)]


def join_rows(ref, lead, pair):
    half = ref.shape[-2] // 2
    for odd in (0, 1):
        ref[(*lead, pl.ds(odd, half, stride=2), slice(None))] = pair[odd]


def load(ref, *lead):
    return [[ref[(*lead, c, odd)] for odd in (0, 1)] for c in range(3)]


def store(ref, lead, value):
    for c in range(3):
        for odd in (0, 1):
            ref[(*lead, c, odd)] = value[c][odd]


def advance(last, here, ahead, alpha, upward=1.0):
    diffuse = alpha * TIME_STEP * VISCOSITY
    carry = alpha * TIME_STEP * 0.5
    result = [[None, None] for _ in range(3)]
    for odd in (0, 1):
        speed = [here[0][odd] * carry, here[1][odd] * carry, here[2][odd] * (carry * upward)]
        to_next = [diffuse - s for s in speed]
        to_last = [diffuse + s for s in speed]
        for c in range(3):
            w = here[c][odd]
            rows, width = w.shape
            other = here[c][1 - odd]
            if odd:
                y_next, y_last = pltpu.roll(other, rows - 1, 0), other
            else:
                y_next, y_last = other, pltpu.roll(other, 1, 0)
            total = (alpha - 6.0 * diffuse) * w
            total = total + (
                to_next[0] * pltpu.roll(w, width - 1, 1) + to_last[0] * pltpu.roll(w, 1, 1)
            )
            total = total + (to_next[1] * y_next + to_last[1] * y_last)
            total = total + (to_next[2] * ahead[c][odd] + to_last[2] * last[c][odd])
            result[c][odd] = total
    return result


def blend(new, beta, base):
    return [[new[c][odd] + beta * base[c][odd] for odd in (0, 1)] for c in range(3)]


def faces_kernel(own_ref, far_ref, near_ref):
    layers, width = own_ref.shape[1], near_ref.shape[1]
    near = near_side()
    top = layers - width
    far_ref[...] = own_ref[:, pl.ds((1 - near) * top, width)]
    near_ref[...] = own_ref[:, pl.ds(near * top, width)]


def inside_kernel(own_ref, rate_ref, edges, middle, faded, damp_ref, kept, damps, inner, *fields):
    layers = own_ref.shape[1]
    near = near_side()
    slices = lax.axis_size("tm")
    keep = (lax.axis_index("tm") != 0).astype(jnp.float32)

    def side_of(z):
        return (0, z) if z < layers - 1 - z else (1, layers - 1 - z)

    def from_near(z):
        return z - STAGES + near * (layers - 1 - 2 * z)

    def save(stage, z, value):
        low, high = z - stage, layers - 1 - stage - z
        if low < 3:
            store(edges, (stage, 0, low), value)
        if high < 3:
            store(edges, (stage, 1, high), value)

    for z in range(layers):
        side, slot = side_of(z)
        damp = [jnp.exp(r * (-1.0 / slices)) for r in split_rows(rate_ref, z)]
        start = [split_rows(own_ref, c, z) for c in range(3)]
        store(fields[0], (z,), start)
        store(kept, (z,), start)
        save(0, z, start)
        lost = [[damp[odd] * keep * start[c][odd] for odd in (0, 1)] for c in range(3)]
        if slot < STAGES:
            store(faded, (side, slot), lost)
            for odd in (0, 1):
                damps[side, odd, slot] = damp[odd]
        else:
            store(middle, (from_near(z),), lost)
            for odd in (0, 1):
                inner[odd, STAGES + from_near(z)] = damp[odd]

    for stage in range(1, STAGES + 1):
        kind = (stage - 1) % 3
        alpha, beta = MIX[kind]
        source, target = fields[kind], fields[(kind + 1) % 3]
        below, here = load(source, stage - 1), load(source, stage)
        for z in range(stage, layers - stage):
            above = load(source, z + 1)
            new = advance(below, here, above, alpha)
            if beta is not None:
                new = blend(new, beta, load(fields[0], z))
            if stage < STAGES:
                store(target, (z,), new)
                save(stage, z, new)
            else:
                lost = load(middle, from_near(z))
                store(
                    middle,
                    (from_near(z),),
                    [[new[c][odd] - lost[c][odd] for odd in (0, 1)] for c in range(3)],
                )
            below, here = here, above

    for odd in (0, 1):
        inner[odd, :STAGES] = damps[near, odd]
    early, late = inner.shape[1] // 2, STAGES // 2
    damp_ref[:early] = share_of(inner, 0, early)
    damp_ref[early:] = share_of(damps.at[1 - near], 0, late)


def border(side, face_ref, edges, middle, faded, jumps, strip):
    width = STAGES
    upward = 1.0 - 2.0 * side.astype(jnp.float32)
    for slot in range(width):
        layer = slot + side * (width - 1 - 2 * slot)
        store(strip, (0, slot), [split_rows(face_ref, c, layer) for c in range(3)])

    def at(stage, slot):
        if slot < width:
            return load(strip, stage, slot)
        return load(edges, stage, side, slot - width)

    def step(turn, _):
        for kind, (alpha, beta) in enumerate(MIX):
            stage = 3 * turn + kind
            last, here = at(stage, 0), at(stage, 1)
            for slot in range(width):
                ahead = at(stage, slot + 2)
                new = advance(last, here, ahead, alpha, upward)
                if beta is not None:
                    new = blend(new, beta, at(3 * turn, slot + 1 + kind))
                store(strip, (stage + 1, slot), new)
                last, here = here, ahead
        return 0

    lax.fori_loop(0, STEPS, step, 0)
    for slot in range(jumps.shape[1]):
        if slot < width:
            end, lost = load(strip, STAGES, slot), load(faded, side, slot)
            jump = [[end[c][odd] - lost[c][odd] for odd in (0, 1)] for c in range(3)]
        else:
            jump = load(middle, slot - width)
        for odd in (0, 1):
            for c in range(3):
                jumps[odd, slot, c] = jump[c][odd]


def jumps_kernel(far, face_ref, edges, middle, faded, *refs):
    outs, strip, jumps = refs[:GROUP], refs[-2], refs[-1]
    side = far + (1 - 2 * far) * near_side()
    border(side, face_ref, edges, middle, faded, jumps, strip)
    for k, out in enumerate(outs):
        out[...] = share_of(jumps, k, out.shape[0])


def run(order, damp, total):
    for j in range(GROUP):
        jump = order[j]
        order[j] = total
        total = damp * total + jump
    return total


def total_of(jumps, damp):
    total = None
    for slice_ in range(GROUP):
        jump = jumps[slice_]
        total = jump if total is None else damp[:, None] * total + jump
    return total


def total_kernel(first, *refs):
    jumps, (damp_ref, out, order) = refs[:GROUP], refs[GROUP:]
    for k in range(GROUP):
        order[lax.bitwise_xor(spot(), partner(k))] = jumps[k][...]
    out[...] = total_of(order, damp_ref[first : first + out.shape[0]])


def news_of(first, carry_ref, jumps, damp_ref, order):
    for k in range(GROUP):
        order[lax.bitwise_xor(spot(), partner(k))] = jumps[k][...]
    damp = damp_ref[first : first + carry_ref.shape[0]][:, None]
    run(order, damp, jnp.where(lax.axis_index("tm") < GROUP, 0.0, carry_ref[...]))


def early_kernel(carry_ref, *refs):
    jumps, damp_ref, outs, order = refs[:GROUP], refs[GROUP], refs[GROUP + 1 : -1], refs[-1]
    news_of(0, carry_ref, jumps, damp_ref, order)
    for k, out in enumerate(outs):
        out[...] = order[lax.bitwise_xor(spot(), partner(k))]


def late_kernel(across_ref, back_ref, carry_ref, *refs):
    jumps, damp_ref, outs, order = refs[:GROUP], refs[GROUP], refs[GROUP + 1 : -1], refs[-1]
    split = across_ref.shape[0]
    news_of(split, carry_ref, jumps, damp_ref, order)
    for k, out in enumerate(outs):
        value = order[lax.bitwise_xor(spot(), partner(k))]
        if k in (1, 2):
            out[:split] = (across_ref if k == 1 else back_ref)[...]
            out[split:] = value
        else:
            out[...] = value


def write(whole, out, sem):
    copy = pltpu.make_async_copy(whole, out, sem)
    copy.start()
    copy.wait()


def first_kernel(kept, out, whole, sem):
    @pl.when(lax.axis_index("tm") == 0)
    def _():
        for layer in range(out.shape[1]):
            pair = load(kept, layer)
            for c in range(3):
                join_rows(whole, (c, layer), pair[c])
        write(whole, out, sem)


def pass_kernel(side_ref, side):
    side[...] = side_ref[...]


def put(whole, held):
    layers, rows = whole.shape[1], whole.shape[2] // 2
    split = (layers - STAGES) // 2
    near = near_side()
    for k, first, piece in held:
        chunk = chunk_of(k)
        for odd in (0, 1):

            @pl.when(chunk // 2 == odd)
            def _():
                for j in range(first, first + piece.shape[0]):
                    if j < split:
                        slot = lax.rem(chunk, 2) * split + j
                    else:
                        slot = layers - 1 - (lax.rem(chunk, 2) * (STAGES // 2) + j - split)
                    layer = slot + near * (layers - 1 - 2 * slot)
                    for c in range(3):
                        whole[c, layer, pl.ds(odd, rows, stride=2), :] = piece[j - first, c]


def gather_kernel(early_own, late_own, across, back, early_side, whole):
    split = early_own.shape[0]
    held = ((0, 0, early_own), (0, split, late_own), (1, 0, across), (3, 0, early_side))
    put(whole, held + ((2, 0, back),))


def finish_kernel(gathered, late_side, _, out, whole, sem):
    split = (whole.shape[1] - STAGES) // 2

    @pl.when(lax.axis_index("tm") != 0)
    def _():
        whole[...] = gathered[...]
        put(whole, ((3, split, late_side),))
        write(whole, out, sem)


def shards(states, rate):
    slices = lax.axis_size("tm")
    slabs = lax.axis_size("gz")
    groups = slices // GROUP
    own = states[0]
    layers, rows, width = own.shape[1:]
    middle_layers = layers - 2 * STAGES
    tile = (3, 2, rows // 2, width)
    face = f32(3, STAGES, rows, width)
    sizes = ((layers - STAGES) // 2, STAGES // 2)
    team = lax.axis_index("tm") // GROUP

    def halo(value, pairs):
        return lax.ppermute(value, "gz", [(i, j % slabs) for i, j in pairs])

    def exchange(value, k):
        return lax.ppermute(value, "tm", [(i, i ^ partner(k)) for i in range(slices)])

    def swap(parts):
        return [parts[0]] + [exchange(parts[k], k) for k in range(1, GROUP)]

    def onward(value, distance):
        step = distance * GROUP
        return lax.ppermute(value, "tm", [(i, (i + step) % slices) for i in range(slices)])

    far_face, near_face = call(faces_kernel, [face, face], own)
    near_face = halo(near_face, [(i, i ^ 1) for i in range(slabs)])
    far_face = halo(far_face, [(i, i + 1 if i % 2 else i - 1 + slabs) for i in range(slabs)])
    row = (rows // 2, width)
    edges, middle, faded, damp, kept = call(
        inside_kernel,
        [
            f32(STAGES, 2, 3, *tile),
            f32(middle_layers, *tile),
            f32(2, STAGES, *tile),
            f32(sum(sizes), *row),
            f32(layers, *tile),
        ],
        own, rate,
        scratch=[
            pltpu.VMEM((2, 2, STAGES, *row), jnp.float32),
            pltpu.VMEM((2, layers - STAGES, *row), jnp.float32),
        ]
        + [pltpu.VMEM((layers, *tile), jnp.float32)] * 3,
        flops=1 << 26,
    )
    strip = pltpu.VMEM((STAGES + 1, STAGES, *tile), jnp.float32)
    shares = [f32(size, 3, *row) for size in sizes]
    whole_share = f32(sum(sizes), 3, *row)

    def after(value, earlier):
        return lax.optimization_barrier((value, earlier))[0]

    halves = []
    for far, face_ref in enumerate((near_face, far_face)):
        jumps = call(
            functools.partial(jumps_kernel, far), [shares[far]] * GROUP,
            face_ref, edges, middle, faded,
            scratch=[strip, pltpu.VMEM((2, 2 * sizes[far], 3, *row), jnp.float32)],
            flops=BUSY,
        )
        halves.append(swap(jumps))

    orders = [pltpu.VMEM((GROUP, *share.shape), jnp.float32) for share in shares]
    carries, total = [], halves[1][0]
    for far, jumps in enumerate(halves):
        jumps[0] = after(jumps[0], total)
        first = far * sizes[0]
        total = call(
            functools.partial(total_kernel, first), shares[far], *jumps, damp,
            scratch=[orders[far]],
            flops=BUSY,
        )
        carry = onward(total, 1)
        if groups > 2:
            carry = jnp.where(team < 1, 0.0, carry)
            fade, distance = damp[first : first + sizes[far], None] ** GROUP, 1
            while distance < groups - 1:
                carry = carry + jnp.where(team < distance, 0.0, fade * onward(carry, distance))
                distance, fade = 2 * distance, fade * fade
        carries.append(carry)
    early = call(
        early_kernel, [shares[0]] * GROUP, carries[0], *halves[0], damp, scratch=[orders[0]],
        flops=BUSY,
    )
    side = exchange(early[3], 3)
    late = call(
        late_kernel, [shares[1], whole_share, whole_share, shares[1]],
        early[1], early[2], carries[1], *halves[1], damp,
        scratch=[orders[1]],
        flops=BUSY,
    )
    late = [*late[:3], call(pass_kernel, shares[1], late[3], flops=BUSY)]
    late_own, across, back, late_side = swap(late)
    gathered = call(
        gather_kernel, f32(*own.shape), early[0], late_own, across, back, side, flops=BUSY
    )
    pieces = [gathered, late_side]
    whole = [pltpu.VMEM(own.shape, jnp.float32), pltpu.SemaphoreType.DMA]
    updated = pl.pallas_call(
        first_kernel,
        out_shape=f32(*own.shape),
        in_specs=[VMEM],
        out_specs=ANY,
        scratch_shapes=whole,
        compiler_params=PARAMS,
        cost_estimate=pl.CostEstimate(flops=BUSY, bytes_accessed=1 << 20, transcendentals=0),
    )(after(kept, early[0]))
    updated = pl.pallas_call(
        finish_kernel,
        out_shape=f32(*own.shape),
        in_specs=[VMEM] * len(pieces) + [ANY],
        out_specs=ANY,
        scratch_shapes=whole,
        input_output_aliases={len(pieces): 0},
        compiler_params=PARAMS,
    )(*pieces, updated)
    return updated[None]


def solution(mesh):
    return jax.shard_map(
        shards,
        mesh=mesh,
        in_specs=(P("tm", None, "gz", None, None), P("gz", None, None)),
        out_specs=P("tm", None, "gz", None, None),
        check_vma=False,
    )
```

```python
import functools

import jax
import jax.numpy as jnp
from jax import lax
from jax.experimental import pallas as pl
from jax.experimental.pallas import tpu as pltpu
from jax.sharding import PartitionSpec as P

STEPS = 2
STAGES = 3 * STEPS
BUSY = 1 << 32
GROUP = 4
VISCOSITY = 0.05
TIME_STEP = 0.2
MIX = ((1.0, None), (0.25, 0.75), (2.0 / 3.0, 1.0 / 3.0))
VMEM = pl.BlockSpec(memory_space=pltpu.VMEM)
ANY = pl.BlockSpec(memory_space=pl.ANY)
PARAMS = pltpu.CompilerParams(vmem_limit_bytes=16 * 1024 * 1024)


def call(kernel, out_shape, *args, scratch=(), flops=None):
    cost = None
    if flops is not None:
        cost = pl.CostEstimate(flops=flops, bytes_accessed=1 << 20, transcendentals=0)
    return pl.pallas_call(
        kernel,
        out_shape=out_shape,
        in_specs=[VMEM] * len(args),
        out_specs=jax.tree.map(lambda _: VMEM, out_shape),
        scratch_shapes=list(scratch),
        compiler_params=PARAMS,
        cost_estimate=cost,
    )(*args)


def f32(*shape):
    return jax.ShapeDtypeStruct(shape, jnp.float32)


def partner(k):
    return (GROUP - k) % GROUP


def spot():
    return lax.rem(lax.axis_index("tm"), GROUP)


def chunk_of(k):
    return lax.bitwise_xor(spot(), partner(k))


def share_of(ref, k, count):
    chunk = chunk_of(k)
    return ref[chunk // 2, pl.ds(lax.rem(chunk, 2) * count, count)]


def near_side():
    return 1 - lax.rem(lax.axis_index("gz"), 2)


def split_rows(ref, *lead):
    half = ref.shape[-2] // 2
    return [ref[(*lead, pl.ds(odd, half, stride=2), slice(None))] for odd in (0, 1)]


def join_rows(ref, lead, pair):
    half = ref.shape[-2] // 2
    for odd in (0, 1):
        ref[(*lead, pl.ds(odd, half, stride=2), slice(None))] = pair[odd]


def load(ref, *lead):
    return [[ref[(*lead, c, odd)] for odd in (0, 1)] for c in range(3)]


def store(ref, lead, value):
    for c in range(3):
        for odd in (0, 1):
            ref[(*lead, c, odd)] = value[c][odd]


def advance(last, here, ahead, alpha, upward=1.0):
    diffuse = alpha * TIME_STEP * VISCOSITY
    carry = alpha * TIME_STEP * 0.5
    result = [[None, None] for _ in range(3)]
    for odd in (0, 1):
        speed = [here[0][odd] * carry, here[1][odd] * carry, here[2][odd] * (carry * upward)]
        to_next = [diffuse - s for s in speed]
        to_last = [diffuse + s for s in speed]
        for c in range(3):
            w = here[c][odd]
            rows, width = w.shape
            other = here[c][1 - odd]
            if odd:
                y_next, y_last = pltpu.roll(other, rows - 1, 0), other
            else:
                y_next, y_last = other, pltpu.roll(other, 1, 0)
            total = (alpha - 6.0 * diffuse) * w
            total = total + (
                to_next[0] * pltpu.roll(w, width - 1, 1) + to_last[0] * pltpu.roll(w, 1, 1)
            )
            total = total + (to_next[1] * y_next + to_last[1] * y_last)
            total = total + (to_next[2] * ahead[c][odd] + to_last[2] * last[c][odd])
            result[c][odd] = total
    return result


def blend(new, beta, base):
    return [[new[c][odd] + beta * base[c][odd] for odd in (0, 1)] for c in range(3)]


def faces_kernel(own_ref, far_ref, near_ref):
    layers, width = own_ref.shape[1], near_ref.shape[1]
    near = near_side()
    top = layers - width
    far_ref[...] = own_ref[:, pl.ds((1 - near) * top, width)]
    near_ref[...] = own_ref[:, pl.ds(near * top, width)]


def inside_kernel(own_ref, rate_ref, edges, middle, faded, damp_ref, kept, damps, inner, *fields):
    layers = own_ref.shape[1]
    near = near_side()
    slices = lax.axis_size("tm")
    keep = (lax.axis_index("tm") != 0).astype(jnp.float32)

    def side_of(z):
        return (0, z) if z < layers - 1 - z else (1, layers - 1 - z)

    def from_near(z):
        return z - STAGES + near * (layers - 1 - 2 * z)

    def save(stage, z, value):
        low, high = z - stage, layers - 1 - stage - z
        if low < 3:
            store(edges, (stage, 0, low), value)
        if high < 3:
            store(edges, (stage, 1, high), value)

    for z in range(layers):
        side, slot = side_of(z)
        damp = [jnp.exp(r * (-1.0 / slices)) for r in split_rows(rate_ref, z)]
        start = [split_rows(own_ref, c, z) for c in range(3)]
        store(fields[0], (z,), start)
        store(kept, (z,), start)
        save(0, z, start)
        lost = [[damp[odd] * keep * start[c][odd] for odd in (0, 1)] for c in range(3)]
        if slot < STAGES:
            store(faded, (side, slot), lost)
            for odd in (0, 1):
                damps[side, odd, slot] = damp[odd]
        else:
            store(middle, (from_near(z),), lost)
            for odd in (0, 1):
                inner[odd, STAGES + from_near(z)] = damp[odd]

    for stage in range(1, STAGES + 1):
        kind = (stage - 1) % 3
        alpha, beta = MIX[kind]
        source, target = fields[kind], fields[(kind + 1) % 3]
        below, here = load(source, stage - 1), load(source, stage)
        for z in range(stage, layers - stage):
            above = load(source, z + 1)
            new = advance(below, here, above, alpha)
            if beta is not None:
                new = blend(new, beta, load(fields[0], z))
            if stage < STAGES:
                store(target, (z,), new)
                save(stage, z, new)
            else:
                lost = load(middle, from_near(z))
                store(
                    middle,
                    (from_near(z),),
                    [[new[c][odd] - lost[c][odd] for odd in (0, 1)] for c in range(3)],
                )
            below, here = here, above

    for odd in (0, 1):
        inner[odd, :STAGES] = damps[near, odd]
    early, late = inner.shape[1] // 2, STAGES // 2
    damp_ref[:early] = share_of(inner, 0, early)
    damp_ref[early:] = share_of(damps.at[1 - near], 0, late)


def border(side, face_ref, edges, middle, faded, jumps, strip):
    width = STAGES
    upward = 1.0 - 2.0 * side.astype(jnp.float32)
    for slot in range(width):
        layer = slot + side * (width - 1 - 2 * slot)
        store(strip, (0, slot), [split_rows(face_ref, c, layer) for c in range(3)])

    def at(stage, slot):
        if slot < width:
            return load(strip, stage, slot)
        return load(edges, stage, side, slot - width)

    def step(turn, _):
        for kind, (alpha, beta) in enumerate(MIX):
            stage = 3 * turn + kind
            last, here = at(stage, 0), at(stage, 1)
            for slot in range(width):
                ahead = at(stage, slot + 2)
                new = advance(last, here, ahead, alpha, upward)
                if beta is not None:
                    new = blend(new, beta, at(3 * turn, slot + 1 + kind))
                store(strip, (stage + 1, slot), new)
                last, here = here, ahead
        return 0

    for turn in range(STEPS):
        step(turn, 0)
    for slot in range(jumps.shape[1]):
        if slot < width:
            end, lost = load(strip, STAGES, slot), load(faded, side, slot)
            jump = [[end[c][odd] - lost[c][odd] for odd in (0, 1)] for c in range(3)]
        else:
            jump = load(middle, slot - width)
        for odd in (0, 1):
            for c in range(3):
                jumps[odd, slot, c] = jump[c][odd]


def jumps_kernel(far, face_ref, edges, middle, faded, *refs):
    outs, strip, jumps = refs[:GROUP], refs[-2], refs[-1]
    side = far + (1 - 2 * far) * near_side()
    border(side, face_ref, edges, middle, faded, jumps, strip)
    for k, out in enumerate(outs):
        out[...] = share_of(jumps, k, out.shape[0])


def run(order, damp, total):
    for j in range(GROUP):
        jump = order[j]
        order[j] = total
        total = damp * total + jump
    return total


def total_of(jumps, damp):
    total = None
    for slice_ in range(GROUP):
        jump = jumps[slice_]
        total = jump if total is None else damp[:, None] * total + jump
    return total


def total_kernel(first, *refs):
    jumps, (damp_ref, out, order) = refs[:GROUP], refs[GROUP:]
    for k in range(GROUP):
        order[lax.bitwise_xor(spot(), partner(k))] = jumps[k][...]
    out[...] = total_of(order, damp_ref[first : first + out.shape[0]])


def news_of(first, carry_ref, jumps, damp_ref, order):
    for k in range(GROUP):
        order[lax.bitwise_xor(spot(), partner(k))] = jumps[k][...]
    damp = damp_ref[first : first + carry_ref.shape[0]][:, None]
    run(order, damp, jnp.where(lax.axis_index("tm") < GROUP, 0.0, carry_ref[...]))


def early_kernel(carry_ref, *refs):
    jumps, damp_ref, outs, order = refs[:GROUP], refs[GROUP], refs[GROUP + 1 : -1], refs[-1]
    news_of(0, carry_ref, jumps, damp_ref, order)
    for k, out in enumerate(outs):
        out[...] = order[lax.bitwise_xor(spot(), partner(k))]


def late_kernel(across_ref, back_ref, carry_ref, *refs):
    jumps, damp_ref, outs, order = refs[:GROUP], refs[GROUP], refs[GROUP + 1 : -1], refs[-1]
    split = across_ref.shape[0]
    news_of(split, carry_ref, jumps, damp_ref, order)
    for k, out in enumerate(outs):
        value = order[lax.bitwise_xor(spot(), partner(k))]
        if k in (1, 2):
            out[:split] = (across_ref if k == 1 else back_ref)[...]
            out[split:] = value
        else:
            out[...] = value


def write(whole, out, sem):
    copy = pltpu.make_async_copy(whole, out, sem)
    copy.start()
    copy.wait()


def first_kernel(kept, out, whole, sem):
    @pl.when(lax.axis_index("tm") == 0)
    def _():
        for layer in range(out.shape[1]):
            pair = load(kept, layer)
            for c in range(3):
                join_rows(whole, (c, layer), pair[c])
        write(whole, out, sem)


def pass_kernel(side_ref, side):
    side[...] = side_ref[...]


def put(whole, held):
    layers, rows = whole.shape[1], whole.shape[2] // 2
    split = (layers - STAGES) // 2
    near = near_side()
    for k, first, piece in held:
        chunk = chunk_of(k)
        for odd in (0, 1):

            @pl.when(chunk // 2 == odd)
            def _():
                for j in range(first, first + piece.shape[0]):
                    if j < split:
                        slot = lax.rem(chunk, 2) * split + j
                    else:
                        slot = layers - 1 - (lax.rem(chunk, 2) * (STAGES // 2) + j - split)
                    layer = slot + near * (layers - 1 - 2 * slot)
                    for c in range(3):
                        whole[c, layer, pl.ds(odd, rows, stride=2), :] = piece[j - first, c]


def gather_kernel(early_own, late_own, across, back, early_side, whole):
    split = early_own.shape[0]
    held = ((0, 0, early_own), (0, split, late_own), (1, 0, across), (3, 0, early_side))
    put(whole, held + ((2, 0, back),))


def finish_kernel(gathered, late_side, _, out, whole, sem):
    split = (whole.shape[1] - STAGES) // 2

    @pl.when(lax.axis_index("tm") != 0)
    def _():
        whole[...] = gathered[...]
        put(whole, ((3, split, late_side),))
        write(whole, out, sem)


def shards(states, rate):
    slices = lax.axis_size("tm")
    slabs = lax.axis_size("gz")
    groups = slices // GROUP
    own = states[0]
    layers, rows, width = own.shape[1:]
    middle_layers = layers - 2 * STAGES
    tile = (3, 2, rows // 2, width)
    face = f32(3, STAGES, rows, width)
    sizes = ((layers - STAGES) // 2, STAGES // 2)
    team = lax.axis_index("tm") // GROUP

    def halo(value, pairs):
        return lax.ppermute(value, "gz", [(i, j % slabs) for i, j in pairs])

    def exchange(value, k):
        return lax.ppermute(value, "tm", [(i, i ^ partner(k)) for i in range(slices)])

    def swap(parts):
        return [parts[0]] + [exchange(parts[k], k) for k in range(1, GROUP)]

    def onward(value, distance):
        step = distance * GROUP
        return lax.ppermute(value, "tm", [(i, (i + step) % slices) for i in range(slices)])

    far_face, near_face = call(faces_kernel, [face, face], own)
    near_face = halo(near_face, [(i, i ^ 1) for i in range(slabs)])
    far_face = halo(far_face, [(i, i + 1 if i % 2 else i - 1 + slabs) for i in range(slabs)])
    row = (rows // 2, width)
    edges, middle, faded, damp, kept = call(
        inside_kernel,
        [
            f32(STAGES, 2, 3, *tile),
            f32(middle_layers, *tile),
            f32(2, STAGES, *tile),
            f32(sum(sizes), *row),
            f32(layers, *tile),
        ],
        own, rate,
        scratch=[
            pltpu.VMEM((2, 2, STAGES, *row), jnp.float32),
            pltpu.VMEM((2, layers - STAGES, *row), jnp.float32),
        ]
        + [pltpu.VMEM((layers, *tile), jnp.float32)] * 3,
        flops=1 << 26,
    )
    strip = pltpu.VMEM((STAGES + 1, STAGES, *tile), jnp.float32)
    shares = [f32(size, 3, *row) for size in sizes]
    whole_share = f32(sum(sizes), 3, *row)

    def after(value, earlier):
        return lax.optimization_barrier((value, earlier))[0]

    halves = []
    for far, face_ref in enumerate((near_face, far_face)):
        jumps = call(
            functools.partial(jumps_kernel, far), [shares[far]] * GROUP,
            face_ref, edges, middle, faded,
            scratch=[strip, pltpu.VMEM((2, 2 * sizes[far], 3, *row), jnp.float32)],
            flops=BUSY,
        )
        halves.append(swap(jumps))

    orders = [pltpu.VMEM((GROUP, *share.shape), jnp.float32) for share in shares]
    carries, total = [], halves[1][0]
    for far, jumps in enumerate(halves):
        jumps[0] = after(jumps[0], total)
        first = far * sizes[0]
        total = call(
            functools.partial(total_kernel, first), shares[far], *jumps, damp,
            scratch=[orders[far]],
            flops=BUSY,
        )
        carry = onward(total, 1)
        if groups > 2:
            carry = jnp.where(team < 1, 0.0, carry)
            fade, distance = damp[first : first + sizes[far], None] ** GROUP, 1
            while distance < groups - 1:
                carry = carry + jnp.where(team < distance, 0.0, fade * onward(carry, distance))
                distance, fade = 2 * distance, fade * fade
        carries.append(carry)
    early = call(
        early_kernel, [shares[0]] * GROUP, carries[0], *halves[0], damp, scratch=[orders[0]],
        flops=BUSY,
    )
    side = exchange(early[3], 3)
    late = call(
        late_kernel, [shares[1], whole_share, whole_share, shares[1]],
        early[1], early[2], carries[1], *halves[1], damp,
        scratch=[orders[1]],
        flops=BUSY,
    )
    late = [*late[:3], call(pass_kernel, shares[1], late[3], flops=BUSY)]
    late_own, across, back, late_side = swap(late)
    gathered = call(
        gather_kernel, f32(*own.shape), early[0], late_own, across, back, side, flops=BUSY
    )
    pieces = [gathered, late_side]
    whole = [pltpu.VMEM(own.shape, jnp.float32), pltpu.SemaphoreType.DMA]
    updated = pl.pallas_call(
        first_kernel,
        out_shape=f32(*own.shape),
        in_specs=[VMEM],
        out_specs=ANY,
        scratch_shapes=whole,
        compiler_params=PARAMS,
        cost_estimate=pl.CostEstimate(flops=BUSY, bytes_accessed=1 << 20, transcendentals=0),
    )(after(kept, early[0]))
    updated = pl.pallas_call(
        finish_kernel,
        out_shape=f32(*own.shape),
        in_specs=[VMEM] * len(pieces) + [ANY],
        out_specs=ANY,
        scratch_shapes=whole,
        input_output_aliases={len(pieces): 0},
        compiler_params=PARAMS,
    )(*pieces, updated)
    return updated[None]


def solution(mesh):
    return jax.shard_map(
        shards,
        mesh=mesh,
        in_specs=(P("tm", None, "gz", None, None), P("gz", None, None)),
        out_specs=P("tm", None, "gz", None, None),
        check_vma=False,
    )
```
